32 devices in a mesh: batch: 8 (over z, x), seq: 4 (over y, core).
Axes of the slice: x: 2, y: 2, z: 4, core: 2. Of those that a mesh axis runs over, the one named last changes fastest.
Arguments:
- tokens: bfloat16 [32, 1024, 768], P('batch', 'seq'), may hold values from -6 to 6
- cotangent: bfloat16 [32, 1024, 768], P('batch', 'seq'), may hold values from -6 to 6
- lengths: int32 [32], replicated, may hold values from 256 to 1024, as said below
- order: int32 [32], P('batch'), may hold values from 0 to 31, as said below
- expert_route: int32 [32, 1024], P('batch', 'seq'), may hold values from 0 to 7, as said below
- slot_index: int32 [32, 1024], P('batch', 'seq'), may hold values from -1 to 39, as said below
- norm_gain: bfloat16 [768], P(('batch', 'seq')), may hold values from 0.5 to 1.5
- in_proj: bfloat16 [768, 3072], P(('batch', 'seq')), may hold values from -0.21875 to 0.21875
- conv_weight: bfloat16 [1536, 4], P(('batch', 'seq')), may hold values from -3 to 3
- conv_bias: bfloat16 [1536], P(('batch', 'seq')), may hold values from -1.5 to 1.5
- x_proj: bfloat16 [1536, 80], P(('batch', 'seq')), may hold values from -0.15625 to 0.15625
- dt_proj: bfloat16 [1536, 48], P(('batch', 'seq')), may hold values from -0.875 to 0.875
- dt_bias: bfloat16 [1536], P(('batch', 'seq')), may hold values from -7 to -3
- a_log: bfloat16 [1536, 16], P(('batch', 'seq')), may hold values from -1 to 2.796875
- skip_gain: bfloat16 [1536], P(('batch', 'seq')), may hold values from 0.5 to 1.5
- out_proj: bfloat16 [1536, 768], P(('batch', 'seq')), may hold values from -0.15625 to 0.15625
- moe_gain: bfloat16 [768], P(('batch', 'seq')), may hold values from 0.5 to 1.5
- router: bfloat16 [768, 8], P(('batch', 'seq')), may hold values from -0.15625 to 0.15625
- expert_in: bfloat16 [8, 768, 3072], P('batch', None, 'seq'), may hold values from -0.21875 to 0.21875
- expert_out: bfloat16 [8, 3072, 768], P('batch', 'seq'), may hold values from -0.875 to 0.875
Outputs:
- activations: bfloat16 [32, 1024, 768], P('batch', 'seq')
- input_grad: float32 [32, 1024, 768], P('batch', 'seq')
- norm_gain_grad: float32 [768], P(('batch', 'seq'))
- in_proj_grad: float32 [768, 3072], P(('batch', 'seq'))
- conv_weight_grad: float32 [1536, 4], P(('batch', 'seq'))
- conv_bias_grad: float32 [1536], P(('batch', 'seq'))
- x_proj_grad: float32 [1536, 80], P(('batch', 'seq'))
- dt_proj_grad: float32 [1536, 48], P(('batch', 'seq'))
- dt_bias_grad: float32 [1536], P(('batch', 'seq'))
- a_log_grad: float32 [1536, 16], P(('batch', 'seq'))
- skip_gain_grad: float32 [1536], P(('batch', 'seq'))
- out_proj_grad: float32 [1536, 768], P(('batch', 'seq'))
- moe_gain_grad: float32 [768], P(('batch', 'seq'))
- router_grad: float32 [768, 8], P(('batch', 'seq'))
- expert_in_grad: float32 [8, 768, 3072], P('batch', None, 'seq')
- expert_out_grad: float32 [8, 3072, 768], P('batch', 'seq')
The draws below stay inside these ranges and needn't reach their ends.
Inputs may be any that keep to these rules, and one draw needn't show every extreme that they name: `lengths`: positions from a sequence's length on are padding. Some sequence has exactly 1024 tokens and some exactly 256. `order`: A permutation of the sequences: taken by decreasing length (ties by number), they are dealt to the batch indices in turns, forward in even turns and backward in odd ones, the j-th turn filling the j-th row of each batch index. `expert_route`: A block is the 1 sequence of one micro-batch (the m-th run of 1 among the 4 rows of a batch index) at the 256 positions of one index of seq. In every block one expert, the same in all blocks of a draw, is chosen by more than 40 tokens. `slot_index`: A token's slot is its rank, counting tokens of its block in order of row then position, among the block's tokens with the same expert; -1 where that rank is 40 or more.
All inputs are finite; a program needn't handle non-finite values.
Results may differ from the reference program's by a relative error of at most 0.015.
Values may be sent and summed in bfloat16 or wider, within the bound.
No kernel may reach another device: no remote copies, remote signals or barrier semaphores. Data moves between devices by JAX's collectives and lax.ppermute only.
A program may use at most 896 MiB of HBM per device.

```python
import jax
import jax.numpy as jnp
from jax import lax

D = 768
DI = 1536
STATE = 16
DT_RANK = 48
CONV = 4
FF = 3072
MB = 4
SEQ_MB = 1
LEN = 1024
EXPERTS = 8
SEQ_GRP = 4
SEQS = 32
SPAN = 256
CAP = 40
N_BATCH = 8
N_SEQ = 4


def length_table(key):
    base_length = jax.random.randint(jax.random.fold_in(key, 21), (SEQS,), LEN // 4, LEN + 1, dtype=jnp.int32)
    first_pick = jax.random.randint(jax.random.fold_in(key, 22), (), 0, SEQS, dtype=jnp.int32)
    offset_pick = jax.random.randint(jax.random.fold_in(key, 23), (), 1, SEQS, dtype=jnp.int32)
    second_pick = (first_pick + offset_pick) % SEQS
    seq_index = jnp.arange(SEQS, dtype=jnp.int32)
    base_length = jnp.where(seq_index == first_pick, LEN, base_length)
    return jnp.where(seq_index == second_pick, LEN // 4, base_length).astype(jnp.int32)


def draw_lengths(key, part):
    return length_table(key)


def draw_order(key, part):
    seq_lengths = length_table(key)
    seq_index = jnp.arange(SEQS, dtype=jnp.int32)
    scores = seq_lengths * SEQS + (SEQS - 1 - seq_index)
    sorted_seq = jnp.argsort(-scores).astype(jnp.int32)
    groups = SEQS // SEQ_GRP
    turn = seq_index // groups
    within = seq_index % groups
    target_group = jnp.where(turn % 2 == 0, within, groups - 1 - within)
    dest_row = (target_group * SEQ_GRP + turn).astype(jnp.int32)
    return jnp.zeros((SEQS,), jnp.int32).at[dest_row].set(sorted_seq)


def route_table(key):
    blocks = SEQS // (MB * SEQ_MB)
    pieces = LEN // SPAN
    block_rows = SEQ_MB * SPAN
    draw_shape = (blocks, MB, pieces, block_rows)
    first_draw = jax.random.randint(jax.random.fold_in(key, 11), draw_shape, 0, EXPERTS, dtype=jnp.int32)
    second_draw = jax.random.randint(jax.random.fold_in(key, 12), draw_shape, 0, EXPERTS, dtype=jnp.int32)
    expert_order = jax.random.permutation(jax.random.fold_in(key, 13), EXPERTS).astype(jnp.int32)
    shared_factor = expert_order[jnp.minimum(first_draw, second_draw)]
    hot_all = jax.random.randint(jax.random.fold_in(key, 14), (), 0, EXPERTS, dtype=jnp.int32)
    hot_block = jax.random.randint(jax.random.fold_in(key, 15), (blocks, MB, pieces, 1), 0, EXPERTS, dtype=jnp.int32)
    scores = jax.random.randint(jax.random.fold_in(key, 16), draw_shape, 0, 1 << 16, dtype=jnp.int32) * block_rows + jnp.arange(block_rows, dtype=jnp.int32)
    ranking = jnp.argsort(jnp.argsort(scores, axis=-1), axis=-1)
    expert_pick = jnp.where(ranking < CAP + 1, hot_all, jnp.where(ranking < 2 * CAP + 2, hot_block, shared_factor))
    onehot = (expert_pick[..., None] == jnp.arange(EXPERTS, dtype=jnp.int32)).astype(jnp.int32)
    seen_count = jnp.sum(jnp.cumsum(onehot, axis=-2) * onehot, axis=-1) - 1
    slot_row = jnp.where(seen_count < CAP, seen_count, -1)

    def layout(array_in):
        array_in = array_in.reshape(blocks, MB, pieces, SEQ_MB, SPAN)
        return jnp.transpose(array_in, (0, 1, 3, 2, 4)).reshape(SEQS, LEN).astype(jnp.int32)
    return (layout(expert_pick), layout(slot_row))


def draw_expert_route(key, part):
    return route_table(key)[0]


def draw_slot_index(key, part):
    return route_table(key)[1]


def block_scale(own_key, shape, cuts, low, high):
    def one(position, blocks):
        draws = jax.random.uniform(jax.random.fold_in(jax.random.fold_in(own_key, 6), position), (blocks,), jnp.float32, low / len(cuts), high / len(cuts))
        return jnp.repeat(jnp.exp(draws), shape[position] // blocks).reshape((-1,) + (1,) * (len(shape) - position - 1))

    loudness = one(*cuts[0])
    for cut in cuts[1:]:
        loudness = loudness * one(*cut)
    return loudness


def scatter_about(stream_key, extent, scale, limit, split=(), held_as=jnp.bfloat16):
    loudness = block_scale(stream_key, extent, split, -0.22, 0.18) if split else 1.0
    values = jax.random.normal(stream_key, extent, jnp.float32) * scale * loudness
    return jnp.minimum(jnp.maximum(values, -limit), limit).astype(held_as)


def setup_inputs(seed: int = 0) -> dict:
    key_of = jax.random.split(jax.random.key(seed), 21)
    tokens = scatter_about(key_of[0], (SEQS, LEN, D), 1.0, 6.0, ((0, 8), (1, 4)))
    cotangent = scatter_about(key_of[1], (SEQS, LEN, D), 1.0, 6.0, ((0, 8), (1, 4)))
    lengths = draw_lengths(jax.random.fold_in(key_of[20], 71), 0)
    order = draw_order(jax.random.fold_in(key_of[20], 71), 0)
    expert_route = draw_expert_route(jax.random.fold_in(key_of[20], 71), 0)
    slot_index = draw_slot_index(jax.random.fold_in(key_of[20], 71), 0)
    norm_gain = jnp.clip(1.0 + 0.1 * jax.random.normal(key_of[6], (D,), jnp.float32), 0.5, 1.5).astype(jnp.bfloat16)
    in_proj = scatter_about(key_of[7], (D, 2 * DI), D ** -0.5, 0.21875, ((0, 32),))
    conv_weight = scatter_about(key_of[8], (DI, CONV), CONV ** -0.5, 3.0, ((0, 32),))
    conv_bias = scatter_about(key_of[9], (DI,), 0.3, 1.5, ((0, 32),))
    x_proj = scatter_about(key_of[10], (DI, DT_RANK + 2 * STATE), DI ** -0.5, 0.15625, ((0, 32),))
    dt_proj = scatter_about(key_of[11], (DI, DT_RANK), DT_RANK ** -0.5, 0.875, ((0, 32),))
    dt_bias = jnp.clip(-7.0 + 4.0 * jax.random.uniform(key_of[12], (DI,), jnp.float32) ** block_scale(key_of[12], (DI,), ((0, 32),), -0.2, 0.2), -7.0, -3.0).astype(jnp.bfloat16)
    a_log = jnp.clip(-1.0 + 3.796875 * jax.random.uniform(key_of[13], (DI, STATE), jnp.float32) ** block_scale(key_of[13], (DI, STATE), ((0, 32),), -0.2, 0.2), -1.0, 2.796875).astype(jnp.bfloat16)
    skip_gain = jnp.clip(0.5 + 1.0 * jax.random.uniform(key_of[14], (DI,), jnp.float32) ** block_scale(key_of[14], (DI,), ((0, 32),), -0.2, 0.2), 0.5, 1.5).astype(jnp.bfloat16)
    out_proj = scatter_about(key_of[15], (DI, D), DI ** -0.5, 0.15625, ((0, 32),))
    moe_gain = jnp.clip(1.0 + 0.1 * jax.random.normal(key_of[16], (D,), jnp.float32), 0.5, 1.5).astype(jnp.bfloat16)
    router = scatter_about(key_of[17], (D, EXPERTS), (2 * D) ** -0.5, 0.15625, ((0, 32),))
    expert_in = scatter_about(key_of[18], (EXPERTS, D, FF), D ** -0.5, 0.21875, ((0, 8), (2, 4)))
    expert_out = scatter_about(key_of[19], (EXPERTS, FF, D), (max(1, FF // (EXPERTS * EXPERTS))) ** -0.5, 0.875, ((0, 8), (1, 4)))
    return {"tokens": tokens, "cotangent": cotangent, "lengths": lengths, "order": order, "expert_route": expert_route, "slot_index": slot_index, "norm_gain": norm_gain, "in_proj": in_proj, "conv_weight": conv_weight, "conv_bias": conv_bias, "x_proj": x_proj, "dt_proj": dt_proj, "dt_bias": dt_bias, "a_log": a_log, "skip_gain": skip_gain, "out_proj": out_proj, "moe_gain": moe_gain, "router": router, "expert_in": expert_in, "expert_out": expert_out}


EPSILON = 1e-05
EXACT_PRECISION = lax.Precision.HIGHEST
TIME_BLOCK = 64

@jax.custom_vjp
def low(v):
    return lax.optimization_barrier(v.astype(jnp.bfloat16)).astype(jnp.float32)

@jax.custom_vjp
def low_back(v):
    return v

def low_keep(v):
    return (low(v), None)

def low_pass(kept, grad):
    return (grad,)

def back_keep(v):
    return (v, None)

def back_low(kept, grad):
    return (low(grad),)
low.defvjp(low_keep, low_pass)
low_back.defvjp(back_keep, back_low)

def selective(step_size, activated, input_map, output_map, decay_rate):
    seq_group, seq_length, inner_width = step_size.shape
    block_count = seq_length // TIME_BLOCK

    def one_step(hidden_state, step_item):
        step_time, step_act, step_in, step_out = step_item
        hidden_state = jnp.exp(step_time[:, :, None] * decay_rate) * hidden_state + (step_time * step_act)[:, :, None] * step_in[:, None, :]
        return (hidden_state, lax.optimization_barrier(jnp.sum(hidden_state * step_out[:, None, :], axis=-1)))

    def one_block(hidden_state, block_items):
        return lax.scan(one_step, hidden_state, block_items)

    def time_major(array_in):
        array_in = jnp.swapaxes(array_in, 0, 1)
        return array_in.reshape((block_count, TIME_BLOCK) + array_in.shape[1:])
    state_init = jnp.zeros((seq_group, inner_width, decay_rate.shape[1]), jnp.float32)
    _, output_rows = lax.scan(jax.checkpoint(one_block), state_init, (time_major(step_size), time_major(activated), time_major(input_map), time_major(output_map)))
    return jnp.swapaxes(output_rows.reshape(seq_length, seq_group, inner_width), 0, 1)

def mixer_layer(seq_block, weights):
    gain_one, w_joint, w_conv, bias_conv, w_proj, w_step, bias_step, log_rate, w_skip, w_back = weights
    scale_one = lax.rsqrt(lax.optimization_barrier(jnp.mean(seq_block * seq_block, axis=-1, keepdims=True)) + EPSILON)
    normed = low(seq_block * scale_one * gain_one)
    joint_proj = low_back(jnp.einsum('gld,de->gle', normed, w_joint, precision=EXACT_PRECISION))
    inner_width = w_conv.shape[0]
    conv_taps = w_conv.shape[1]
    seq_length = seq_block.shape[1]
    conv_in = joint_proj[..., :inner_width]
    gate_in = joint_proj[..., inner_width:]
    padded = jnp.pad(conv_in, ((0, 0), (conv_taps - 1, 0), (0, 0)))
    conv_out = bias_conv + sum((padded[:, tap_index:tap_index + seq_length, :] * w_conv[:, tap_index] for tap_index in range(conv_taps)))
    activated = low(jax.nn.silu(conv_out))
    projected = low_back(jnp.einsum('gli,ie->gle', activated, w_proj, precision=EXACT_PRECISION))
    dt_width = w_step.shape[1]
    state_dimension = log_rate.shape[1]
    delta_low = low(projected[..., :dt_width])
    input_map = projected[..., dt_width:dt_width + state_dimension]
    output_map = projected[..., dt_width + state_dimension:]
    pre_step = low_back(jnp.einsum('glr,ir->gli', delta_low, w_step, precision=EXACT_PRECISION))
    step_size = jax.nn.softplus(pre_step + bias_step)
    decay_rate = -jnp.exp(log_rate)
    mixed_out = selective(step_size, activated, input_map, output_map, decay_rate) + w_skip * activated
    gated_out = low(mixed_out * jax.nn.silu(gate_in))
    return seq_block + low_back(jnp.einsum('gli,id->gld', gated_out, w_back, precision=EXACT_PRECISION))

def expert_apply(block_items):
    rows_in, first_weight, second_weight = block_items
    hidden = low_back(jnp.dot(rows_in, first_weight, precision=EXACT_PRECISION))
    activation = low(jax.nn.gelu(hidden, approximate=True))
    return low(low_back(jnp.dot(activation, second_weight, precision=EXACT_PRECISION)))

def reference(tokens, cotangent, lengths, order, expert_route, slot_index, norm_gain, in_proj, conv_weight, conv_bias, x_proj, dt_proj, dt_bias, a_log, skip_gain, out_proj, moe_gain, router, expert_in, expert_out):
    seq_ids = jnp.arange(SEQS, dtype=jnp.int32)[:, None]
    positions = jnp.arange(LEN, dtype=jnp.int32)[None, :]
    row_length = lengths[order.astype(jnp.int32)]
    keep_mask = (positions < row_length[:, None]).astype(jnp.float32)
    block_ids = (seq_ids // SEQ_GRP * MB + seq_ids % SEQ_GRP // SEQ_MB) * N_SEQ + positions // SPAN
    slot_rows = N_BATCH * MB * N_SEQ * CAP
    kept_slot = slot_index >= 0
    valid_weight = kept_slot.astype(jnp.float32)
    token_total = SEQS * LEN
    slot_place = jnp.where(kept_slot, expert_route * slot_rows + block_ids * CAP + jnp.maximum(slot_index, 0), EXPERTS * slot_rows).reshape(-1).astype(jnp.int32)
    source_row = jnp.full((EXPERTS * slot_rows,), token_total, jnp.int32).at[slot_place].set(jnp.arange(token_total, dtype=jnp.int32), mode='drop').reshape(EXPERTS, slot_rows)
    fetch_row = jnp.minimum(slot_place, EXPERTS * slot_rows - 1).astype(jnp.int32)

    def forward(inputs, dense_weights, first_weight, second_weight):
        gain_one, w_joint, w_conv, bias_conv, w_proj, w_step, bias_step, log_rate, w_skip, w_back, gain_two, router_weight = dense_weights
        mixer_weights = (gain_one, w_joint, w_conv, bias_conv, w_proj, w_step, bias_step, log_rate, w_skip, w_back)
        checked_layer = jax.checkpoint(mixer_layer)

        def group_apply(seq_block):
            return checked_layer(seq_block, mixer_weights)
        seq_groups = inputs.reshape(SEQS // 4, 4, LEN, D)
        mixed_rows = lax.map(group_apply, seq_groups).reshape(SEQS, LEN, D)
        scale_two = lax.rsqrt(lax.optimization_barrier(jnp.mean(mixed_rows * mixed_rows, axis=-1, keepdims=True)) + EPSILON)
        routed_tokens = low(mixed_rows * scale_two * gain_two)
        router_logits = low_back(jnp.einsum('kpg,gt->kpt', routed_tokens, router_weight, precision=EXACT_PRECISION))
        softmax_out = jax.nn.softmax(router_logits, axis=-1)
        flat_rows = jnp.concatenate([routed_tokens.reshape(token_total, D), jnp.zeros((1, D), jnp.float32)], axis=0)
        dispatched = low_back(flat_rows[source_row])
        returned = lax.map(jax.checkpoint(expert_apply), (dispatched, first_weight, second_weight))
        picked = returned.reshape(EXPERTS * slot_rows, D)[fetch_row].reshape(SEQS, LEN, D)
        gate_value = jnp.take_along_axis(softmax_out, expert_route[..., None], axis=-1)[..., 0] * valid_weight
        return mixed_rows + gate_value[..., None] * picked
    dense_in = tuple((array_in.astype(jnp.float32) for array_in in (norm_gain, in_proj, conv_weight, conv_bias, x_proj, dt_proj, dt_bias, a_log, skip_gain, out_proj, moe_gain, router)))
    result, pullback = jax.vjp(forward, tokens.astype(jnp.float32), dense_in, expert_in.astype(jnp.float32), expert_out.astype(jnp.float32))
    grad_tokens, grad_dense, grad_first, grad_second = pullback(cotangent.astype(jnp.float32) * keep_mask[..., None])
    return (result.astype(jnp.bfloat16), grad_tokens, grad_dense[0], grad_dense[1], grad_dense[2], grad_dense[3], grad_dense[4], grad_dense[5], grad_dense[6], grad_dense[7], grad_dense[8], grad_dense[9], grad_dense[10], grad_dense[11], grad_first, grad_second)
```

```python
import functools
import math

import jax
import jax.numpy as jnp
from jax import lax
from jax.experimental import pallas as pl
from jax.experimental.pallas import tpu as pltpu
from jax.sharding import PartitionSpec as P

DI = 1536
STATE = 16
DT_RANK = 48
CONV = 4
SEQ_MB = 1
EPSILON = 1e-05
F32 = jnp.float32
BF = jnp.bfloat16
U = 16
CB = 512
LOG2E = 1.0 / math.log(2.0)
LN2 = math.log(2.0)
HALO = 8


def end_kernel(backward, chunks, s_ref, x_ref, bt_ref, r_ref, h_ref):
    r = r_ref[...]
    width = r.shape[1]
    def chunk(c, h):
        if backward: c = chunks-1-c
        rows = pl.ds(pl.multiple_of(c*U,U),U)
        s8 = s_ref[0, rows, :]
        d8 = x_ref[0, rows, :].astype(F32)
        if not backward: d8 = d8*s8
        bt = bt_ref[0, c]
        for k in (range(U-1,-1,-1) if backward else range(U)):
            s = jnp.broadcast_to(s8[k:k+1], (STATE,width))
            d = jnp.broadcast_to(d8[k:k+1], (STATE,width))
            b = jnp.broadcast_to(bt[(STATE if backward else 0):(2*STATE if backward else STATE), k:k+1], (STATE,width))
            if backward:
                h = jnp.exp2(s*r)*(h + d*b)
            else:
                h = jnp.exp2(s*r)*h + d*b
        return h
    h_ref[0] = lax.fori_loop(0, chunks, chunk, jnp.zeros((STATE,width),F32))

def scan_end(s, x, bt, r, backward):
    S,T,C = s.shape
    cb=min(CB,C)
    row=pl.BlockSpec((1,T,cb), lambda i,j:(i,0,j))
    return pl.pallas_call(functools.partial(end_kernel, backward, T//U),
        grid=(S,C//cb),
        in_specs=[row,row,pl.BlockSpec((1,T//U,2*STATE,U),lambda i,j:(i,0,0,0)),pl.BlockSpec((STATE,cb),lambda i,j:(0,j))],
        out_specs=pl.BlockSpec((1,STATE,cb),lambda i,j:(i,0,j)),
        out_shape=jax.ShapeDtypeStruct((S,STATE,C),F32),
        compiler_params=pltpu.CompilerParams(vmem_limit_bytes=48<<20),
        cost_estimate=pl.CostEstimate(flops=6*S*T*C*STATE,bytes_accessed=8*S*T*C,transcendentals=S*T*C*STATE),
        name="scan_end_b" if backward else "scan_end_f",
    )(s,x,bt,r)

def fwd_kernel(chunks, s_ref, x_ref, bt_ref, l_ref, r_ref, h0_ref, y_ref, h_ref):
    r = r_ref[...]
    width = r.shape[1]
    def chunk(c, h):
        rows = pl.ds(pl.multiple_of(c*U,U),U)
        s8 = s_ref[0, rows, :]
        d8 = x_ref[0, rows, :].astype(F32)*s8
        bt = bt_ref[0, c]
        for k in range(U):
            s = jnp.broadcast_to(s8[k:k+1], (STATE,width))
            d = jnp.broadcast_to(d8[k:k+1], (STATE,width))
            b = jnp.broadcast_to(bt[0:STATE, k:k+1], (STATE,width))
            h = jnp.exp2(s*r)*h + d*b
            h_ref[0, pl.ds(pl.multiple_of(c*U*STATE+k*STATE,STATE),STATE), :] = h.astype(BF)
        y_ref[0, rows, :] = jnp.dot(l_ref[0, rows, :], h_ref[0, pl.ds(pl.multiple_of(c*U*STATE,U*STATE),U*STATE), :], preferred_element_type=F32)
        return h
    lax.fori_loop(0, chunks, chunk, h0_ref[0])

def scan_fwd(s, x, bt, l, r, h0):
    S,T,C = s.shape
    cb=min(CB,C)
    row=pl.BlockSpec((1,T,cb), lambda i,j:(i,0,j))
    st=pl.BlockSpec((1,STATE,cb),lambda i,j:(i,0,j))
    return pl.pallas_call(functools.partial(fwd_kernel, T//U),
        grid=(S,C//cb),
        in_specs=[row,row,pl.BlockSpec((1,T//U,2*STATE,U),lambda i,j:(i,0,0,0)),pl.BlockSpec((1,T,U*STATE),lambda i,j:(i,0,0)),pl.BlockSpec((STATE,cb),lambda i,j:(0,j)),st],
        out_specs=[row,pl.BlockSpec((1,T*STATE,cb),lambda i,j:(i,0,j))],
        out_shape=[jax.ShapeDtypeStruct((S,T,C),F32),jax.ShapeDtypeStruct((S,T*STATE,C),BF)],
        compiler_params=pltpu.CompilerParams(vmem_limit_bytes=48<<20),
        cost_estimate=pl.CostEstimate(flops=8*S*T*C*STATE,bytes_accessed=42*S*T*C,transcendentals=S*T*C*STATE),
        name="scan_fwd",
    )(s,x,bt,l,r,h0)

def bwd_kernel(chunks, s_ref, x_ref, g_ref, bt_ref, l_ref, one_ref, r_ref, h0_ref, m0_ref, h_ref,
               pull_ref, gs_ref, alog_ref, gi_ref, go_ref, lam_s, fr_s):
    r = r_ref[...]
    width = r.shape[1]
    j = pl.program_id(1)
    @pl.when(j==0)
    def _():
        gi_ref[...]=jnp.zeros_like(gi_ref)
        go_ref[...]=jnp.zeros_like(go_ref)
    def chunk(c, carry):
        c = chunks-1-c
        lam_c, alog = carry
        rows = pl.ds(pl.multiple_of(c*U,U),U)
        big = pl.ds(pl.multiple_of(c*U*STATE,U*STATE),U*STATE)
        s8 = s_ref[0, rows, :]
        g8 = g_ref[0, rows, :]
        bt = bt_ref[0, c]
        for k in range(U-1,-1,-1):
            s = jnp.broadcast_to(s8[k:k+1], (STATE,width))
            g = jnp.broadcast_to(g8[k:k+1], (STATE,width))
            cc = jnp.broadcast_to(bt[STATE:2*STATE, k:k+1], (STATE,width))
            if k:
                hp = h_ref[0, pl.ds(pl.multiple_of(c*U*STATE+(k-1)*STATE,STATE),STATE), :].astype(F32)
            else:
                hp = h_ref[0, pl.ds(pl.multiple_of(jnp.maximum(c*U*STATE-STATE,0),STATE),STATE), :].astype(F32)
                hp = jnp.where(c==0, h0_ref[0], hp)
            lam = lam_c + g*cc
            lam_c = jnp.exp2(s*r)*lam
            fr = lam_c*hp*r
            alog = alog + fr*s
            lam_s[k*STATE:(k+1)*STATE,:] = lam.astype(BF)
            fr_s[k*STATE:(k+1)*STATE,:] = fr.astype(BF)
        lam_all = lam_s[...]
        d8 = (x_ref[0, rows, :].astype(F32)*s8).astype(BF)
        pull_ref[0, rows, :] = jnp.dot(l_ref[0, rows, :], lam_all, preferred_element_type=F32)
        gs_ref[0, rows, :] = jnp.dot(one_ref[...], fr_s[...], preferred_element_type=F32)
        nt=(((1,),(1,)),((),()))
        gi_ref[0, rows, :] += lax.dot_general(d8, lam_all, nt, preferred_element_type=F32)
        go_ref[0, rows, :] += lax.dot_general(g8.astype(BF), h_ref[0, big, :], nt, preferred_element_type=F32)
        return lam_c, alog
    _, alog = lax.fori_loop(0, chunks, chunk, (m0_ref[0], jnp.zeros((STATE,width),F32)))
    alog_ref[0] = alog

def scan_bwd(s, x, g, bt, l, one, r, h0, m0, h):
    S,T,C = s.shape
    cb=min(CB,C)
    row=pl.BlockSpec((1,T,cb), lambda i,j:(i,0,j))
    st=pl.BlockSpec((1,STATE,cb),lambda i,j:(i,0,j))
    lo=pl.BlockSpec((1,T,U*STATE),lambda i,j:(i,0,0))
    return pl.pallas_call(functools.partial(bwd_kernel, T//U),
        grid=(S,C//cb),
        in_specs=[row,row,row,pl.BlockSpec((1,T//U,2*STATE,U),lambda i,j:(i,0,0,0)),lo,pl.BlockSpec((U,U*STATE),lambda i,j:(0,0)),pl.BlockSpec((STATE,cb),lambda i,j:(0,j)),st,st,pl.BlockSpec((1,T*STATE,cb),lambda i,j:(i,0,j))],
        out_specs=[row,row,st,lo,lo],
        out_shape=[jax.ShapeDtypeStruct((S,T,C),F32),jax.ShapeDtypeStruct((S,T,C),F32),jax.ShapeDtypeStruct((S,STATE,C),F32),jax.ShapeDtypeStruct((S,T,U*STATE),F32),jax.ShapeDtypeStruct((S,T,U*STATE),F32)],
        scratch_shapes=[pltpu.VMEM((U*STATE,cb),BF),pltpu.VMEM((U*STATE,cb),BF)],
        compiler_params=pltpu.CompilerParams(vmem_limit_bytes=48<<20),
        cost_estimate=pl.CostEstimate(flops=16*S*T*C*STATE,bytes_accessed=50*S*T*C,transcendentals=S*T*C*STATE),
        name="scan_bwd",
    )(s,x,g,bt,l,one,r,h0,m0,h)


def fold(z):
    seqs, span, _ = z.shape
    same = jnp.arange(span)[:, None] % U == jnp.arange(U * STATE)[None] // STATE
    return jnp.sum(jnp.where(same, z, 0).reshape(seqs, span, U, STATE), 2)


def spread_rows(m):
    same = jnp.arange(m.shape[1])[:, None] % U == jnp.arange(U * STATE)[None] // STATE
    return jnp.where(same, jnp.tile(m, (1, 1, U)), 0).astype(BF)


def bits_of(axis):
    return lax.axis_size(axis).bit_length() - 1


def my_bit(axis, k):
    return (lax.axis_index(axis) >> k) & 1


def swap(x, axis, k):
    count = lax.axis_size(axis)
    return lax.ppermute(x, axis, [(i, i ^ (1 << k)) for i in range(count)])


def shift(x, axis, distance):
    count = lax.axis_size(axis)
    return lax.ppermute(
        x, axis, [(i, i + distance) for i in range(count) if 0 <= i + distance < count]
    )


def mesh_bits():
    return [("batch", k) for k in reversed(range(bits_of("batch")))] + [
        ("seq", k) for k in reversed(range(bits_of("seq")))
    ]


def ordered(which):
    bits = mesh_bits()
    core = ("seq", 0)
    y_bits = [b for b in bits if b[0] == "seq" and b != core]
    x_bits = [("batch", 0)]
    z_bits = [b for b in bits if b[0] == "batch" and b[1] > 0]
    parts = {
        0: z_bits + x_bits + y_bits,
        1: y_bits + z_bits + x_bits,
        2: x_bits + y_bits + z_bits,
    }[which]
    return parts + [core]


def gather_all(x, which):
    bits = mesh_bits()
    out = x.reshape((1,) * len(bits) + x.shape)
    for axis, k in ordered(which):
        place = bits.index((axis, k))
        other = swap(out, axis, k)
        high = my_bit(axis, k) == 1
        out = jnp.concatenate(
            [jnp.where(high, other, out), jnp.where(high, out, other)], axis=place
        )
    return out.reshape((-1,) + x.shape[1:])


def scatter_sum(x, which, kind):
    bits = mesh_bits()
    rows = x.shape[0] >> len(bits)
    out = x.reshape((2,) * len(bits) + (rows,) + x.shape[1:])
    for axis, k in reversed(ordered(which)):
        place = bits.index((axis, k))
        bit = my_bit(axis, k)
        mine = lax.dynamic_index_in_dim(out, bit, place, True)
        theirs = lax.dynamic_index_in_dim(out, 1 - bit, place, True).astype(kind)
        out = mine + swap(theirs, axis, k).astype(F32)
    return out.reshape((rows,) + x.shape[1:])


def gather_seq(x):
    parts = [x]
    for k in reversed(range(bits_of("seq"))):
        parts = parts + [swap(p, "seq", k) for p in parts]
    count = len(parts)
    order = []
    for k in reversed(range(bits_of("seq"))):
        order = (order or [0]) + [o ^ (1 << k) for o in (order or [0])]
    return [parts[order.index(j)] for j in range(count)]


def scatter_seq(parts):
    parts = dict(enumerate(parts))
    for k in range(bits_of("seq")):
        bit = 1 << k
        moved = {j ^ bit: swap(p.astype(BF), "seq", k) for j, p in parts.items() if j & bit}
        parts = {j: p + moved[j].astype(F32) for j, p in parts.items() if not j & bit}
    return parts[0]


def prefix(total, state, rate, backward):
    before = jnp.zeros_like(state)
    before_total = jnp.zeros_like(total)
    stages = bits_of("seq")
    for k in range(stages):
        other_total = swap(total, "seq", k)
        other = swap(state.astype(BF), "seq", k).astype(F32)
        first = my_bit("seq", k) == (0 if backward else 1)
        before = jnp.where(
            first, before + jnp.exp2(before_total[:, None, :] * rate) * other, before
        )
        before_total = jnp.where(first, before_total + other_total, before_total)
        if k + 1 < stages:
            near = jnp.where(first, state, other)
            far = jnp.where(first, other, state)
            near_total = jnp.where(first, total, other_total)
            state = near + jnp.exp2(near_total[:, None, :] * rate) * far
            total = total + other_total
    return before


def mm(left, right, dims):
    return lax.dot_general(left, right, (dims, ((), ())), preferred_element_type=F32)


def nn(left, right):
    return mm(left, right, ((left.ndim - 1,), (0,)))


def nt(left, right):
    return mm(left, right, ((left.ndim - 1,), (1,)))


def tn(left, right):
    lead = tuple(range(left.ndim - 1))
    return mm(left, right, (lead, lead))


def silu_slope(v):
    s = jax.nn.sigmoid(v)
    return s * (1.0 + v * (1.0 - s))


def norm_back(grad_norm, x, scale):
    return scale * grad_norm - x * scale**3 * jnp.mean(grad_norm * x, axis=-1, keepdims=True)


def gelu_tanh(v):
    return jax.nn.gelu(v, approximate=True)


def rms(x):
    return lax.rsqrt(jnp.mean(x * x, axis=-1, keepdims=True) + EPSILON)


def pad_cols(x, width):
    return jnp.pad(x, ((0, 0), (0, width - x.shape[1])))


def shards(
    tokens,
    cotangent,
    lengths,
    order,
    expert_route,
    slot_index,
    norm_gain,
    in_proj,
    conv_weight,
    conv_bias,
    x_proj,
    dt_proj,
    dt_bias,
    a_log,
    skip_gain,
    out_proj,
    moe_gain,
    router,
    expert_in,
    expert_out,
):
    seqs, span, width = tokens.shape
    batch = lax.axis_size("batch")
    experts = expert_in.shape[0] * batch
    capacity = max(2, (5 * SEQ_MB * span + 4 * experts - 1) // (4 * experts))
    maps = DT_RANK + 2 * STATE

    chan = jnp.concatenate(
        [
            x_proj,
            dt_proj,
            a_log,
            conv_weight,
            conv_bias[:, None],
            dt_bias[:, None],
            skip_gain[:, None],
        ],
        axis=1,
    )
    feat = jnp.concatenate([norm_gain[:, None], moe_gain[:, None], router], axis=1)
    feat = gather_all(pad_cols(feat, 128), 1)
    w_conv_in = gather_all(in_proj[:, :DI], 0)
    chan = gather_all(pad_cols(chan, 256), 2)
    w_gate_in = gather_all(in_proj[:, DI:], 1)
    w_back = gather_all(out_proj, 2)
    gain_one = feat[:, 0].astype(F32)
    gain_two = feat[:, 1].astype(F32)
    router_weight = feat[:, 2 : 2 + experts]
    w_proj = chan[:, :maps]
    at = maps + DT_RANK
    w_step = chan[:, maps:at]
    rate = -jnp.exp(chan[:, at : at + STATE].astype(F32)).T * LOG2E
    at = at + STATE
    taps = chan[:, at : at + CONV].astype(F32).T
    bias_conv = chan[:, at + CONV].astype(F32)
    bias_step = chan[:, at + CONV + 1].astype(F32)
    skip = chan[:, at + CONV + 2].astype(F32)

    halo = shift(tokens[:, span - HALO :, :], "seq", 1)
    tail = jnp.arange(HALO)[:, None] >= HALO - (CONV - 1)
    halo = jnp.where(tail, halo, 0)

    first_weight = jnp.concatenate(gather_seq(expert_in[0]), axis=1)
    second_weight = jnp.concatenate(gather_seq(expert_out[0]), axis=0)

    positions = lax.axis_index("seq") * span + jnp.arange(span, dtype=jnp.int32)
    row_length = jnp.sum(
        jnp.where(
            order[:, None] == jnp.arange(lengths.shape[0], dtype=jnp.int32)[None, :],
            lengths[None, :],
            0,
        ),
        axis=1,
    )
    keep = (positions[None, :] < row_length[:, None]).astype(F32)
    grad_out = cotangent.astype(F32) * keep[..., None]

    block = tokens.astype(F32)
    scale_one = rms(block)
    ext = jnp.concatenate([halo, tokens], axis=1).astype(F32)
    normed_ext = (ext * rms(ext) * gain_one).astype(BF)
    normed = normed_ext[:, HALO:]
    conv_ext = nn(normed_ext, w_conv_in)
    gate_in = nn(normed, w_gate_in)
    lo = HALO - (CONV - 1)
    conv_out = bias_conv + sum(conv_ext[:, lo + k : lo + k + span, :] * taps[k] for k in range(CONV))
    act = jax.nn.silu(conv_out).astype(BF)
    projected = nn(act, w_proj)
    delta = projected[..., :DT_RANK].astype(BF)
    input_map = projected[..., DT_RANK : DT_RANK + STATE]
    output_map = projected[..., DT_RANK + STATE :]
    step_arg = nt(delta, w_step) + bias_step
    step = jax.nn.softplus(step_arg)
    total = jnp.sum(step, axis=1)
    both = jnp.swapaxes(projected[..., DT_RANK:].reshape(seqs, span // U, U, 2 * STATE), 2, 3)
    in_rows = spread_rows(input_map)
    out_rows = spread_rows(output_map)
    ones = (jnp.arange(U)[:, None] == jnp.arange(U * STATE)[None] // STATE).astype(BF)
    end = scan_end(step, act, both, rate, False)
    init = prefix(total, end, rate, False)
    y, states = scan_fwd(step, act, both, out_rows, rate, init)
    actf = act.astype(F32)
    mix = y + skip * actf
    gate_act = jax.nn.silu(gate_in)
    gated = (mix * gate_act).astype(BF)
    mixed = block + nn(gated, w_back)

    scale_two = rms(mixed)
    routed = (mixed * scale_two * gain_two).astype(BF)
    probs = jax.nn.softmax(nn(routed, router_weight), axis=-1)
    kept = slot_index >= 0
    target = jnp.where(kept, expert_route * capacity + slot_index, -1)
    slots = jnp.arange(experts * capacity, dtype=jnp.int32)
    selector = (target[..., None] == slots).astype(BF)
    chosen = jnp.logical_and(
        expert_route[..., None] == jnp.arange(experts, dtype=jnp.int32), kept[..., None]
    )
    gate = jnp.sum(jnp.where(chosen, probs, 0.0), axis=-1)[..., None]
    grad_value = (gate * grad_out).astype(BF)
    packed = jnp.concatenate([routed, grad_value], axis=-1)
    send = jnp.einsum("stc,std->scd", selector, packed, preferred_element_type=F32).astype(BF)
    send = jnp.swapaxes(send.reshape(seqs, batch, capacity, 2 * width), 0, 1)
    arrived = lax.all_to_all(send, "batch", split_axis=0, concat_axis=0, tiled=True)
    arrived = arrived.reshape(batch * seqs * capacity, 2 * width)

    rows_in = arrived[:, :width]
    grad_rows = arrived[:, width:]
    hidden = nn(rows_in, first_weight)
    value, gelu_back = jax.vjp(gelu_tanh, hidden)
    value = value.astype(BF)
    rows_out = nn(value, second_weight).astype(BF)
    grad_hidden = gelu_back(nt(grad_rows, second_weight))[0].astype(BF)
    grad_in = nt(grad_hidden, first_weight).astype(BF)
    back = jnp.concatenate([rows_out, grad_in], axis=-1)
    back = back.reshape(batch, seqs, capacity, 2 * width)
    back = lax.all_to_all(back, "batch", split_axis=0, concat_axis=0, tiled=True)
    back = jnp.swapaxes(back, 0, 1).reshape(seqs, experts * capacity, 2 * width)
    quarter = expert_in.shape[2]
    pieces = first_weight.shape[1] // quarter
    grad_first = tn(rows_in, grad_hidden)
    grad_second = tn(value, grad_rows)
    grad_first = scatter_seq([grad_first[:, j * quarter : (j + 1) * quarter] for j in range(pieces)])
    grad_second = scatter_seq([grad_second[j * quarter : (j + 1) * quarter] for j in range(pieces)])

    picked = jnp.einsum("stc,scd->std", selector, back, preferred_element_type=F32)
    expert_tok = picked[..., :width]
    activations = (mixed + gate * expert_tok).astype(BF)

    grad_gate = jnp.sum(expert_tok * grad_out, axis=-1, keepdims=True)
    grad_prob = jnp.where(chosen, grad_gate, 0.0)
    grad_logits = (
        probs * (grad_prob - jnp.sum(probs * grad_prob, axis=-1, keepdims=True))
    ).astype(BF)
    g_router = tn(routed, grad_logits)
    grad_routed = picked[..., width:] + nt(grad_logits, router_weight)
    g_gain_two = jnp.sum(grad_routed * mixed * scale_two, axis=(0, 1))
    grad_mixed = grad_out + norm_back(grad_routed * gain_two, mixed, scale_two)
    grad_branch = grad_mixed.astype(BF)

    grad_gated = nt(grad_branch, w_back)
    grad_mix = grad_gated * gate_act
    grad_gate_in = (grad_gated * mix * silu_slope(gate_in)).astype(BF)
    behind = scan_end(step, grad_mix, both, rate, True)
    after = prefix(total, behind, rate, True)
    g_back = scatter_sum(tn(gated, grad_branch), 2, BF)
    g_gate_half = scatter_sum(tn(normed, grad_gate_in), 1, BF)
    g_skip = jnp.sum(grad_mix * actf, axis=(0, 1))
    pull, grad_rate, g_log, grad_in_map, grad_out_map = scan_bwd(
        step, act, grad_mix, both, in_rows, ones, rate, init, after, states
    )
    g_log = jnp.sum(g_log, axis=0).T * LN2
    grad_arg = (grad_rate * LN2 + actf * pull) * jax.nn.sigmoid(step_arg)
    g_step_bias = jnp.sum(grad_arg, axis=(0, 1))
    grad_pre = grad_arg.astype(BF)
    g_step = tn(grad_pre, delta)
    grad_proj = jnp.concatenate(
        [nn(grad_pre, w_step), fold(grad_in_map), fold(grad_out_map)], axis=-1
    ).astype(BF)
    g_proj = tn(act, grad_proj)
    grad_act = skip * grad_mix + step * pull + nt(grad_proj, w_proj)
    grad_conv = grad_act * silu_slope(conv_out)
    g_conv_bias = jnp.sum(grad_conv, axis=(0, 1))
    g_taps = jnp.stack(
        [
            jnp.sum(grad_conv * conv_ext[:, lo + k : lo + k + span, :], axis=(0, 1))
            for k in range(CONV)
        ],
        axis=-1,
    )
    rim = shift(grad_conv[:, :HALO, :], "seq", -1)
    longer = jnp.concatenate([grad_conv, rim], axis=1)
    grad_conv_in = sum(
        longer[:, CONV - 1 - k : CONV - 1 - k + span, :] * taps[k] for k in range(CONV)
    ).astype(BF)
    g_conv_half = scatter_sum(tn(normed, grad_conv_in), 0, BF)
    grad_normed = nt(grad_conv_in, w_conv_in) + nt(grad_gate_in, w_gate_in)
    g_gain_one = jnp.sum(grad_normed * block * scale_one, axis=(0, 1))
    input_grad = grad_mixed + norm_back(grad_normed * gain_one, block, scale_one)

    g_chan = jnp.concatenate(
        [
            g_proj,
            g_step,
            g_log,
            g_taps,
            g_conv_bias[:, None],
            g_step_bias[:, None],
            g_skip[:, None],
        ],
        axis=1,
    )
    g_chan = scatter_sum(pad_cols(g_chan, 256), 2, F32)
    g_feat = jnp.concatenate([g_gain_one[:, None], g_gain_two[:, None], g_router], axis=1)
    g_feat = scatter_sum(pad_cols(g_feat, 128), 1, F32)
    at = maps + DT_RANK
    return (
        activations,
        input_grad,
        g_feat[:, 0],
        jnp.concatenate([g_conv_half, g_gate_half], axis=1),
        g_chan[:, at + STATE : at + STATE + CONV],
        g_chan[:, at + STATE + CONV],
        g_chan[:, :maps],
        g_chan[:, maps:at],
        g_chan[:, at + STATE + CONV + 1],
        g_chan[:, at : at + STATE],
        g_chan[:, at + STATE + CONV + 2],
        g_back,
        g_feat[:, 1],
        g_feat[:, 2 : 2 + experts],
        grad_first[None],
        grad_second[None],
    )


def solution(mesh):
    return jax.shard_map(
        shards,
        mesh=mesh,
        in_specs=(
            P("batch", "seq", None),
            P("batch", "seq", None),
            P(),
            P("batch"),
            P("batch", "seq"),
            P("batch", "seq"),
            P(("batch", "seq")),
            P(("batch", "seq"), None),
            P(("batch", "seq"), None),
            P(("batch", "seq")),
            P(("batch", "seq"), None),
            P(("batch", "seq"), None),
            P(("batch", "seq")),
            P(("batch", "seq"), None),
            P(("batch", "seq")),
            P(("batch", "seq"), None),
            P(("batch", "seq")),
            P(("batch", "seq"), None),
            P("batch", None, "seq"),
            P("batch", "seq", None),
        ),
        out_specs=(
            P("batch", "seq", None),
            P("batch", "seq", None),
            P(("batch", "seq")),
            P(("batch", "seq"), None),
            P(("batch", "seq"), None),
            P(("batch", "seq")),
            P(("batch", "seq"), None),
            P(("batch", "seq"), None),
            P(("batch", "seq")),
            P(("batch", "seq"), None),
            P(("batch", "seq")),
            P(("batch", "seq"), None),
            P(("batch", "seq")),
            P(("batch", "seq"), None),
            P("batch", None, "seq"),
            P("batch", "seq", None),
        ),
        check_vma=False,
    )
```

```python
import functools
import math

import jax
import jax.numpy as jnp
from jax import lax
from jax.experimental import pallas as pl
from jax.experimental.pallas import tpu as pltpu
from jax.sharding import PartitionSpec as P

DI = 1536
STATE = 16
DT_RANK = 48
CONV = 4
SEQ_MB = 1
EPSILON = 1e-05
F32 = jnp.float32
BF = jnp.bfloat16
U = 16
CB = 512
CE = 768
VM = 48 << 20
COST = 1
LOG2E = 1.0 / math.log(2.0)
LN2 = math.log(2.0)
HALO = 8


def end_f_kernel(chunks, s_ref, x_ref, bt_ref, r_ref, h_ref):
    r = r_ref[...]
    width = r.shape[1]
    def chunk(c, h):
        rows = pl.ds(pl.multiple_of(c*U,U),U)
        s8 = s_ref[0, rows, :]
        d8 = x_ref[0, rows, :].astype(F32)*s8
        bt = bt_ref[0, c]
        for k in range(U):
            s = jnp.broadcast_to(s8[k:k+1], (STATE,width))
            d = jnp.broadcast_to(d8[k:k+1], (STATE,width))
            b = jnp.broadcast_to(bt[0:STATE, k:k+1], (STATE,width))
            h = jnp.exp2(s*r)*h + d*b
        return h
    h_ref[0] = lax.fori_loop(0, chunks, chunk, jnp.zeros((STATE,width),F32))


def scan_end_f(s, x, bt, r):
    S,T,C = s.shape
    cb=min(CE,C)
    row=pl.BlockSpec((1,T,cb), lambda i,j:(i,0,j))
    return pl.pallas_call(functools.partial(end_f_kernel, T//U),
        grid=(S,C//cb),
        in_specs=[row,row,pl.BlockSpec((1,T//U,2*STATE,U),lambda i,j:(i,0,0,0)),pl.BlockSpec((STATE,cb),lambda i,j:(0,j))],
        out_specs=pl.BlockSpec((1,STATE,cb),lambda i,j:(i,0,j)),
        out_shape=jax.ShapeDtypeStruct((S,STATE,C),F32),
        compiler_params=pltpu.CompilerParams(vmem_limit_bytes=VM),
        cost_estimate=pl.CostEstimate(flops=COST*S*T*C,bytes_accessed=COST*S*T*C,transcendentals=0),
        name="scan_end_f",
    )(s,x,bt,r)


def end_b_kernel(chunks, s_ref, g_ref, bt_ref, r_ref, h_ref, out_ref, go_ref):
    r = r_ref[...]
    width = r.shape[1]
    @pl.when(pl.program_id(1)==0)
    def _():
        go_ref[...]=jnp.zeros_like(go_ref)
    def chunk(c, h):
        c = chunks-1-c
        rows = pl.ds(pl.multiple_of(c*U,U),U)
        s8 = s_ref[0, rows, :]
        g8 = g_ref[0, rows, :]
        bt = bt_ref[0, c]
        go_ref[0, rows, :] += lax.dot_general(g8.astype(BF), h_ref[0, pl.ds(pl.multiple_of(c*U*STATE,U*STATE),U*STATE), :], (((1,),(1,)),((),())), preferred_element_type=F32)
        for k in range(U-1,-1,-1):
            s = jnp.broadcast_to(s8[k:k+1], (STATE,width))
            g = jnp.broadcast_to(g8[k:k+1], (STATE,width))
            cc = jnp.broadcast_to(bt[STATE:2*STATE, k:k+1], (STATE,width))
            h = jnp.exp2(s*r)*(h + g*cc)
        return h
    out_ref[0] = lax.fori_loop(0, chunks, chunk, jnp.zeros((STATE,width),F32))


def scan_end_b(s, g, bt, r, h):
    S,T,C = s.shape
    cb=min(CE,C)
    row=pl.BlockSpec((1,T,cb), lambda i,j:(i,0,j))
    return pl.pallas_call(functools.partial(end_b_kernel, T//U),
        grid=(S,C//cb),
        in_specs=[row,row,pl.BlockSpec((1,T//U,2*STATE,U),lambda i,j:(i,0,0,0)),pl.BlockSpec((STATE,cb),lambda i,j:(0,j)),pl.BlockSpec((1,T*STATE,cb),lambda i,j:(i,0,j))],
        out_specs=[pl.BlockSpec((1,STATE,cb),lambda i,j:(i,0,j)),pl.BlockSpec((1,T,U*STATE),lambda i,j:(i,0,0))],
        out_shape=[jax.ShapeDtypeStruct((S,STATE,C),F32),jax.ShapeDtypeStruct((S,T,U*STATE),F32)],
        compiler_params=pltpu.CompilerParams(vmem_limit_bytes=VM),
        cost_estimate=pl.CostEstimate(flops=COST*S*T*C,bytes_accessed=COST*S*T*C,transcendentals=0),
        name="scan_end_b",
    )(s,g,bt,r,h)


def fwd_kernel(chunks, s_ref, x_ref, bt_ref, l_ref, r_ref, h0_ref, y_ref, h_ref, even, odd):
    r = r_ref[...]
    width = r.shape[1]
    def rows_at(c, size):
        return pl.ds(pl.multiple_of(c*size,size),size)
    def chunk(c, h, mine, other):
        before = jnp.maximum(c-1,0)
        y_ref[0, rows_at(before,U), :] = jnp.dot(l_ref[0, rows_at(before,U), :], other[...], preferred_element_type=F32)
        rows = rows_at(c,U)
        s8 = s_ref[0, rows, :]
        d8 = x_ref[0, rows, :].astype(F32)*s8
        bt = bt_ref[0, c]
        for k in range(U):
            s = jnp.broadcast_to(s8[k:k+1], (STATE,width))
            d = jnp.broadcast_to(d8[k:k+1], (STATE,width))
            b = jnp.broadcast_to(bt[0:STATE, k:k+1], (STATE,width))
            h = jnp.exp2(s*r)*h + d*b
            low = h.astype(BF)
            mine[k*STATE:(k+1)*STATE, :] = low
            h_ref[0, pl.ds(pl.multiple_of(c*U*STATE+k*STATE,STATE),STATE), :] = low
        return h
    def pair(i, h):
        h = chunk(2*i, h, even, odd)
        return chunk(2*i+1, h, odd, even)
    odd[...] = jnp.zeros_like(odd)
    lax.fori_loop(0, chunks//2, pair, h0_ref[0])
    last = pl.ds((chunks-1)*U,U)
    y_ref[0, last, :] = jnp.dot(l_ref[0, last, :], odd[...], preferred_element_type=F32)

def scan_fwd(s, x, bt, l, r, h0):
    S,T,C = s.shape
    cb=min(CB,C)
    row=pl.BlockSpec((1,T,cb), lambda i,j:(i,0,j))
    st=pl.BlockSpec((1,STATE,cb),lambda i,j:(i,0,j))
    return pl.pallas_call(functools.partial(fwd_kernel, T//U),
        grid=(S,C//cb),
        in_specs=[row,row,pl.BlockSpec((1,T//U,2*STATE,U),lambda i,j:(i,0,0,0)),pl.BlockSpec((1,T,U*STATE),lambda i,j:(i,0,0)),pl.BlockSpec((STATE,cb),lambda i,j:(0,j)),st],
        out_specs=[row,pl.BlockSpec((1,T*STATE,cb),lambda i,j:(i,0,j))],
        out_shape=[jax.ShapeDtypeStruct((S,T,C),F32),jax.ShapeDtypeStruct((S,T*STATE,C),BF)],
        scratch_shapes=[pltpu.VMEM((U*STATE,cb),BF)]*2,
        compiler_params=pltpu.CompilerParams(vmem_limit_bytes=VM),
        cost_estimate=pl.CostEstimate(flops=COST*S*T*C,bytes_accessed=COST*S*T*C,transcendentals=0),
        name="scan_fwd",
    )(s,x,bt,l,r,h0)


def bwd_kernel(chunks, s_ref, x_ref, g_ref, bt_ref, l_ref, one_ref, r_ref, h0_ref, m0_ref, h_ref,
               pull_ref, gs_ref, alog_ref, gi_ref, lam_e, fr_e, lam_o, fr_o):
    r = r_ref[...]
    width = r.shape[1]
    j = pl.program_id(1)
    nt=(((1,),(1,)),((),()))
    def rows_at(c, size):
        return pl.ds(pl.multiple_of(c*size,size),size)
    @pl.when(j==0)
    def _():
        gi_ref[...]=jnp.zeros_like(gi_ref)
    lam_o[...] = jnp.zeros_like(lam_o)
    fr_o[...] = jnp.zeros_like(fr_o)
    def sums(c, lam_s, fr_s, first=None):
        rows = rows_at(c,U)
        d8 = (x_ref[0, rows, :].astype(F32)*s_ref[0, rows, :]).astype(BF)
        lam_all = lam_s[...]
        pull_ref[0, rows, :] = jnp.dot(l_ref[0, rows, :], lam_all, preferred_element_type=F32)
        gs_ref[0, rows, :] = jnp.dot(one_ref[...], fr_s[...], preferred_element_type=F32)
        gi = lax.dot_general(d8, lam_all, nt, preferred_element_type=F32)
        if first is not None:
            gi = jnp.where(first, 0.0, gi)
        gi_ref[0, rows, :] += gi
    def chunk(c, carry, mine, other, first=None):
        lam_c, alog = carry
        sums(jnp.minimum(c+1,chunks-1), *other, first)
        lam_s, fr_s = mine
        rows = rows_at(c,U)
        s8 = s_ref[0, rows, :]
        g8 = g_ref[0, rows, :]
        bt = bt_ref[0, c]
        for k in range(U-1,-1,-1):
            s = jnp.broadcast_to(s8[k:k+1], (STATE,width))
            g = jnp.broadcast_to(g8[k:k+1], (STATE,width))
            cc = jnp.broadcast_to(bt[STATE:2*STATE, k:k+1], (STATE,width))
            if k:
                hp = h_ref[0, pl.ds(pl.multiple_of(c*U*STATE+(k-1)*STATE,STATE),STATE), :].astype(F32)
            else:
                hp = h_ref[0, pl.ds(pl.multiple_of(jnp.maximum(c*U*STATE-STATE,0),STATE),STATE), :].astype(F32)
                hp = jnp.where(c==0, h0_ref[0], hp)
            lam = lam_c + g*cc
            lam_c = jnp.exp2(s*r)*lam
            fr = lam_c*hp*r
            alog = alog + fr*s
            lam_s[k*STATE:(k+1)*STATE,:] = lam.astype(BF)
            fr_s[k*STATE:(k+1)*STATE,:] = fr.astype(BF)
        return lam_c, alog
    E=(lam_e,fr_e); O=(lam_o,fr_o)
    def pair(i, carry):
        c = chunks-1-2*i
        carry = chunk(c, carry, E, O, i==0)
        return chunk(c-1, carry, O, E)
    _, alog = lax.fori_loop(0, chunks//2, pair, (m0_ref[0], jnp.zeros((STATE,width),F32)))
    sums(0, *O)
    alog_ref[0] = alog

def scan_bwd(s, x, g, bt, l, one, r, h0, m0, h):
    S,T,C = s.shape
    cb=min(CB,C)
    row=pl.BlockSpec((1,T,cb), lambda i,j:(i,0,j))
    st=pl.BlockSpec((1,STATE,cb),lambda i,j:(i,0,j))
    lo=pl.BlockSpec((1,T,U*STATE),lambda i,j:(i,0,0))
    return pl.pallas_call(functools.partial(bwd_kernel, T//U),
        grid=(S,C//cb),
        in_specs=[row,row,row,pl.BlockSpec((1,T//U,2*STATE,U),lambda i,j:(i,0,0,0)),lo,pl.BlockSpec((U,U*STATE),lambda i,j:(0,0)),pl.BlockSpec((STATE,cb),lambda i,j:(0,j)),st,st,pl.BlockSpec((1,T*STATE,cb),lambda i,j:(i,0,j))],
        out_specs=[row,row,st,lo],
        out_shape=[jax.ShapeDtypeStruct((S,T,C),F32),jax.ShapeDtypeStruct((S,T,C),F32),jax.ShapeDtypeStruct((S,STATE,C),F32),jax.ShapeDtypeStruct((S,T,U*STATE),F32)],
        scratch_shapes=[pltpu.VMEM((U*STATE,cb),BF)]*4,
        compiler_params=pltpu.CompilerParams(vmem_limit_bytes=VM),
        cost_estimate=pl.CostEstimate(flops=COST*S*T*C,bytes_accessed=COST*S*T*C,transcendentals=0),
        name="scan_bwd",
    )(s,x,g,bt,l,one,r,h0,m0,h)


def gelu_and_slope(x):
    root = math.sqrt(2.0 / math.pi)
    square = x * x
    t = jnp.tanh(x * (root + (root * 0.044715) * square))
    half = 0.5 + 0.5 * t
    slope = half + (0.5 * x) * (1.0 - t * t) * (root + (3.0 * root * 0.044715) * square)
    return x * half, slope


def expert_kernel(pieces, tile, x_ref, *refs):
    w_refs = refs[: 2 * pieces]
    back_ref, value_ref, grad_ref, first_s, second_s, out_s, gin_s, sems = refs[-8:]
    j = pl.program_id(0)
    rows, width = out_s.shape
    copies = [
        pltpu.make_async_copy(w_refs[q], (first_s if q < pieces else second_s).at[q % pieces], sems.at[q])
        for q in range(2 * pieces)
    ]

    @pl.when(j == 0)
    def _():
        for q in range(pieces):
            copies[q].start()
            copies[q + pieces].start()

    for q in range(pieces):
        @pl.when(j == q)
        def _():
            copies[q].wait()
            copies[q + pieces].wait()

    def mm(a, b, dims):
        return lax.dot_general(a, b, (dims, ((), ())), preferred_element_type=F32)

    first = first_s[j]
    second = second_s[j]
    for i in range(rows // tile):
        at = slice(i * tile, (i + 1) * tile)
        hidden = mm(x_ref[at, :width], first, ((1,), (0,)))
        grad = mm(x_ref[at, width:], second, ((1,), (1,)))
        value, slope = gelu_and_slope(hidden)
        value = value.astype(BF)
        grad = (grad * slope).astype(BF)
        value_ref[at, :] = value
        grad_ref[at, :] = grad
        out = mm(value, second, ((1,), (0,)))
        gin = mm(grad, first, ((1,), (1,)))

        @pl.when(j == 0)
        def _():
            out_s[at, :] = out
            gin_s[at, :] = gin

        @pl.when(j > 0)
        def _():
            out_s[at, :] += out
            gin_s[at, :] += gin

    @pl.when(j == pieces - 1)
    def _():
        back_ref[:, :width] = out_s[...].astype(BF)
        back_ref[:, width:] = gin_s[...].astype(BF)


def expert_call(x, firsts, seconds, part, groups, shared):
    rows, width = x.shape[0], x.shape[1] // 2
    pieces = len(firsts)
    quarter = firsts[0].shape[1]
    tile = math.gcd(rows, 320)
    wide = pl.BlockSpec((rows, quarter), lambda j: (part, j))
    anywhere = pl.BlockSpec(memory_space=pl.ANY)
    whole = pl.BlockSpec((rows, 2 * width), lambda j: (0, 0))
    big = jax.ShapeDtypeStruct((groups * rows, pieces * quarter), BF)
    count = 1 + 2 * pieces
    return pl.pallas_call(
        functools.partial(expert_kernel, pieces, tile),
        grid=(pieces,),
        in_specs=[whole] + [anywhere] * (2 * pieces + len(shared)),
        out_specs=[whole, wide, wide],
        out_shape=[jax.ShapeDtypeStruct((rows, 2 * width), BF), big, big],
        scratch_shapes=[
            pltpu.VMEM((pieces, width, quarter), BF),
            pltpu.VMEM((pieces, quarter, width), BF),
            pltpu.VMEM((rows, width), F32),
            pltpu.VMEM((rows, width), F32),
            pltpu.SemaphoreType.DMA((2 * pieces,)),
        ],
        input_output_aliases={count: 1, count + 1: 2} if shared else {},
        compiler_params=pltpu.CompilerParams(vmem_limit_bytes=VM),
        cost_estimate=pl.CostEstimate(
            flops=8 * rows * width * quarter * pieces,
            bytes_accessed=4 * pieces * width * quarter + 16 * rows * width,
            transcendentals=rows * quarter * pieces,
        ),
        name="expert",
    )(x, *firsts, *seconds, *shared)


def own_rows(span):
    return jnp.arange(span)[:, None] % U == jnp.arange(U * STATE)[None] // STATE


def state_picker():
    return (jnp.arange(STATE)[:, None] == jnp.arange(U * STATE)[None] % STATE).astype(BF)


def fold(z):
    z = jnp.where(own_rows(z.shape[1]), z, 0).astype(BF)
    return nt(z, state_picker())


def spread_rows(m):
    wide = nn(m.astype(BF), state_picker())
    return jnp.where(own_rows(m.shape[1]), wide, 0).astype(BF)


def bits_of(axis):
    return lax.axis_size(axis).bit_length() - 1


def my_bit(axis, k):
    return (lax.axis_index(axis) >> k) & 1


def swap(x, axis, k):
    count = lax.axis_size(axis)
    return lax.ppermute(x, axis, [(i, i ^ (1 << k)) for i in range(count)])


def shift(x, axis, distance):
    count = lax.axis_size(axis)
    return lax.ppermute(
        x, axis, [(i, i + distance) for i in range(count) if 0 <= i + distance < count]
    )


def joined_pair(x, other, axis, k, place):
    high = my_bit(axis, k) == 1
    return jnp.where(
        high,
        jnp.concatenate([other, x], axis=place),
        jnp.concatenate([x, other], axis=place),
    )


def from_batch(x):
    copies = jnp.broadcast_to(x[None], (lax.axis_size("batch"),) + x.shape)
    return lax.all_to_all(copies, "batch", split_axis=0, concat_axis=0, tiled=True)


def over_seq(x):
    bits = bits_of("seq")
    out = x.reshape(x.shape[:1] + (1,) * bits + x.shape[1:])
    for k in reversed(range(bits)):
        out = joined_pair(out, swap(out, "seq", k), "seq", k, bits - k)
    return out.reshape((-1,) + x.shape[2:])


def over_batch(x):
    got = lax.all_to_all(x.astype(BF), "batch", split_axis=0, concat_axis=0, tiled=True)
    return jnp.sum(got.astype(F32), axis=0)


def halved(x, k, place):
    bit = my_bit("seq", k)
    mine = lax.dynamic_index_in_dim(x, bit, place, True)
    theirs = lax.dynamic_index_in_dim(x, 1 - bit, place, True).astype(BF)
    return mine + swap(theirs, "seq", k).astype(F32)


def scatter_sum(x):
    bits = bits_of("seq")
    rows = x.shape[0] // (lax.axis_size("batch") << bits)
    out = x.reshape((lax.axis_size("batch"),) + (2,) * bits + (rows,) + x.shape[1:])
    for k in range(bits):
        out = halved(out, k, bits - k)
    return over_batch(out).reshape((rows,) + x.shape[1:])


def gather_seq(x, event):
    parts = [x]
    for k in reversed(range(bits_of("seq"))):
        more = [swap(p, "seq", k) for p in parts]
        parts = parts + (after(more, event) if k else more)
    count = len(parts)
    order = []
    for k in reversed(range(bits_of("seq"))):
        order = (order or [0]) + [o ^ (1 << k) for o in (order or [0])]
    return [parts[order.index(j)] for j in range(count)]


def scatter_seq(parts, k, event):
    bit = 1 << k
    moved = {j ^ bit: swap(p.astype(BF), "seq", k) for j, p in parts.items() if j & bit}
    moved = after(moved, event)
    return {j: p + moved[j].astype(F32) for j, p in parts.items() if not j & bit}


def totals_of(total):
    levels = []
    for k in range(bits_of("seq")):
        other = swap(total, "seq", k)
        levels.append((total, other))
        total = total + other
    return levels


def prefix(levels, state, rate, backward):
    before = jnp.zeros_like(state)
    before_total = jnp.zeros_like(levels[0][0])
    for k, (total, other_total) in enumerate(levels):
        other = swap(state.astype(BF), "seq", k).astype(F32)
        first = my_bit("seq", k) == (0 if backward else 1)
        before = jnp.where(
            first, before + jnp.exp2(before_total[:, None, :] * rate) * other, before
        )
        before_total = jnp.where(first, before_total + other_total, before_total)
        if k + 1 < len(levels):
            near = jnp.where(first, state, other)
            far = jnp.where(first, other, state)
            near_total = jnp.where(first, total, other_total)
            state = near + jnp.exp2(near_total[:, None, :] * rate) * far
    return before


def after(value, event):
    return lax.optimization_barrier((value, event))[0]


def mm(left, right, dims):
    return lax.dot_general(left, right, (dims, ((), ())), preferred_element_type=F32)


def nn(left, right):
    return mm(left, right, ((left.ndim - 1,), (0,)))


def nt(left, right):
    return mm(left, right, ((left.ndim - 1,), (1,)))


def tn(left, right):
    lead = tuple(range(left.ndim - 1))
    return mm(left, right, (lead, lead))


def silu_slope(v):
    s = jax.nn.sigmoid(v)
    return s * (1.0 + v * (1.0 - s))


def norm_back(grad_norm, x, scale):
    return scale * grad_norm - x * scale**3 * jnp.mean(grad_norm * x, axis=-1, keepdims=True)


def gelu_tanh(v):
    return jax.nn.gelu(v, approximate=True)


def rms(x):
    return lax.rsqrt(jnp.mean(x * x, axis=-1, keepdims=True) + EPSILON)


def pad_cols(x, width):
    return jnp.pad(x, ((0, 0), (0, width - x.shape[1])))


def shards(
    tokens,
    cotangent,
    lengths,
    order,
    expert_route,
    slot_index,
    norm_gain,
    in_proj,
    conv_weight,
    conv_bias,
    x_proj,
    dt_proj,
    dt_bias,
    a_log,
    skip_gain,
    out_proj,
    moe_gain,
    router,
    expert_in,
    expert_out,
):
    seqs, span, width = tokens.shape
    batch = lax.axis_size("batch")
    experts = expert_in.shape[0] * batch
    capacity = max(2, (5 * SEQ_MB * span + 4 * experts - 1) // (4 * experts))
    maps = DT_RANK + 2 * STATE
    lo = HALO - (CONV - 1)
    groups = 2
    size = seqs // groups

    rows = in_proj.shape[0]
    chan = jnp.concatenate(
        [
            x_proj,
            dt_proj,
            a_log,
            conv_weight,
            conv_bias[:, None],
            dt_bias[:, None],
            skip_gain[:, None],
        ],
        axis=1,
    )
    feat = jnp.concatenate([norm_gain[:, None], moe_gain[:, None], router], axis=1)
    cut = 1024
    first_set = from_batch(in_proj[:, :cut])
    later = jnp.concatenate([in_proj[:, DI:], out_proj.reshape(rows, 2 * width)], axis=1)
    later = after(later, first_set)
    later = lax.all_gather(later, ("batch", "seq"), axis=0, tiled=True)
    w_gate_in = later[:, :DI]
    w_back = later[:, DI:].reshape(DI, width)
    first_set = over_seq(first_set)
    second_set = over_seq(
        from_batch(
            jnp.concatenate(
                [in_proj[:, cut:DI], pad_cols(chan, 256).reshape(rows, 512), pad_cols(feat, 128)],
                axis=1,
            )
        )
    )
    w_conv_in = jnp.concatenate([first_set, second_set[:, : DI - cut]], axis=1)
    chan = second_set[:, DI - cut : DI - cut + 512].reshape(-1, 256)
    feat = second_set[:, DI - cut + 512 :]
    gain_one = feat[:, 0].astype(F32)
    gain_two = feat[:, 1].astype(F32)
    router_weight = feat[:, 2 : 2 + experts]
    w_proj = chan[:, :maps]
    at = maps + DT_RANK
    w_step = chan[:, maps:at]
    rate = -jnp.exp(chan[:, at : at + STATE].astype(F32)).T * LOG2E
    at = at + STATE
    taps = chan[:, at : at + CONV].astype(F32).T
    bias_conv = chan[:, at + CONV].astype(F32)
    bias_step = chan[:, at + CONV + 1].astype(F32)
    skip = chan[:, at + CONV + 2].astype(F32)

    halo_all = shift(tokens[:, span - HALO :, :], "seq", 1)
    tail = jnp.arange(HALO)[:, None] >= lo
    halo_all = jnp.where(tail, halo_all, 0)


    positions = lax.axis_index("seq") * span + jnp.arange(span, dtype=jnp.int32)
    row_length = jnp.sum(
        jnp.where(
            order[:, None] == jnp.arange(lengths.shape[0], dtype=jnp.int32)[None, :],
            lengths[None, :],
            0,
        ),
        axis=1,
    )
    keep_all = (positions[None, :] < row_length[:, None]).astype(F32)
    ones = (jnp.arange(U)[:, None] == jnp.arange(U * STATE)[None] // STATE).astype(BF)
    slots = jnp.arange(experts * capacity, dtype=jnp.int32)
    expert_ids = jnp.arange(experts, dtype=jnp.int32)

    class Part:
        pass

    def forward(m, event, second_event):
        p = Part()
        here = slice(m * size, (m + 1) * size)
        own = tokens[here]
        if event is not None:
            own = after(own, event)
        p.block = own.astype(F32)
        p.scale_one = rms(p.block)
        ext = jnp.concatenate([halo_all[here], own], axis=1).astype(F32)
        normed_ext = (ext * rms(ext) * gain_one).astype(BF)
        p.normed = normed_ext[:, HALO:]
        p.conv_ext = nn(normed_ext, w_conv_in)
        p.conv_out = bias_conv + sum(
            p.conv_ext[:, lo + k : lo + k + span, :] * taps[k] for k in range(CONV)
        )
        p.act = jax.nn.silu(p.conv_out).astype(BF)
        projected = nn(p.act, w_proj)
        p.delta = projected[..., :DT_RANK].astype(BF)
        input_map = projected[..., DT_RANK : DT_RANK + STATE]
        output_map = projected[..., DT_RANK + STATE :]
        p.step_arg = nt(p.delta, w_step) + bias_step
        p.step = jax.nn.softplus(p.step_arg)
        p.levels = totals_of(jnp.sum(p.step, axis=1))
        p.both = jnp.swapaxes(
            projected[..., DT_RANK:].reshape(size, span // U, U, 2 * STATE), 2, 3
        )
        p.in_rows = spread_rows(input_map)
        out_rows = spread_rows(output_map)
        end = scan_end_f(p.step, p.act, p.both, rate)
        p.init = prefix(p.levels, end, rate, False)
        if second_event is not None:
            p.init = after(p.init, second_event)
        p.gate_in = nn(p.normed, w_gate_in)
        y, p.states = scan_fwd(p.step, p.act, p.both, out_rows, rate, p.init)
        p.actf = p.act.astype(F32)
        p.mix = y + skip * p.actf
        p.gate_act = jax.nn.silu(p.gate_in)
        p.gated = (p.mix * p.gate_act).astype(BF)
        p.mixed = p.block + nn(p.gated, w_back)
        p.scale_two = rms(p.mixed)
        p.routed = (p.mixed * p.scale_two * gain_two).astype(BF)
        p.probs = jax.nn.softmax(nn(p.routed, router_weight), axis=-1)
        route = expert_route[here]
        slot = slot_index[here]
        kept = slot >= 0
        target = jnp.where(kept, route * capacity + slot, -1)
        p.selector = (target[..., None] == slots).astype(BF)
        p.chosen = jnp.logical_and(route[..., None] == expert_ids, kept[..., None])
        p.gate = jnp.sum(jnp.where(p.chosen, p.probs, 0.0), axis=-1)[..., None]
        p.grad_out = cotangent[here].astype(F32) * keep_all[here][..., None]
        grad_value = (p.gate * p.grad_out).astype(BF)
        packed = jnp.concatenate([p.routed, grad_value], axis=-1)
        send = jnp.einsum("stc,std->scd", p.selector, packed, preferred_element_type=F32)
        send = jnp.swapaxes(send.astype(BF).reshape(size, batch, capacity, 2 * width), 0, 1)
        p.send = send
        p.arrived = lax.all_to_all(send, "batch", split_axis=0, concat_axis=0, tiled=True)
        return p

    def expert(m, shared):
        p = parts[m]
        p.rows_in = p.arrived.reshape(batch * size * capacity, 2 * width)
        p.back, *shared = expert_call(
            p.rows_in, first_parts, second_parts, m, groups, shared
        )
        back = p.back.reshape(batch, size, capacity, 2 * width)
        back = lax.all_to_all(back, "batch", split_axis=0, concat_axis=0, tiled=True)
        p.returned = jnp.swapaxes(back, 0, 1).reshape(size, experts * capacity, 2 * width)
        return shared

    def backward_router(p):
        picked = jnp.einsum("stc,scd->std", p.selector, p.returned, preferred_element_type=F32)
        expert_tok = picked[..., :width]
        p.activations = (p.mixed + p.gate * expert_tok).astype(BF)
        grad_gate = jnp.sum(expert_tok * p.grad_out, axis=-1, keepdims=True)
        grad_prob = jnp.where(p.chosen, grad_gate, 0.0)
        grad_logits = (
            p.probs * (grad_prob - jnp.sum(p.probs * grad_prob, axis=-1, keepdims=True))
        ).astype(BF)
        p.g_router = tn(p.routed, grad_logits)
        grad_routed = picked[..., width:] + nt(grad_logits, router_weight)
        p.g_gain_two = jnp.sum(grad_routed * p.mixed * p.scale_two, axis=(0, 1))
        p.grad_mixed = p.grad_out + norm_back(grad_routed * gain_two, p.mixed, p.scale_two)
        p.grad_branch = p.grad_mixed.astype(BF)
        grad_gated = nt(p.grad_branch, w_back)
        p.grad_mix = grad_gated * p.gate_act
        p.grad_gate_in = (grad_gated * p.mix * silu_slope(p.gate_in)).astype(BF)
        p.behind, p.grad_out_map = scan_end_b(p.step, p.grad_mix, p.both, rate, p.states)
        p.after = prefix(p.levels, p.behind, rate, True)
        p.g_skip = jnp.sum(p.grad_mix * p.actf, axis=(0, 1))

    def backward_mixer(p):
        pull, grad_rate, g_log, grad_in_map = scan_bwd(
            p.step, p.act, p.grad_mix, p.both, p.in_rows, ones, rate, p.init, p.after, p.states
        )
        p.pull = pull
        p.g_log = jnp.sum(g_log, axis=0).T * LN2
        grad_arg = (grad_rate * LN2 + p.actf * pull) * jax.nn.sigmoid(p.step_arg)
        p.g_step_bias = jnp.sum(grad_arg, axis=(0, 1))
        grad_pre = grad_arg.astype(BF)
        p.g_step = tn(grad_pre, p.delta)
        grad_proj = jnp.concatenate(
            [nn(grad_pre, w_step), fold(grad_in_map), fold(p.grad_out_map)], axis=-1
        ).astype(BF)
        p.g_proj = tn(p.act, grad_proj)
        grad_act = skip * p.grad_mix + p.step * pull + nt(grad_proj, w_proj)
        grad_conv = grad_act * silu_slope(p.conv_out)
        p.g_conv_bias = jnp.sum(grad_conv, axis=(0, 1))
        p.g_taps = jnp.stack(
            [
                jnp.sum(grad_conv * p.conv_ext[:, lo + k : lo + k + span, :], axis=(0, 1))
                for k in range(CONV)
            ],
            axis=-1,
        )
        rim = shift(grad_conv[:, :HALO, :], "seq", -1)
        longer = jnp.concatenate([grad_conv, rim], axis=1)
        p.grad_conv_in = sum(
            longer[:, CONV - 1 - k : CONV - 1 - k + span, :] * taps[k] for k in range(CONV)
        ).astype(BF)

    def backward_input(p):
        grad_normed = nt(p.grad_conv_in, w_conv_in) + nt(p.grad_gate_in, w_gate_in)
        p.input_grad = p.grad_mixed + norm_back(grad_normed * gain_one, p.block, p.scale_one)

    parts = []
    parts.append(forward(0, None, None))
    first_parts = gather_seq(after(expert_in[0], parts[0].init), parts[0].send)
    for m in range(1, groups):
        parts.append(forward(m, parts[-1].send, parts[-1].arrived))
    second_parts = gather_seq(after(expert_out[0], parts[-1].init), parts[-1].mixed)
    shared = ()
    for m in range(groups):
        shared = expert(m, shared)
    values, grad_hidden = shared

    def joined(name):
        return jnp.concatenate([getattr(p, name) for p in parts], axis=0)

    def added(name):
        return functools.reduce(jnp.add, [getattr(p, name) for p in parts])

    def added_products(left, right):
        return functools.reduce(
            jnp.add, [tn(getattr(p, left), getattr(p, right)) for p in parts]
        )

    quarter = expert_in.shape[2]
    rows_in = joined("rows_in")
    rows_in, values, grad_hidden = after((rows_in, values, grad_hidden), parts[-1].back)
    grad_first = []
    grad_second = []
    for q in range(len(first_parts)):
        at = slice(q * quarter, (q + 1) * quarter)
        grad_first.append(tn(rows_in[:, :width], grad_hidden[:, at]))
        grad_second.append(tn(values[:, at], rows_in[:, width:]))

    parts[0].returned = after(parts[0].returned, parts[-1].back)
    backward_router(parts[0])
    for p, earlier in zip(parts[1:], parts):
        p.returned = after(p.returned, earlier.grad_mix)
        backward_router(p)
    g_feat = jnp.concatenate([added("g_gain_two")[:, None], added("g_router")], axis=1)
    background = jnp.concatenate(
        [
            added_products("normed", "grad_gate_in").astype(BF),
            added_products("gated", "grad_branch").astype(BF).reshape(-1, 2 * width),
            pad_cols(g_feat, 128).astype(BF),
        ],
        axis=1,
    )
    background = lax.psum_scatter(background, ("batch", "seq"), scatter_dimension=0, tiled=True)
    background = background.astype(F32)
    g_gate_half = background[:, :DI]
    g_back = background[:, DI : 2 * DI].reshape(-1, width)
    g_feat = background[:, 2 * DI :]
    grad_first = dict(enumerate(grad_first))
    grad_second = dict(enumerate(grad_second))
    grad_first = scatter_seq(grad_first, 0, parts[0].grad_mix)
    grad_second = scatter_seq(grad_second, 0, parts[0].grad_mix)
    for p in parts:
        backward_mixer(p)
    g_chan = jnp.concatenate(
        [
            added("g_proj"),
            added("g_step"),
            added("g_log"),
            added("g_taps"),
            added("g_conv_bias")[:, None],
            added("g_step_bias")[:, None],
            added("g_skip")[:, None],
        ],
        axis=1,
    )
    g_chan = pad_cols(g_chan, 256).reshape(-1, 512)
    g_conv_half = added_products("normed", "grad_conv_in")
    g_rest = scatter_sum(jnp.concatenate([g_conv_half, g_chan], axis=1))
    for p in parts:
        p.grad_conv_in = after(p.grad_conv_in, g_conv_half)
    for k in range(1, bits_of("seq")):
        grad_first = scatter_seq(grad_first, k, g_conv_half)
        grad_second = scatter_seq(grad_second, k, g_conv_half)
    g_conv_half = g_rest[:, :DI]
    g_chan = g_rest[:, DI:].reshape(-1, 256)
    grad_first = grad_first[0]
    grad_second = grad_second[0]
    for p in parts:
        backward_input(p)
    g_in = jnp.concatenate([g_conv_half, g_gate_half], axis=1)
    g_gain_one = jnp.sum(g_in * in_proj.astype(F32), axis=1) / norm_gain.astype(F32)
    at = maps + DT_RANK
    return (
        joined("activations"),
        joined("input_grad"),
        g_gain_one,
        g_in,
        g_chan[:, at + STATE : at + STATE + CONV],
        g_chan[:, at + STATE + CONV],
        g_chan[:, :maps],
        g_chan[:, maps:at],
        g_chan[:, at + STATE + CONV + 1],
        g_chan[:, at : at + STATE],
        g_chan[:, at + STATE + CONV + 2],
        g_back,
        g_feat[:, 0],
        g_feat[:, 1 : 1 + experts],
        grad_first[None],
        grad_second[None],
    )


def solution(mesh):
    return jax.shard_map(
        shards,
        mesh=mesh,
        in_specs=(
            P("batch", "seq", None),
            P("batch", "seq", None),
            P(),
            P("batch"),
            P("batch", "seq"),
            P("batch", "seq"),
            P(("batch", "seq")),
            P(("batch", "seq"), None),
            P(("batch", "seq"), None),
            P(("batch", "seq")),
            P(("batch", "seq"), None),
            P(("batch", "seq"), None),
            P(("batch", "seq")),
            P(("batch", "seq"), None),
            P(("batch", "seq")),
            P(("batch", "seq"), None),
            P(("batch", "seq")),
            P(("batch", "seq"), None),
            P("batch", None, "seq"),
            P("batch", "seq", None),
        ),
        out_specs=(
            P("batch", "seq", None),
            P("batch", "seq", None),
            P(("batch", "seq")),
            P(("batch", "seq"), None),
            P(("batch", "seq"), None),
            P(("batch", "seq")),
            P(("batch", "seq"), None),
            P(("batch", "seq"), None),
            P(("batch", "seq")),
            P(("batch", "seq"), None),
            P(("batch", "seq")),
            P(("batch", "seq"), None),
            P(("batch", "seq")),
            P(("batch", "seq"), None),
            P("batch", None, "seq"),
            P("batch", "seq", None),
        ),
        check_vma=False,
    )
```

```python
import functools
import math

import jax
import jax.numpy as jnp
from jax import lax
from jax.experimental import pallas as pl
from jax.experimental.pallas import tpu as pltpu
from jax.sharding import PartitionSpec as P

DI = 1536
STATE = 16
DT_RANK = 48
CONV = 4
SEQ_MB = 1
EPSILON = 1e-05
F32 = jnp.float32
BF = jnp.bfloat16
U = 16
CB = 512
CE = 768
VM = 48 << 20
EXPERT_VM = 48 << 20
COST = 1
LOG2E = 1.0 / math.log(2.0)
LN2 = math.log(2.0)
HALO = 8


def end_f_kernel(chunks, s_ref, x_ref, bt_ref, r_ref, h_ref):
    r = r_ref[...]
    width = r.shape[1]
    def chunk(c, h):
        rows = pl.ds(pl.multiple_of(c*U,U),U)
        s8 = s_ref[0, rows, :]
        d8 = x_ref[0, rows, :].astype(F32)*s8
        bt = bt_ref[0, c]
        for k in range(U):
            s = jnp.broadcast_to(s8[k:k+1], (STATE,width))
            d = jnp.broadcast_to(d8[k:k+1], (STATE,width))
            b = jnp.broadcast_to(bt[0:STATE, k:k+1], (STATE,width))
            h = jnp.exp2(s*r)*h + d*b
        return h
    h_ref[0] = lax.fori_loop(0, chunks, chunk, jnp.zeros((STATE,width),F32))


def scan_end_f(s, x, bt, r):
    S,T,C = s.shape
    cb=min(CE,C)
    row=pl.BlockSpec((1,T,cb), lambda i,j:(i,0,j))
    return pl.pallas_call(functools.partial(end_f_kernel, T//U),
        grid=(S,C//cb),
        in_specs=[row,row,pl.BlockSpec((1,T//U,2*STATE,U),lambda i,j:(i,0,0,0)),pl.BlockSpec((STATE,cb),lambda i,j:(0,j))],
        out_specs=pl.BlockSpec((1,STATE,cb),lambda i,j:(i,0,j)),
        out_shape=jax.ShapeDtypeStruct((S,STATE,C),F32),
        compiler_params=pltpu.CompilerParams(vmem_limit_bytes=VM),
        cost_estimate=pl.CostEstimate(flops=COST*S*T*C,bytes_accessed=COST*S*T*C,transcendentals=0),
        name="scan_end_f",
    )(s,x,bt,r)


def end_b_kernel(chunks, s_ref, g_ref, bt_ref, r_ref, h_ref, out_ref, go_ref):
    r = r_ref[...]
    width = r.shape[1]
    @pl.when(pl.program_id(1)==0)
    def _():
        go_ref[...]=jnp.zeros_like(go_ref)
    def chunk(c, h):
        c = chunks-1-c
        rows = pl.ds(pl.multiple_of(c*U,U),U)
        s8 = s_ref[0, rows, :]
        g8 = g_ref[0, rows, :]
        bt = bt_ref[0, c]
        go_ref[0, rows, :] += lax.dot_general(g8.astype(BF), h_ref[0, pl.ds(pl.multiple_of(c*U*STATE,U*STATE),U*STATE), :], (((1,),(1,)),((),())), preferred_element_type=F32)
        for k in range(U-1,-1,-1):
            s = jnp.broadcast_to(s8[k:k+1], (STATE,width))
            g = jnp.broadcast_to(g8[k:k+1], (STATE,width))
            cc = jnp.broadcast_to(bt[STATE:2*STATE, k:k+1], (STATE,width))
            h = jnp.exp2(s*r)*(h + g*cc)
        return h
    out_ref[0] = lax.fori_loop(0, chunks, chunk, jnp.zeros((STATE,width),F32))


def scan_end_b(s, g, bt, r, h):
    S,T,C = s.shape
    cb=min(CE,C)
    row=pl.BlockSpec((1,T,cb), lambda i,j:(i,0,j))
    return pl.pallas_call(functools.partial(end_b_kernel, T//U),
        grid=(S,C//cb),
        in_specs=[row,row,pl.BlockSpec((1,T//U,2*STATE,U),lambda i,j:(i,0,0,0)),pl.BlockSpec((STATE,cb),lambda i,j:(0,j)),pl.BlockSpec((1,T*STATE,cb),lambda i,j:(i,0,j))],
        out_specs=[pl.BlockSpec((1,STATE,cb),lambda i,j:(i,0,j)),pl.BlockSpec((1,T,U*STATE),lambda i,j:(i,0,0))],
        out_shape=[jax.ShapeDtypeStruct((S,STATE,C),F32),jax.ShapeDtypeStruct((S,T,U*STATE),F32)],
        compiler_params=pltpu.CompilerParams(vmem_limit_bytes=VM),
        cost_estimate=pl.CostEstimate(flops=COST*S*T*C,bytes_accessed=COST*S*T*C,transcendentals=0),
        name="scan_end_b",
    )(s,g,bt,r,h)


def fwd_kernel(chunks, s_ref, x_ref, bt_ref, l_ref, r_ref, h0_ref, y_ref, h_ref, even, odd):
    r = r_ref[...]
    width = r.shape[1]
    def rows_at(c, size):
        return pl.ds(pl.multiple_of(c*size,size),size)
    def chunk(c, h, mine, other):
        before = jnp.maximum(c-1,0)
        y_ref[0, rows_at(before,U), :] = jnp.dot(l_ref[0, rows_at(before,U), :], other[...], preferred_element_type=F32)
        rows = rows_at(c,U)
        s8 = s_ref[0, rows, :]
        d8 = x_ref[0, rows, :].astype(F32)*s8
        bt = bt_ref[0, c]
        for k in range(U):
            s = jnp.broadcast_to(s8[k:k+1], (STATE,width))
            d = jnp.broadcast_to(d8[k:k+1], (STATE,width))
            b = jnp.broadcast_to(bt[0:STATE, k:k+1], (STATE,width))
            h = jnp.exp2(s*r)*h + d*b
            low = h.astype(BF)
            mine[k*STATE:(k+1)*STATE, :] = low
            h_ref[0, pl.ds(pl.multiple_of(c*U*STATE+k*STATE,STATE),STATE), :] = low
        return h
    def pair(i, h):
        h = chunk(2*i, h, even, odd)
        return chunk(2*i+1, h, odd, even)
    odd[...] = jnp.zeros_like(odd)
    lax.fori_loop(0, chunks//2, pair, h0_ref[0])
    last = pl.ds((chunks-1)*U,U)
    y_ref[0, last, :] = jnp.dot(l_ref[0, last, :], odd[...], preferred_element_type=F32)

def scan_fwd(s, x, bt, l, r, h0):
    S,T,C = s.shape
    cb=min(CB,C)
    row=pl.BlockSpec((1,T,cb), lambda i,j:(i,0,j))
    st=pl.BlockSpec((1,STATE,cb),lambda i,j:(i,0,j))
    return pl.pallas_call(functools.partial(fwd_kernel, T//U),
        grid=(S,C//cb),
        in_specs=[row,row,pl.BlockSpec((1,T//U,2*STATE,U),lambda i,j:(i,0,0,0)),pl.BlockSpec((1,T,U*STATE),lambda i,j:(i,0,0)),pl.BlockSpec((STATE,cb),lambda i,j:(0,j)),st],
        out_specs=[row,pl.BlockSpec((1,T*STATE,cb),lambda i,j:(i,0,j))],
        out_shape=[jax.ShapeDtypeStruct((S,T,C),F32),jax.ShapeDtypeStruct((S,T*STATE,C),BF)],
        scratch_shapes=[pltpu.VMEM((U*STATE,cb),BF)]*2,
        compiler_params=pltpu.CompilerParams(vmem_limit_bytes=VM),
        cost_estimate=pl.CostEstimate(flops=COST*S*T*C,bytes_accessed=COST*S*T*C,transcendentals=0),
        name="scan_fwd",
    )(s,x,bt,l,r,h0)


def bwd_kernel(chunks, s_ref, x_ref, g_ref, bt_ref, l_ref, one_ref, r_ref, k_ref, h0_ref, m0_ref, h_ref,
               pre_ref, base_ref, bias_ref, alog_ref, gi_ref, lam_e, fr_e, lam_o, fr_o):
    r = r_ref[...]
    width = r.shape[1]
    j = pl.program_id(1)
    nt=(((1,),(1,)),((),()))
    def rows_at(c, size):
        return pl.ds(pl.multiple_of(c*size,size),size)
    @pl.when(j==0)
    def _():
        gi_ref[...]=jnp.zeros_like(gi_ref)
    bias_ref[...] = jnp.zeros_like(bias_ref)
    lam_o[...] = jnp.zeros_like(lam_o)
    fr_o[...] = jnp.zeros_like(fr_o)
    def sums(c, lam_s, fr_s, first=None):
        rows = rows_at(c,U)
        s8 = s_ref[0, rows, :]
        x8 = x_ref[0, rows, :].astype(F32)
        d8 = (x8*s8).astype(BF)
        lam_all = lam_s[...]
        pull = jnp.dot(l_ref[0, rows, :], lam_all, preferred_element_type=F32)
        gs = jnp.dot(one_ref[...], fr_s[...], preferred_element_type=F32)
        slope = jnp.where(s8 < 0.03, s8*(1.0-s8*(0.5-s8*(1.0/6.0))), 1.0-jnp.exp(-s8))
        arg = (gs*LN2 + x8*pull)*slope
        pre_ref[0, rows, :] = arg.astype(BF)
        base_ref[0, rows, :] = k_ref[...]*g_ref[0, rows, :] + s8*pull
        part = arg[:8]+arg[8:]
        gi = lax.dot_general(d8, lam_all, nt, preferred_element_type=F32)
        if first is not None:
            gi = jnp.where(first, 0.0, gi)
            part = jnp.where(first, 0.0, part)
        gi_ref[0, rows, :] += gi
        bias_ref[0] += part
    def chunk(c, carry, mine, other, first=None):
        lam_c, alog = carry
        sums(jnp.minimum(c+1,chunks-1), *other, first)
        lam_s, fr_s = mine
        rows = rows_at(c,U)
        s8 = s_ref[0, rows, :]
        g8 = g_ref[0, rows, :]
        bt = bt_ref[0, c]
        for k in range(U-1,-1,-1):
            s = jnp.broadcast_to(s8[k:k+1], (STATE,width))
            g = jnp.broadcast_to(g8[k:k+1], (STATE,width))
            cc = jnp.broadcast_to(bt[STATE:2*STATE, k:k+1], (STATE,width))
            if k:
                hp = h_ref[0, pl.ds(pl.multiple_of(c*U*STATE+(k-1)*STATE,STATE),STATE), :].astype(F32)
            else:
                hp = h_ref[0, pl.ds(pl.multiple_of(jnp.maximum(c*U*STATE-STATE,0),STATE),STATE), :].astype(F32)
                hp = jnp.where(c==0, h0_ref[0], hp)
            lam = lam_c + g*cc
            lam_c = jnp.exp2(s*r)*lam
            fr = lam_c*hp*r
            alog = alog + fr*s
            lam_s[k*STATE:(k+1)*STATE,:] = lam.astype(BF)
            fr_s[k*STATE:(k+1)*STATE,:] = fr.astype(BF)
        return lam_c, alog
    E=(lam_e,fr_e); O=(lam_o,fr_o)
    def pair(i, carry):
        c = chunks-1-2*i
        carry = chunk(c, carry, E, O, i==0)
        return chunk(c-1, carry, O, E)
    _, alog = lax.fori_loop(0, chunks//2, pair, (m0_ref[0], jnp.zeros((STATE,width),F32)))
    sums(0, *O)
    alog_ref[0] = alog

def scan_bwd(s, x, g, bt, l, one, r, k, h0, m0, h):
    S,T,C = s.shape
    cb=min(CB,C)
    row=pl.BlockSpec((1,T,cb), lambda i,j:(i,0,j))
    st=pl.BlockSpec((1,STATE,cb),lambda i,j:(i,0,j))
    lo=pl.BlockSpec((1,T,U*STATE),lambda i,j:(i,0,0))
    return pl.pallas_call(functools.partial(bwd_kernel, T//U),
        grid=(S,C//cb),
        in_specs=[row,row,row,pl.BlockSpec((1,T//U,2*STATE,U),lambda i,j:(i,0,0,0)),lo,pl.BlockSpec((U,U*STATE),lambda i,j:(0,0)),pl.BlockSpec((STATE,cb),lambda i,j:(0,j)),pl.BlockSpec((1,cb),lambda i,j:(0,j)),st,st,pl.BlockSpec((1,T*STATE,cb),lambda i,j:(i,0,j))],
        out_specs=[row,row,pl.BlockSpec((1,8,cb),lambda i,j:(i,0,j)),st,lo],
        out_shape=[jax.ShapeDtypeStruct((S,T,C),BF),jax.ShapeDtypeStruct((S,T,C),F32),jax.ShapeDtypeStruct((S,8,C),F32),jax.ShapeDtypeStruct((S,STATE,C),F32),jax.ShapeDtypeStruct((S,T,U*STATE),F32)],
        scratch_shapes=[pltpu.VMEM((U*STATE,cb),BF)]*4,
        compiler_params=pltpu.CompilerParams(vmem_limit_bytes=VM),
        cost_estimate=pl.CostEstimate(flops=COST*S*T*C,bytes_accessed=COST*S*T*C,transcendentals=0),
        name="scan_bwd",
    )(s,x,g,bt,l,one,r,k,h0,m0,h)


def gelu_and_slope(x):
    root = math.sqrt(2.0 / math.pi)
    square = x * x
    t = jnp.tanh(x * (root + (root * 0.044715) * square))
    half = 0.5 + 0.5 * t
    slope = half + (0.5 * x) * (1.0 - t * t) * (root + (3.0 * root * 0.044715) * square)
    return x * half, slope


def expert_kernel(pieces, tile, second_at, x_ref, f_ref, w_ref, *refs):
    back_ref, value_ref, grad_ref, first_s, second_s, out_s, gin_s, sems = refs[-8:]
    j = pl.program_id(0)
    rows, width = out_s.shape
    hidden = first_s.shape[2]
    copies = [
        pltpu.make_async_copy(f_ref.at[q, pl.ds(0, width), :], first_s.at[q], sems.at[q])
        for q in range(pieces)
    ] + [
        pltpu.make_async_copy(
            w_ref.at[q, pl.ds(second_at, hidden), :], second_s.at[q], sems.at[pieces + q]
        )
        for q in range(pieces)
    ]

    @pl.when(j == 0)
    def _():
        for q in range(pieces):
            copies[q].start()
            copies[q + pieces].start()

    for q in range(pieces):
        @pl.when(j == q)
        def _():
            copies[q].wait()
            copies[q + pieces].wait()

    def mm(a, b, dims):
        return lax.dot_general(a, b, (dims, ((), ())), preferred_element_type=F32)

    first = first_s[j]
    second = second_s[j]
    for i in range(rows // tile):
        at = slice(i * tile, (i + 1) * tile)
        hidden = mm(x_ref[at, :width], first, ((1,), (0,)))
        grad = mm(x_ref[at, width:], second, ((1,), (1,)))
        value, slope = gelu_and_slope(hidden)
        value = value.astype(BF)
        grad = (grad * slope).astype(BF)
        value_ref[at, :] = value
        grad_ref[at, :] = grad
        out = mm(value, second, ((1,), (0,)))
        gin = mm(grad, first, ((1,), (1,)))

        @pl.when(j == 0)
        def _():
            out_s[at, :] = out
            gin_s[at, :] = gin

        @pl.when(j > 0)
        def _():
            out_s[at, :] += out
            gin_s[at, :] += gin

    @pl.when(j == pieces - 1)
    def _():
        back_ref[:, :width] = out_s[...].astype(BF)
        back_ref[:, width:] = gin_s[...].astype(BF)


def expert_call(x, firsts, seconds, second_at, part, groups, shared):
    rows, width = x.shape[0], x.shape[1] // 2
    pieces, _, quarter = firsts.shape
    tile = math.gcd(rows, 320)
    wide = pl.BlockSpec((rows, quarter), lambda j: (part, j))
    anywhere = pl.BlockSpec(memory_space=pl.ANY)
    whole = pl.BlockSpec((rows, 2 * width), lambda j: (0, 0))
    big = jax.ShapeDtypeStruct((groups * rows, pieces * quarter), BF)
    count = 3
    return pl.pallas_call(
        functools.partial(expert_kernel, pieces, tile, second_at),
        grid=(pieces,),
        in_specs=[whole] + [anywhere] * (2 + len(shared)),
        out_specs=[whole, wide, wide],
        out_shape=[jax.ShapeDtypeStruct((rows, 2 * width), BF), big, big],
        scratch_shapes=[
            pltpu.VMEM((pieces, width, quarter), BF),
            pltpu.VMEM((pieces, quarter, width), BF),
            pltpu.VMEM((rows, width), F32),
            pltpu.VMEM((rows, width), F32),
            pltpu.SemaphoreType.DMA((2 * pieces,)),
        ],
        input_output_aliases={count: 1, count + 1: 2} if shared else {},
        compiler_params=pltpu.CompilerParams(vmem_limit_bytes=EXPERT_VM),
        cost_estimate=pl.CostEstimate(
            flops=COST * rows * width, bytes_accessed=COST * rows * width, transcendentals=0
        ),
        name="expert",
    )(x, firsts, seconds, *shared)


def own_rows(span):
    return jnp.arange(span)[:, None] % U == jnp.arange(U * STATE)[None] // STATE


def state_picker():
    return (jnp.arange(STATE)[:, None] == jnp.arange(U * STATE)[None] % STATE).astype(BF)


def fold(z):
    z = jnp.where(own_rows(z.shape[1]), z, 0).astype(BF)
    return nt(z, state_picker())


def spread_rows(m):
    wide = nn(m.astype(BF), state_picker())
    return jnp.where(own_rows(m.shape[1]), wide, 0).astype(BF)


def bits_of(axis):
    return lax.axis_size(axis).bit_length() - 1


def my_bit(axis, k):
    return (lax.axis_index(axis) >> k) & 1


def swap(x, axis, k):
    count = lax.axis_size(axis)
    return lax.ppermute(x, axis, [(i, i ^ (1 << k)) for i in range(count)])


def shift(x, axis, distance):
    count = lax.axis_size(axis)
    return lax.ppermute(
        x, axis, [(i, i + distance) for i in range(count) if 0 <= i + distance < count]
    )


def joined_pair(x, other, axis, k, place):
    high = my_bit(axis, k) == 1
    return jnp.where(
        high,
        jnp.concatenate([other, x], axis=place),
        jnp.concatenate([x, other], axis=place),
    )


def from_batch(x):
    copies = jnp.broadcast_to(x[None], (lax.axis_size("batch"),) + x.shape)
    return lax.all_to_all(copies, "batch", split_axis=0, concat_axis=0, tiled=True)


def over_seq(x):
    bits = bits_of("seq")
    out = x.reshape(x.shape[:1] + (1,) * bits + x.shape[1:])
    for k in reversed(range(bits)):
        out = joined_pair(out, swap(out, "seq", k), "seq", k, bits - k)
    return out.reshape((-1,) + x.shape[2:])


def over_batch(x):
    got = lax.all_to_all(x.astype(BF), "batch", split_axis=0, concat_axis=0, tiled=True)
    return jnp.sum(got.astype(F32), axis=0)


def halved(x, k, place):
    bit = my_bit("seq", k)
    mine = lax.dynamic_index_in_dim(x, bit, place, True)
    theirs = lax.dynamic_index_in_dim(x, 1 - bit, place, True).astype(BF)
    return mine + swap(theirs, "seq", k).astype(F32)


def sum_over_seq(x):
    bits = bits_of("seq")
    rows = x.shape[0] // (lax.axis_size("batch") << bits)
    out = x.reshape((lax.axis_size("batch"),) + (2,) * bits + (rows,) + x.shape[1:])
    for k in range(bits):
        out = halved(out, k, bits - k)
    return out.reshape((lax.axis_size("batch"), rows) + x.shape[1:])


def totals_of(total):
    levels = []
    for k in range(bits_of("seq")):
        other = swap(total, "seq", k)
        levels.append((total, other))
        total = total + other
    return levels


def prefix(levels, state, rate, backward):
    before = jnp.zeros_like(state)
    before_total = jnp.zeros_like(levels[0][0])
    for k, (total, other_total) in enumerate(levels):
        other = swap(state.astype(BF), "seq", k).astype(F32)
        first = my_bit("seq", k) == (0 if backward else 1)
        before = jnp.where(
            first, before + jnp.exp2(before_total[:, None, :] * rate) * other, before
        )
        before_total = jnp.where(first, before_total + other_total, before_total)
        if k + 1 < len(levels):
            near = jnp.where(first, state, other)
            far = jnp.where(first, other, state)
            near_total = jnp.where(first, total, other_total)
            state = near + jnp.exp2(near_total[:, None, :] * rate) * far
    return before


def after(value, event):
    return lax.optimization_barrier((value, event))[0]


def mm(left, right, dims):
    return lax.dot_general(left, right, (dims, ((), ())), preferred_element_type=F32)


def nn(left, right):
    return mm(left, right, ((left.ndim - 1,), (0,)))


def nt(left, right):
    return mm(left, right, ((left.ndim - 1,), (1,)))


def tn(left, right):
    lead = tuple(range(left.ndim - 1))
    return mm(left, right, (lead, lead))


def silu_slope(v):
    s = jax.nn.sigmoid(v)
    return s * (1.0 + v * (1.0 - s))


def norm_back(grad_norm, x, scale):
    return scale * grad_norm - x * scale**3 * jnp.mean(grad_norm * x, axis=-1, keepdims=True)


def gelu_tanh(v):
    return jax.nn.gelu(v, approximate=True)


def rms(x):
    return lax.rsqrt(jnp.mean(x * x, axis=-1, keepdims=True) + EPSILON)


def side_by_side(x, rows):
    x = x.reshape(-1, 2, rows, x.shape[1])
    return jnp.swapaxes(x, 1, 2).reshape(-1, 2 * x.shape[3])


def one_below(x, rows):
    x = x.reshape(-1, rows, 2, x.shape[1] // 2)
    return jnp.swapaxes(x, 1, 2).reshape(-1, x.shape[3])


def pad_cols(x, width):
    return jnp.pad(x, ((0, 0), (0, width - x.shape[1])))


def shards(
    tokens,
    cotangent,
    lengths,
    order,
    expert_route,
    slot_index,
    norm_gain,
    in_proj,
    conv_weight,
    conv_bias,
    x_proj,
    dt_proj,
    dt_bias,
    a_log,
    skip_gain,
    out_proj,
    moe_gain,
    router,
    expert_in,
    expert_out,
):
    seqs, span, width = tokens.shape
    batch = lax.axis_size("batch")
    experts = expert_in.shape[0] * batch
    capacity = max(2, (5 * SEQ_MB * span + 4 * experts - 1) // (4 * experts))
    maps = DT_RANK + 2 * STATE
    lo = HALO - (CONV - 1)
    groups = 2
    size = seqs // groups

    rows = in_proj.shape[0]
    chan = jnp.concatenate(
        [
            x_proj,
            dt_proj,
            a_log,
            conv_weight,
            conv_bias[:, None],
            dt_bias[:, None],
            skip_gain[:, None],
        ],
        axis=1,
    )
    feat = jnp.concatenate([norm_gain[:, None], moe_gain[:, None], router], axis=1)
    cut = 1024
    first_set = from_batch(in_proj[:, :cut])
    later = jnp.concatenate([in_proj[:, DI:], side_by_side(out_proj, rows)], axis=1)
    later = after(later, first_set)
    later = lax.all_gather(later, ("batch", "seq"), axis=0, tiled=True)
    w_gate_in = later[:, :DI]
    w_back = one_below(later[:, DI:], rows)
    if expert_in.shape[2] == width:
        both = jnp.concatenate([expert_in[0], expert_out[0]], axis=0)
        both = lax.all_gather(after(both, later), "seq", axis=0, tiled=False)
        expert_weights = both, both, width
    else:
        own = after((expert_in[0], expert_out[0]), later)
        expert_weights = *(lax.all_gather(x, "seq", axis=0, tiled=False) for x in own), 0
    first_set = over_seq(first_set)
    second_set = over_seq(
        from_batch(
            jnp.concatenate(
                [in_proj[:, cut:DI], pad_cols(chan, 256).reshape(rows, 512), pad_cols(feat, 128)],
                axis=1,
            )
        )
    )
    w_conv_in = jnp.concatenate([first_set, second_set[:, : DI - cut]], axis=1)
    chan = second_set[:, DI - cut : DI - cut + 512].reshape(-1, 256)
    feat = second_set[:, DI - cut + 512 :]
    gain_one = feat[:, 0].astype(F32)
    gain_two = feat[:, 1].astype(F32)
    router_weight = feat[:, 2 : 2 + experts]
    w_proj = chan[:, :maps]
    at = maps + DT_RANK
    w_step = chan[:, maps:at]
    rate = -jnp.exp(chan[:, at : at + STATE].astype(F32)).T * LOG2E
    at = at + STATE
    taps = chan[:, at : at + CONV].astype(F32).T
    bias_conv = chan[:, at + CONV].astype(F32)
    bias_step = chan[:, at + CONV + 1].astype(F32)
    skip = chan[:, at + CONV + 2].astype(F32)

    halo_all = shift(tokens[:, span - HALO :, :], "seq", 1)
    tail = jnp.arange(HALO)[:, None] >= lo
    halo_all = jnp.where(tail, halo_all, 0)


    positions = lax.axis_index("seq") * span + jnp.arange(span, dtype=jnp.int32)
    row_length = jnp.sum(
        jnp.where(
            order[:, None] == jnp.arange(lengths.shape[0], dtype=jnp.int32)[None, :],
            lengths[None, :],
            0,
        ),
        axis=1,
    )
    keep_all = (positions[None, :] < row_length[:, None]).astype(F32)
    ones = (jnp.arange(U)[:, None] == jnp.arange(U * STATE)[None] // STATE).astype(BF)
    slots = jnp.arange(experts * capacity, dtype=jnp.int32)
    expert_ids = jnp.arange(experts, dtype=jnp.int32)

    class Part:
        pass

    def forward(m, event, second_event):
        p = Part()
        here = slice(m * size, (m + 1) * size)
        own = tokens[here]
        if event is not None:
            own = after(own, event)
        p.block = own.astype(F32)
        p.scale_one = rms(p.block)
        ext = jnp.concatenate([halo_all[here], own], axis=1).astype(F32)
        normed_ext = (ext * rms(ext) * gain_one).astype(BF)
        p.normed = normed_ext[:, HALO:]
        p.conv_ext = nn(normed_ext, w_conv_in)
        p.conv_out = bias_conv + sum(
            p.conv_ext[:, lo + k : lo + k + span, :] * taps[k] for k in range(CONV)
        )
        p.act = jax.nn.silu(p.conv_out).astype(BF)
        projected = nn(p.act, w_proj)
        p.delta = projected[..., :DT_RANK].astype(BF)
        input_map = projected[..., DT_RANK : DT_RANK + STATE]
        output_map = projected[..., DT_RANK + STATE :]
        p.step_arg = nt(p.delta, w_step) + bias_step
        p.step = jax.nn.softplus(p.step_arg)
        p.levels = totals_of(jnp.sum(p.step, axis=1))
        p.both = jnp.swapaxes(
            projected[..., DT_RANK:].reshape(size, span // U, U, 2 * STATE), 2, 3
        )
        p.in_rows = spread_rows(input_map)
        out_rows = spread_rows(output_map)
        end = scan_end_f(p.step, p.act, p.both, rate)
        p.init = prefix(p.levels, end, rate, False)
        if second_event is not None:
            p.init = after(p.init, second_event)
        p.gate_in = nn(p.normed, w_gate_in)
        y, p.states = scan_fwd(p.step, p.act, p.both, out_rows, rate, p.init)
        p.actf = p.act.astype(F32)
        p.mix = y + skip * p.actf
        p.gate_act = jax.nn.silu(p.gate_in)
        p.gated = (p.mix * p.gate_act).astype(BF)
        p.mixed = p.block + nn(p.gated, w_back)
        p.scale_two = rms(p.mixed)
        p.routed = (p.mixed * p.scale_two * gain_two).astype(BF)
        p.probs = jax.nn.softmax(nn(p.routed, router_weight), axis=-1)
        route = expert_route[here]
        slot = slot_index[here]
        kept = slot >= 0
        target = jnp.where(kept, route * capacity + slot, -1)
        p.selector = (target[..., None] == slots).astype(BF)
        p.chosen = jnp.logical_and(route[..., None] == expert_ids, kept[..., None])
        p.gate = jnp.sum(jnp.where(p.chosen, p.probs, 0.0), axis=-1)[..., None]
        p.grad_out = cotangent[here].astype(F32) * keep_all[here][..., None]
        grad_value = (p.gate * p.grad_out).astype(BF)
        packed = jnp.concatenate([p.routed, grad_value], axis=-1)
        send = jnp.einsum("stc,std->scd", p.selector, packed, preferred_element_type=F32)
        send = jnp.swapaxes(send.astype(BF).reshape(size, batch, capacity, 2 * width), 0, 1)
        p.send = send
        p.arrived = lax.all_to_all(send, "batch", split_axis=0, concat_axis=0, tiled=True)
        return p

    def expert(m, shared):
        p = parts[m]
        arrived = after(p.arrived, parts[m - 1].back) if m else p.arrived
        p.rows_in = arrived.reshape(batch * size * capacity, 2 * width)
        p.back, *shared = expert_call(p.rows_in, *expert_weights, m, groups, shared)
        back = p.back.reshape(batch, size, capacity, 2 * width)
        if m:
            back = after(back, parts[m - 1].returned)
        back = lax.all_to_all(back, "batch", split_axis=0, concat_axis=0, tiled=True)
        p.returned = jnp.swapaxes(back, 0, 1).reshape(size, experts * capacity, 2 * width)
        return shared

    def backward_router(p):
        picked = jnp.einsum("stc,scd->std", p.selector, p.returned, preferred_element_type=F32)
        expert_tok = picked[..., :width]
        p.activations = (p.mixed + p.gate * expert_tok).astype(BF)
        grad_gate = jnp.sum(expert_tok * p.grad_out, axis=-1, keepdims=True)
        grad_prob = jnp.where(p.chosen, grad_gate, 0.0)
        grad_logits = (
            p.probs * (grad_prob - jnp.sum(p.probs * grad_prob, axis=-1, keepdims=True))
        ).astype(BF)
        p.g_router = tn(p.routed, grad_logits)
        grad_routed = picked[..., width:] + nt(grad_logits, router_weight)
        p.g_gain_two = jnp.sum(grad_routed * p.mixed * p.scale_two, axis=(0, 1))
        p.grad_mixed = p.grad_out + norm_back(grad_routed * gain_two, p.mixed, p.scale_two)
        p.grad_branch = p.grad_mixed.astype(BF)
        grad_gated = nt(p.grad_branch, w_back)
        p.grad_mix = grad_gated * p.gate_act
        p.grad_gate_in = (grad_gated * p.mix * silu_slope(p.gate_in)).astype(BF)
        p.behind, p.grad_out_map = scan_end_b(p.step, p.grad_mix, p.both, rate, p.states)
        p.after = prefix(p.levels, p.behind, rate, True)
        p.g_skip = jnp.sum(p.grad_mix * p.actf, axis=(0, 1))

    def backward_mixer(p):
        grad_pre, base, bias, g_log, grad_in_map = scan_bwd(
            p.step,
            p.act,
            p.grad_mix,
            p.both,
            p.in_rows,
            ones,
            rate,
            skip[None],
            p.init,
            p.after,
            p.states,
        )
        p.g_log = jnp.sum(g_log, axis=0).T * LN2
        p.g_step_bias = jnp.sum(bias, axis=(0, 1))
        p.g_step = tn(grad_pre, p.delta)
        grad_proj = jnp.concatenate(
            [nn(grad_pre, w_step), fold(grad_in_map), fold(p.grad_out_map)], axis=-1
        ).astype(BF)
        p.g_proj = tn(p.act, grad_proj)
        grad_act = base + nt(grad_proj, w_proj)
        grad_conv = grad_act * silu_slope(p.conv_out)
        p.grad_conv = grad_conv
        rim = shift(grad_conv[:, :HALO, :], "seq", -1)
        longer = lax.optimization_barrier(jnp.concatenate([grad_conv, rim], axis=1))
        p.grad_conv_in = sum(
            longer[:, CONV - 1 - k : CONV - 1 - k + span, :] * taps[k] for k in range(CONV)
        ).astype(BF)

    def backward_taps(p, event):
        grad_conv = after(p.grad_conv, event)
        p.g_conv_bias = jnp.sum(grad_conv, axis=(0, 1))
        p.g_taps = jnp.stack(
            [
                jnp.sum(grad_conv * p.conv_ext[:, lo + k : lo + k + span, :], axis=(0, 1))
                for k in range(CONV)
            ],
            axis=-1,
        )

    def backward_input(p):
        grad_normed = nt(p.grad_conv_in, w_conv_in) + nt(p.grad_gate_in, w_gate_in)
        p.input_grad = p.grad_mixed + norm_back(grad_normed * gain_one, p.block, p.scale_one)

    parts = []
    parts.append(forward(0, None, None))
    for m in range(1, groups):
        parts.append(forward(m, parts[-1].send, parts[-1].arrived))
    shared = ()
    for m in range(groups):
        shared = expert(m, shared)
    values, grad_hidden = shared

    def joined(name):
        return jnp.concatenate([getattr(p, name) for p in parts], axis=0)

    def added(name):
        return functools.reduce(jnp.add, [getattr(p, name) for p in parts])

    def added_products(left, right):
        return functools.reduce(
            jnp.add, [tn(getattr(p, left), getattr(p, right)) for p in parts]
        )

    rows_in = joined("rows_in")
    rows_in, values, grad_hidden = after((rows_in, values, grad_hidden), parts[-1].back)
    grad_second = tn(values, rows_in[:, width:]).astype(BF)
    grad_first = tn(grad_hidden, rows_in[:, :width]).astype(BF)
    products = grad_first, grad_second
    parts[0].returned = after(parts[0].returned, products)
    backward_router(parts[0])
    grad_first, grad_second = after(products, parts[0].grad_mix)
    grad_second = lax.psum_scatter(grad_second, "seq", scatter_dimension=0, tiled=True)
    grad_first = lax.psum_scatter(grad_first, "seq", scatter_dimension=0, tiled=True)
    for p, earlier in zip(parts[1:], parts):
        p.returned = after(p.returned, earlier.grad_mix)
        backward_router(p)
    g_feat = jnp.concatenate([added("g_gain_two")[:, None], added("g_router")], axis=1)
    background = jnp.concatenate(
        [
            added_products("normed", "grad_gate_in").astype(BF),
            side_by_side(added_products("gated", "grad_branch").astype(BF), rows),
            pad_cols(g_feat, 128).astype(BF),
        ],
        axis=1,
    )
    background = lax.psum_scatter(background, ("batch", "seq"), scatter_dimension=0, tiled=True)
    background = background.astype(F32)
    g_gate_half = background[:, :DI]
    g_back = one_below(background[:, DI : 2 * DI], rows)
    g_feat = background[:, 2 * DI :]
    for p in parts:
        backward_mixer(p)
    g_conv_half = added_products("normed", "grad_conv_in")
    for p in parts:
        backward_taps(p, g_conv_half)
    g_chan = jnp.concatenate(
        [
            added("g_proj"),
            added("g_step"),
            added("g_log"),
            added("g_taps"),
            added("g_conv_bias")[:, None],
            added("g_step_bias")[:, None],
            added("g_skip")[:, None],
        ],
        axis=1,
    )
    g_chan = pad_cols(g_chan, 256).reshape(-1, 512)
    g_rest = jnp.concatenate([sum_over_seq(g_conv_half), sum_over_seq(g_chan)], axis=2)
    for p in parts:
        p.grad_conv_in = after(p.grad_conv_in, (g_conv_half, background))
        backward_input(p)
    grad_first, grad_second = after((grad_first, grad_second), g_conv_half)
    grad_first = grad_first.astype(F32).T
    grad_second = grad_second.astype(F32)
    g_rest = after(g_rest, (parts[0].input_grad, grad_first, grad_second))
    g_rest = over_batch(g_rest)
    g_rest = after(g_rest, parts[-1].input_grad)
    g_conv_half = g_rest[:, :DI]
    g_chan = g_rest[:, DI:].reshape(-1, 256)
    g_in = jnp.concatenate([g_conv_half, g_gate_half], axis=1)
    g_gain_one = jnp.sum(g_in * in_proj.astype(F32), axis=1) / norm_gain.astype(F32)
    at = maps + DT_RANK
    return (
        joined("activations"),
        joined("input_grad"),
        g_gain_one,
        g_in,
        g_chan[:, at + STATE : at + STATE + CONV],
        g_chan[:, at + STATE + CONV],
        g_chan[:, :maps],
        g_chan[:, maps:at],
        g_chan[:, at + STATE + CONV + 1],
        g_chan[:, at : at + STATE],
        g_chan[:, at + STATE + CONV + 2],
        g_back,
        g_feat[:, 0],
        g_feat[:, 1 : 1 + experts],
        grad_first[None],
        grad_second[None],
    )


def solution(mesh):
    return jax.shard_map(
        shards,
        mesh=mesh,
        in_specs=(
            P("batch", "seq", None),
            P("batch", "seq", None),
            P(),
            P("batch"),
            P("batch", "seq"),
            P("batch", "seq"),
            P(("batch", "seq")),
            P(("batch", "seq"), None),
            P(("batch", "seq"), None),
            P(("batch", "seq")),
            P(("batch", "seq"), None),
            P(("batch", "seq"), None),
            P(("batch", "seq")),
            P(("batch", "seq"), None),
            P(("batch", "seq")),
            P(("batch", "seq"), None),
            P(("batch", "seq")),
            P(("batch", "seq"), None),
            P("batch", None, "seq"),
            P("batch", "seq", None),
        ),
        out_specs=(
            P("batch", "seq", None),
            P("batch", "seq", None),
            P(("batch", "seq")),
            P(("batch", "seq"), None),
            P(("batch", "seq"), None),
            P(("batch", "seq")),
            P(("batch", "seq"), None),
            P(("batch", "seq"), None),
            P(("batch", "seq")),
            P(("batch", "seq"), None),
            P(("batch", "seq")),
            P(("batch", "seq"), None),
            P(("batch", "seq")),
            P(("batch", "seq"), None),
            P("batch", None, "seq"),
            P("batch", "seq", None),
        ),
        check_vma=False,
    )
```

```python
import functools
import math

import jax
import jax.numpy as jnp
from jax import lax
from jax.experimental import pallas as pl
from jax.experimental.pallas import tpu as pltpu
from jax.sharding import PartitionSpec as P

DI = 1536
STATE = 16
DT_RANK = 48
CONV = 4
SEQ_MB = 1
EPSILON = 1e-05
F32 = jnp.float32
BF = jnp.bfloat16
U = 16
CB = 512
CE = 768
VM = 48 << 20
EXPERT_VM = 48 << 20
COST = 1
LOG2E = 1.0 / math.log(2.0)
LN2 = math.log(2.0)
HALO = 8


def end_f_kernel(chunks, s_ref, x_ref, bt_ref, r_ref, h_ref):
    r = r_ref[...]
    width = r.shape[1]
    def chunk(c, h):
        rows = pl.ds(pl.multiple_of(c*U,U),U)
        s8 = s_ref[0, rows, :]
        d8 = x_ref[0, rows, :].astype(F32)*s8
        bt = bt_ref[0, c]
        for k in range(U):
            s = jnp.broadcast_to(s8[k:k+1], (STATE,width))
            d = jnp.broadcast_to(d8[k:k+1], (STATE,width))
            b = jnp.broadcast_to(bt[0:STATE, k:k+1], (STATE,width))
            h = jnp.exp2(s*r)*h + d*b
        return h
    h_ref[0] = lax.fori_loop(0, chunks, chunk, jnp.zeros((STATE,width),F32))


def scan_end_f(s, x, bt, r):
    S,T,C = s.shape
    cb=min(CE,C)
    row=pl.BlockSpec((1,T,cb), lambda i,j:(i,0,j))
    return pl.pallas_call(functools.partial(end_f_kernel, T//U),
        grid=(S,C//cb),
        in_specs=[row,row,pl.BlockSpec((1,T//U,2*STATE,U),lambda i,j:(i,0,0,0)),pl.BlockSpec((STATE,cb),lambda i,j:(0,j))],
        out_specs=pl.BlockSpec((1,STATE,cb),lambda i,j:(i,0,j)),
        out_shape=jax.ShapeDtypeStruct((S,STATE,C),F32),
        compiler_params=pltpu.CompilerParams(vmem_limit_bytes=VM),
        cost_estimate=pl.CostEstimate(flops=COST*S*T*C,bytes_accessed=COST*S*T*C,transcendentals=0),
        name="scan_end_f",
    )(s,x,bt,r)


def end_b_kernel(chunks, s_ref, g_ref, bt_ref, r_ref, h_ref, out_ref, go_ref):
    r = r_ref[...]
    width = r.shape[1]
    @pl.when(pl.program_id(1)==0)
    def _():
        go_ref[...]=jnp.zeros_like(go_ref)
    def chunk(c, h):
        c = chunks-1-c
        rows = pl.ds(pl.multiple_of(c*U,U),U)
        s8 = s_ref[0, rows, :]
        g8 = g_ref[0, rows, :]
        bt = bt_ref[0, c]
        go_ref[0, rows, :] += lax.dot_general(g8.astype(BF), h_ref[0, pl.ds(pl.multiple_of(c*U*STATE,U*STATE),U*STATE), :], (((1,),(1,)),((),())), preferred_element_type=F32)
        for k in range(U-1,-1,-1):
            s = jnp.broadcast_to(s8[k:k+1], (STATE,width))
            g = jnp.broadcast_to(g8[k:k+1], (STATE,width))
            cc = jnp.broadcast_to(bt[STATE:2*STATE, k:k+1], (STATE,width))
            h = jnp.exp2(s*r)*(h + g*cc)
        return h
    out_ref[0] = lax.fori_loop(0, chunks, chunk, jnp.zeros((STATE,width),F32))


def scan_end_b(s, g, bt, r, h):
    S,T,C = s.shape
    cb=min(CE,C)
    row=pl.BlockSpec((1,T,cb), lambda i,j:(i,0,j))
    return pl.pallas_call(functools.partial(end_b_kernel, T//U),
        grid=(S,C//cb),
        in_specs=[row,row,pl.BlockSpec((1,T//U,2*STATE,U),lambda i,j:(i,0,0,0)),pl.BlockSpec((STATE,cb),lambda i,j:(0,j)),pl.BlockSpec((1,T*STATE,cb),lambda i,j:(i,0,j))],
        out_specs=[pl.BlockSpec((1,STATE,cb),lambda i,j:(i,0,j)),pl.BlockSpec((1,T,U*STATE),lambda i,j:(i,0,0))],
        out_shape=[jax.ShapeDtypeStruct((S,STATE,C),F32),jax.ShapeDtypeStruct((S,T,U*STATE),F32)],
        compiler_params=pltpu.CompilerParams(vmem_limit_bytes=VM),
        cost_estimate=pl.CostEstimate(flops=COST*S*T*C,bytes_accessed=COST*S*T*C,transcendentals=0),
        name="scan_end_b",
    )(s,g,bt,r,h)


def fwd_kernel(chunks, s_ref, x_ref, bt_ref, l_ref, r_ref, h0_ref, y_ref, h_ref, even, odd):
    r = r_ref[...]
    width = r.shape[1]
    def rows_at(c, size):
        return pl.ds(pl.multiple_of(c*size,size),size)
    def chunk(c, h, mine, other):
        before = jnp.maximum(c-1,0)
        y_ref[0, rows_at(before,U), :] = jnp.dot(l_ref[0, rows_at(before,U), :], other[...], preferred_element_type=F32)
        rows = rows_at(c,U)
        s8 = s_ref[0, rows, :]
        d8 = x_ref[0, rows, :].astype(F32)*s8
        bt = bt_ref[0, c]
        for k in range(U):
            s = jnp.broadcast_to(s8[k:k+1], (STATE,width))
            d = jnp.broadcast_to(d8[k:k+1], (STATE,width))
            b = jnp.broadcast_to(bt[0:STATE, k:k+1], (STATE,width))
            h = jnp.exp2(s*r)*h + d*b
            low = h.astype(BF)
            mine[k*STATE:(k+1)*STATE, :] = low
            h_ref[0, pl.ds(pl.multiple_of(c*U*STATE+k*STATE,STATE),STATE), :] = low
        return h
    def pair(i, h):
        h = chunk(2*i, h, even, odd)
        return chunk(2*i+1, h, odd, even)
    odd[...] = jnp.zeros_like(odd)
    lax.fori_loop(0, chunks//2, pair, h0_ref[0])
    last = pl.ds((chunks-1)*U,U)
    y_ref[0, last, :] = jnp.dot(l_ref[0, last, :], odd[...], preferred_element_type=F32)

def scan_fwd(s, x, bt, l, r, h0):
    S,T,C = s.shape
    cb=min(CB,C)
    row=pl.BlockSpec((1,T,cb), lambda i,j:(i,0,j))
    st=pl.BlockSpec((1,STATE,cb),lambda i,j:(i,0,j))
    return pl.pallas_call(functools.partial(fwd_kernel, T//U),
        grid=(S,C//cb),
        in_specs=[row,row,pl.BlockSpec((1,T//U,2*STATE,U),lambda i,j:(i,0,0,0)),pl.BlockSpec((1,T,U*STATE),lambda i,j:(i,0,0)),pl.BlockSpec((STATE,cb),lambda i,j:(0,j)),st],
        out_specs=[row,pl.BlockSpec((1,T*STATE,cb),lambda i,j:(i,0,j))],
        out_shape=[jax.ShapeDtypeStruct((S,T,C),F32),jax.ShapeDtypeStruct((S,T*STATE,C),BF)],
        scratch_shapes=[pltpu.VMEM((U*STATE,cb),BF)]*2,
        compiler_params=pltpu.CompilerParams(vmem_limit_bytes=VM),
        cost_estimate=pl.CostEstimate(flops=COST*S*T*C,bytes_accessed=COST*S*T*C,transcendentals=0),
        name="scan_fwd",
    )(s,x,bt,l,r,h0)


def bwd_kernel(chunks, s_ref, x_ref, g_ref, bt_ref, l_ref, one_ref, r_ref, k_ref, h0_ref, m0_ref, h_ref,
               pre_ref, base_ref, bias_ref, alog_ref, gi_ref, lam_e, fr_e, lam_o, fr_o):
    r = r_ref[...]
    width = r.shape[1]
    j = pl.program_id(1)
    nt=(((1,),(1,)),((),()))
    def rows_at(c, size):
        return pl.ds(pl.multiple_of(c*size,size),size)
    @pl.when(j==0)
    def _():
        gi_ref[...]=jnp.zeros_like(gi_ref)
    bias_ref[...] = jnp.zeros_like(bias_ref)
    lam_o[...] = jnp.zeros_like(lam_o)
    fr_o[...] = jnp.zeros_like(fr_o)
    def sums(c, lam_s, fr_s, first=None):
        rows = rows_at(c,U)
        s8 = s_ref[0, rows, :]
        x8 = x_ref[0, rows, :].astype(F32)
        d8 = (x8*s8).astype(BF)
        lam_all = lam_s[...]
        pull = jnp.dot(l_ref[0, rows, :], lam_all, preferred_element_type=F32)
        gs = jnp.dot(one_ref[...], fr_s[...], preferred_element_type=F32)
        slope = jnp.where(s8 < 0.03, s8*(1.0-s8*(0.5-s8*(1.0/6.0))), 1.0-jnp.exp(-s8))
        arg = (gs*LN2 + x8*pull)*slope
        pre_ref[0, rows, :] = arg.astype(BF)
        base_ref[0, rows, :] = k_ref[...]*g_ref[0, rows, :] + s8*pull
        part = arg[:8]+arg[8:]
        gi = lax.dot_general(d8, lam_all, nt, preferred_element_type=F32)
        if first is not None:
            gi = jnp.where(first, 0.0, gi)
            part = jnp.where(first, 0.0, part)
        gi_ref[0, rows, :] += gi
        bias_ref[0] += part
    def chunk(c, carry, mine, other, first=None):
        lam_c, alog = carry
        sums(jnp.minimum(c+1,chunks-1), *other, first)
        lam_s, fr_s = mine
        rows = rows_at(c,U)
        s8 = s_ref[0, rows, :]
        g8 = g_ref[0, rows, :]
        bt = bt_ref[0, c]
        for k in range(U-1,-1,-1):
            s = jnp.broadcast_to(s8[k:k+1], (STATE,width))
            g = jnp.broadcast_to(g8[k:k+1], (STATE,width))
            cc = jnp.broadcast_to(bt[STATE:2*STATE, k:k+1], (STATE,width))
            if k:
                hp = h_ref[0, pl.ds(pl.multiple_of(c*U*STATE+(k-1)*STATE,STATE),STATE), :].astype(F32)
            else:
                hp = h_ref[0, pl.ds(pl.multiple_of(jnp.maximum(c*U*STATE-STATE,0),STATE),STATE), :].astype(F32)
                hp = jnp.where(c==0, h0_ref[0], hp)
            lam = lam_c + g*cc
            lam_c = jnp.exp2(s*r)*lam
            fr = lam_c*hp*r
            alog = alog + fr*s
            lam_s[k*STATE:(k+1)*STATE,:] = lam.astype(BF)
            fr_s[k*STATE:(k+1)*STATE,:] = fr.astype(BF)
        return lam_c, alog
    E=(lam_e,fr_e); O=(lam_o,fr_o)
    def pair(i, carry):
        c = chunks-1-2*i
        carry = chunk(c, carry, E, O, i==0)
        return chunk(c-1, carry, O, E)
    _, alog = lax.fori_loop(0, chunks//2, pair, (m0_ref[0], jnp.zeros((STATE,width),F32)))
    sums(0, *O)
    alog_ref[0] = alog

def scan_bwd(s, x, g, bt, l, one, r, k, h0, m0, h):
    S,T,C = s.shape
    cb=min(CB,C)
    row=pl.BlockSpec((1,T,cb), lambda i,j:(i,0,j))
    st=pl.BlockSpec((1,STATE,cb),lambda i,j:(i,0,j))
    lo=pl.BlockSpec((1,T,U*STATE),lambda i,j:(i,0,0))
    return pl.pallas_call(functools.partial(bwd_kernel, T//U),
        grid=(S,C//cb),
        in_specs=[row,row,row,pl.BlockSpec((1,T//U,2*STATE,U),lambda i,j:(i,0,0,0)),lo,pl.BlockSpec((U,U*STATE),lambda i,j:(0,0)),pl.BlockSpec((STATE,cb),lambda i,j:(0,j)),pl.BlockSpec((1,cb),lambda i,j:(0,j)),st,st,pl.BlockSpec((1,T*STATE,cb),lambda i,j:(i,0,j))],
        out_specs=[row,row,pl.BlockSpec((1,8,cb),lambda i,j:(i,0,j)),st,lo],
        out_shape=[jax.ShapeDtypeStruct((S,T,C),BF),jax.ShapeDtypeStruct((S,T,C),F32),jax.ShapeDtypeStruct((S,8,C),F32),jax.ShapeDtypeStruct((S,STATE,C),F32),jax.ShapeDtypeStruct((S,T,U*STATE),F32)],
        scratch_shapes=[pltpu.VMEM((U*STATE,cb),BF)]*4,
        compiler_params=pltpu.CompilerParams(vmem_limit_bytes=VM),
        cost_estimate=pl.CostEstimate(flops=COST*S*T*C,bytes_accessed=COST*S*T*C,transcendentals=0),
        name="scan_bwd",
    )(s,x,g,bt,l,one,r,k,h0,m0,h)


def gelu_and_slope(x):
    root = math.sqrt(2.0 / math.pi)
    square = x * x
    t = jnp.tanh(x * (root + (root * 0.044715) * square))
    half = 0.5 + 0.5 * t
    slope = half + (0.5 * x) * (1.0 - t * t) * (root + (3.0 * root * 0.044715) * square)
    return x * half, slope


def expert_kernel(pieces, tile, second_at, x_ref, f_ref, w_ref, *refs):
    back_ref, value_ref, grad_ref, first_s, second_s, out_s, gin_s, sems = refs[-8:]
    j = pl.program_id(0)
    rows, width = out_s.shape
    hidden = first_s.shape[2]
    copies = [
        pltpu.make_async_copy(f_ref.at[q, pl.ds(0, width), :], first_s.at[q], sems.at[q])
        for q in range(pieces)
    ] + [
        pltpu.make_async_copy(
            w_ref.at[q, pl.ds(second_at, hidden), :], second_s.at[q], sems.at[pieces + q]
        )
        for q in range(pieces)
    ]

    @pl.when(j == 0)
    def _():
        for q in range(pieces):
            copies[q].start()
            copies[q + pieces].start()

    for q in range(pieces):
        @pl.when(j == q)
        def _():
            copies[q].wait()
            copies[q + pieces].wait()

    def mm(a, b, dims):
        return lax.dot_general(a, b, (dims, ((), ())), preferred_element_type=F32)

    first = first_s[j]
    second = second_s[j]
    for i in range(rows // tile):
        at = slice(i * tile, (i + 1) * tile)
        hidden = mm(x_ref[at, :width], first, ((1,), (0,)))
        grad = mm(x_ref[at, width:], second, ((1,), (1,)))
        value, slope = gelu_and_slope(hidden)
        value = value.astype(BF)
        grad = (grad * slope).astype(BF)
        value_ref[at, :] = value
        grad_ref[at, :] = grad
        out = mm(value, second, ((1,), (0,)))
        gin = mm(grad, first, ((1,), (1,)))

        @pl.when(j == 0)
        def _():
            out_s[at, :] = out
            gin_s[at, :] = gin

        @pl.when(j > 0)
        def _():
            out_s[at, :] += out
            gin_s[at, :] += gin

    @pl.when(j == pieces - 1)
    def _():
        back_ref[:, :width] = out_s[...].astype(BF)
        back_ref[:, width:] = gin_s[...].astype(BF)


def expert_call(x, firsts, seconds, second_at, part, groups, shared):
    rows, width = x.shape[0], x.shape[1] // 2
    pieces, _, quarter = firsts.shape
    tile = math.gcd(rows, 320)
    wide = pl.BlockSpec((rows, quarter), lambda j: (part, j))
    anywhere = pl.BlockSpec(memory_space=pl.ANY)
    whole = pl.BlockSpec((rows, 2 * width), lambda j: (0, 0))
    big = jax.ShapeDtypeStruct((groups * rows, pieces * quarter), BF)
    count = 3
    return pl.pallas_call(
        functools.partial(expert_kernel, pieces, tile, second_at),
        grid=(pieces,),
        in_specs=[whole] + [anywhere] * (2 + len(shared)),
        out_specs=[whole, wide, wide],
        out_shape=[jax.ShapeDtypeStruct((rows, 2 * width), BF), big, big],
        scratch_shapes=[
            pltpu.VMEM((pieces, width, quarter), BF),
            pltpu.VMEM((pieces, quarter, width), BF),
            pltpu.VMEM((rows, width), F32),
            pltpu.VMEM((rows, width), F32),
            pltpu.SemaphoreType.DMA((2 * pieces,)),
        ],
        input_output_aliases={count: 1, count + 1: 2} if shared else {},
        compiler_params=pltpu.CompilerParams(vmem_limit_bytes=EXPERT_VM),
        cost_estimate=pl.CostEstimate(
            flops=COST * rows * width, bytes_accessed=COST * rows * width, transcendentals=0
        ),
        name="expert",
    )(x, firsts, seconds, *shared)


def own_rows(span):
    return jnp.arange(span)[:, None] % U == jnp.arange(U * STATE)[None] // STATE


def state_picker():
    return (jnp.arange(STATE)[:, None] == jnp.arange(U * STATE)[None] % STATE).astype(BF)


def fold(z):
    z = jnp.where(own_rows(z.shape[1]), z, 0).astype(BF)
    return nt(z, state_picker())


def spread_rows(m):
    wide = nn(m.astype(BF), state_picker())
    return jnp.where(own_rows(m.shape[1]), wide, 0).astype(BF)


def bits_of(axis):
    return lax.axis_size(axis).bit_length() - 1


def my_bit(axis, k):
    return (lax.axis_index(axis) >> k) & 1


def swap(x, axis, k):
    count = lax.axis_size(axis)
    return lax.ppermute(x, axis, [(i, i ^ (1 << k)) for i in range(count)])


def shift(x, axis, distance):
    count = lax.axis_size(axis)
    return lax.ppermute(
        x, axis, [(i, i + distance) for i in range(count) if 0 <= i + distance < count]
    )


def joined_pair(x, other, axis, k, place):
    high = my_bit(axis, k) == 1
    return jnp.where(
        high,
        jnp.concatenate([other, x], axis=place),
        jnp.concatenate([x, other], axis=place),
    )


def from_batch(x):
    copies = jnp.broadcast_to(x[None], (lax.axis_size("batch"),) + x.shape)
    return lax.all_to_all(copies, "batch", split_axis=0, concat_axis=0, tiled=True)


def over_seq(x):
    bits = bits_of("seq")
    out = x.reshape(x.shape[:1] + (1,) * bits + x.shape[1:])
    for k in reversed(range(bits)):
        out = joined_pair(out, swap(out, "seq", k), "seq", k, bits - k)
    return out.reshape((-1,) + x.shape[2:])


def over_batch(x):
    got = lax.all_to_all(x.astype(BF), "batch", split_axis=0, concat_axis=0, tiled=True)
    return jnp.sum(got.astype(F32), axis=0)


def halved(x, k, place):
    bit = my_bit("seq", k)
    mine = lax.dynamic_index_in_dim(x, bit, place, True)
    theirs = lax.dynamic_index_in_dim(x, 1 - bit, place, True).astype(BF)
    return mine + swap(theirs, "seq", k).astype(F32)


def sum_over_seq(x):
    bits = bits_of("seq")
    rows = x.shape[0] // (lax.axis_size("batch") << bits)
    out = x.reshape((lax.axis_size("batch"),) + (2,) * bits + (rows,) + x.shape[1:])
    for k in range(bits):
        out = halved(out, k, bits - k)
    return out.reshape((lax.axis_size("batch"), rows) + x.shape[1:])


def totals_of(total):
    levels = []
    for k in range(bits_of("seq")):
        other = swap(total, "seq", k)
        levels.append((total, other))
        total = total + other
    return levels


def prefix(levels, state, rate, backward):
    before = jnp.zeros_like(state)
    before_total = jnp.zeros_like(levels[0][0])
    for k, (total, other_total) in enumerate(levels):
        other = swap(state.astype(BF), "seq", k).astype(F32)
        first = my_bit("seq", k) == (0 if backward else 1)
        before = jnp.where(
            first, before + jnp.exp2(before_total[:, None, :] * rate) * other, before
        )
        before_total = jnp.where(first, before_total + other_total, before_total)
        if k + 1 < len(levels):
            near = jnp.where(first, state, other)
            far = jnp.where(first, other, state)
            near_total = jnp.where(first, total, other_total)
            state = near + jnp.exp2(near_total[:, None, :] * rate) * far
    return before


def after(value, event):
    return lax.optimization_barrier((value, event))[0]


def mm(left, right, dims):
    return lax.dot_general(left, right, (dims, ((), ())), preferred_element_type=F32)


def nn(left, right):
    return mm(left, right, ((left.ndim - 1,), (0,)))


def nt(left, right):
    return mm(left, right, ((left.ndim - 1,), (1,)))


def tn(left, right):
    lead = tuple(range(left.ndim - 1))
    return mm(left, right, (lead, lead))


def silu_slope(v):
    s = jax.nn.sigmoid(v)
    return s * (1.0 + v * (1.0 - s))


def norm_back(grad_norm, x, scale):
    return scale * grad_norm - x * scale**3 * jnp.mean(grad_norm * x, axis=-1, keepdims=True)


def gelu_tanh(v):
    return jax.nn.gelu(v, approximate=True)


def rms(x):
    return lax.rsqrt(jnp.mean(x * x, axis=-1, keepdims=True) + EPSILON)


def side_by_side(x, rows):
    width = x.shape[1]
    x = x.reshape(-1, 2, rows, width)
    return jnp.concatenate([x[:, h].reshape(-1, width) for h in range(2)], axis=1)


def one_below(x, rows):
    width = x.shape[1] // 2
    halves = [x[:, h * width : (h + 1) * width].reshape(-1, rows, width) for h in range(2)]
    return jnp.concatenate(halves, axis=1).reshape(-1, width)


def pad_cols(x, width):
    return jnp.pad(x, ((0, 0), (0, width - x.shape[1])))


def shards(
    tokens,
    cotangent,
    lengths,
    order,
    expert_route,
    slot_index,
    norm_gain,
    in_proj,
    conv_weight,
    conv_bias,
    x_proj,
    dt_proj,
    dt_bias,
    a_log,
    skip_gain,
    out_proj,
    moe_gain,
    router,
    expert_in,
    expert_out,
):
    seqs, span, width = tokens.shape
    batch = lax.axis_size("batch")
    experts = expert_in.shape[0] * batch
    capacity = max(2, (5 * SEQ_MB * span + 4 * experts - 1) // (4 * experts))
    maps = DT_RANK + 2 * STATE
    lo = HALO - (CONV - 1)
    groups = 2
    size = seqs // groups

    rows = in_proj.shape[0]
    chan = jnp.concatenate(
        [
            x_proj,
            dt_proj,
            a_log,
            conv_weight,
            conv_bias[:, None],
            dt_bias[:, None],
            skip_gain[:, None],
        ],
        axis=1,
    )
    feat = jnp.concatenate([norm_gain[:, None], moe_gain[:, None], router], axis=1)
    first_set = from_batch(in_proj[:, :DI])
    later = jnp.concatenate([in_proj[:, DI:], side_by_side(out_proj, rows)], axis=1)
    later = after(later, first_set)
    later = lax.all_gather(later, ("batch", "seq"), axis=0, tiled=True)
    w_gate_in = later[:, :DI]
    w_back = one_below(later[:, DI:], rows)
    if expert_in.shape[2] == width:
        both = jnp.concatenate([expert_in[0], expert_out[0]], axis=0)
        both = lax.all_gather(after(both, later), "seq", axis=0, tiled=False)
        expert_weights = both, both, width
    else:
        own = after((expert_in[0], expert_out[0]), later)
        expert_weights = *(lax.all_gather(x, "seq", axis=0, tiled=False) for x in own), 0
    first_set = over_seq(first_set)
    second_set = over_seq(
        from_batch(
            jnp.concatenate([pad_cols(chan, 256).reshape(rows, 512), pad_cols(feat, 128)], axis=1)
        )
    )
    w_conv_in = first_set
    chan = second_set[:, :512].reshape(-1, 256)
    feat = second_set[:, 512:]
    gain_one = feat[:, 0].astype(F32)
    gain_two = feat[:, 1].astype(F32)
    router_weight = feat[:, 2 : 2 + experts]
    w_proj = chan[:, :maps]
    at = maps + DT_RANK
    w_step = chan[:, maps:at]
    rate = -jnp.exp(chan[:, at : at + STATE].astype(F32)).T * LOG2E
    at = at + STATE
    taps = chan[:, at : at + CONV].astype(F32).T
    bias_conv = chan[:, at + CONV].astype(F32)
    bias_step = chan[:, at + CONV + 1].astype(F32)
    skip = chan[:, at + CONV + 2].astype(F32)

    halo_all = shift(tokens[:, span - HALO :, :], "seq", 1)
    tail = jnp.arange(HALO)[:, None] >= lo
    halo_all = jnp.where(tail, halo_all, 0)


    positions = lax.axis_index("seq") * span + jnp.arange(span, dtype=jnp.int32)
    row_length = jnp.sum(
        jnp.where(
            order[:, None] == jnp.arange(lengths.shape[0], dtype=jnp.int32)[None, :],
            lengths[None, :],
            0,
        ),
        axis=1,
    )
    keep_all = (positions[None, :] < row_length[:, None]).astype(F32)
    ones = (jnp.arange(U)[:, None] == jnp.arange(U * STATE)[None] // STATE).astype(BF)
    slots = jnp.arange(experts * capacity, dtype=jnp.int32)
    expert_ids = jnp.arange(experts, dtype=jnp.int32)

    class Part:
        pass

    def forward(m, event, second_event):
        p = Part()
        here = slice(m * size, (m + 1) * size)
        own = tokens[here]
        if event is not None:
            own = after(own, event)
        p.block = own.astype(F32)
        p.scale_one = rms(p.block)
        ext = jnp.concatenate([halo_all[here], own], axis=1).astype(F32)
        normed_ext = (ext * rms(ext) * gain_one).astype(BF)
        p.normed = normed_ext[:, HALO:]
        p.conv_ext = nn(normed_ext, w_conv_in)
        p.conv_out = bias_conv + sum(
            p.conv_ext[:, lo + k : lo + k + span, :] * taps[k] for k in range(CONV)
        )
        p.act = jax.nn.silu(p.conv_out).astype(BF)
        projected = nn(p.act, w_proj)
        p.delta = projected[..., :DT_RANK].astype(BF)
        input_map = projected[..., DT_RANK : DT_RANK + STATE]
        output_map = projected[..., DT_RANK + STATE :]
        p.step_arg = nt(p.delta, w_step) + bias_step
        p.step = jax.nn.softplus(p.step_arg)
        p.levels = totals_of(jnp.sum(p.step, axis=1))
        p.both = jnp.swapaxes(
            projected[..., DT_RANK:].reshape(size, span // U, U, 2 * STATE), 2, 3
        )
        p.in_rows = spread_rows(input_map)
        out_rows = spread_rows(output_map)
        end = scan_end_f(p.step, p.act, p.both, rate)
        p.init = prefix(p.levels, end, rate, False)
        if second_event is not None:
            p.init = after(p.init, second_event)
        p.gate_in = nn(p.normed, w_gate_in)
        y, p.states = scan_fwd(p.step, p.act, p.both, out_rows, rate, p.init)
        p.actf = p.act.astype(F32)
        p.mix = y + skip * p.actf
        p.gate_act = jax.nn.silu(p.gate_in)
        p.gated = (p.mix * p.gate_act).astype(BF)
        p.mixed = p.block + nn(p.gated, w_back)
        p.scale_two = rms(p.mixed)
        p.routed = (p.mixed * p.scale_two * gain_two).astype(BF)
        p.probs = jax.nn.softmax(nn(p.routed, router_weight), axis=-1)
        route = expert_route[here]
        slot = slot_index[here]
        kept = slot >= 0
        target = jnp.where(kept, route * capacity + slot, -1)
        p.selector = (target[..., None] == slots).astype(BF)
        p.chosen = jnp.logical_and(route[..., None] == expert_ids, kept[..., None])
        p.gate = jnp.sum(jnp.where(p.chosen, p.probs, 0.0), axis=-1)[..., None]
        p.grad_out = cotangent[here].astype(F32) * keep_all[here][..., None]
        grad_value = (p.gate * p.grad_out).astype(BF)
        packed = jnp.concatenate([p.routed, grad_value], axis=-1)
        send = jnp.einsum("stc,std->scd", p.selector, packed, preferred_element_type=F32)
        send = jnp.swapaxes(send.astype(BF).reshape(size, batch, capacity, 2 * width), 0, 1)
        p.send = send
        p.arrived = lax.all_to_all(send, "batch", split_axis=0, concat_axis=0, tiled=True)
        return p

    def expert(m, shared):
        p = parts[m]
        arrived = after(p.arrived, parts[m - 1].back) if m else p.arrived
        p.rows_in = arrived.reshape(batch * size * capacity, 2 * width)
        p.back, *shared = expert_call(p.rows_in, *expert_weights, m, groups, shared)
        back = p.back.reshape(batch, size, capacity, 2 * width)
        if m:
            back = after(back, parts[m - 1].returned)
        back = lax.all_to_all(back, "batch", split_axis=0, concat_axis=0, tiled=True)
        p.returned = jnp.swapaxes(back, 0, 1).reshape(size, experts * capacity, 2 * width)
        return shared

    def backward_router(p):
        picked = jnp.einsum("stc,scd->std", p.selector, p.returned, preferred_element_type=F32)
        expert_tok = picked[..., :width]
        p.activations = (p.mixed + p.gate * expert_tok).astype(BF)
        grad_gate = jnp.sum(expert_tok * p.grad_out, axis=-1, keepdims=True)
        grad_prob = jnp.where(p.chosen, grad_gate, 0.0)
        grad_logits = (
            p.probs * (grad_prob - jnp.sum(p.probs * grad_prob, axis=-1, keepdims=True))
        ).astype(BF)
        p.g_router = tn(p.routed, grad_logits)
        grad_routed = picked[..., width:] + nt(grad_logits, router_weight)
        p.g_gain_two = jnp.sum(grad_routed * p.mixed * p.scale_two, axis=(0, 1))
        p.grad_mixed = p.grad_out + norm_back(grad_routed * gain_two, p.mixed, p.scale_two)
        p.grad_branch = p.grad_mixed.astype(BF)
        grad_gated = nt(p.grad_branch, w_back)
        p.grad_mix = grad_gated * p.gate_act
        p.grad_gate_in = (grad_gated * p.mix * silu_slope(p.gate_in)).astype(BF)
        p.behind, p.grad_out_map = scan_end_b(p.step, p.grad_mix, p.both, rate, p.states)
        p.after = prefix(p.levels, p.behind, rate, True)
        p.g_skip = jnp.sum(p.grad_mix * p.actf, axis=(0, 1))

    def backward_mixer(p):
        grad_pre, base, bias, g_log, grad_in_map = scan_bwd(
            p.step,
            p.act,
            p.grad_mix,
            p.both,
            p.in_rows,
            ones,
            rate,
            skip[None],
            p.init,
            p.after,
            p.states,
        )
        p.g_log = jnp.sum(g_log, axis=0).T * LN2
        p.g_step_bias = jnp.sum(bias, axis=(0, 1))
        p.g_step = tn(grad_pre, p.delta)
        grad_proj = jnp.concatenate(
            [nn(grad_pre, w_step), fold(grad_in_map), fold(p.grad_out_map)], axis=-1
        ).astype(BF)
        p.g_proj = tn(p.act, grad_proj)
        grad_act = base + nt(grad_proj, w_proj)
        grad_conv = grad_act * silu_slope(p.conv_out)
        p.grad_conv = grad_conv
        rim = shift(grad_conv[:, :HALO, :], "seq", -1)
        longer = lax.optimization_barrier(jnp.concatenate([grad_conv, rim], axis=1))
        p.grad_conv_in = sum(
            longer[:, CONV - 1 - k : CONV - 1 - k + span, :] * taps[k] for k in range(CONV)
        ).astype(BF)

    def backward_taps(p, event):
        grad_conv = after(p.grad_conv, event)
        p.g_conv_bias = jnp.sum(grad_conv, axis=(0, 1))
        p.g_taps = jnp.stack(
            [
                jnp.sum(grad_conv * p.conv_ext[:, lo + k : lo + k + span, :], axis=(0, 1))
                for k in range(CONV)
            ],
            axis=-1,
        )

    def backward_input(p):
        grad_normed = nt(p.grad_conv_in, w_conv_in) + nt(p.grad_gate_in, w_gate_in)
        p.input_grad = p.grad_mixed + norm_back(grad_normed * gain_one, p.block, p.scale_one)

    parts = []
    parts.append(forward(0, None, None))
    for m in range(1, groups):
        parts.append(forward(m, parts[-1].send, parts[-1].arrived))
    shared = ()
    for m in range(groups):
        shared = expert(m, shared)
    values, grad_hidden = shared

    def joined(name):
        return jnp.concatenate([getattr(p, name) for p in parts], axis=0)

    def added(name):
        return functools.reduce(jnp.add, [getattr(p, name) for p in parts])

    def added_products(left, right):
        return functools.reduce(
            jnp.add, [tn(getattr(p, left), getattr(p, right)) for p in parts]
        )

    rows_in = joined("rows_in")
    rows_in, values, grad_hidden = after((rows_in, values, grad_hidden), parts[-1].back)
    grad_second = tn(values, rows_in[:, width:]).astype(BF)
    grad_first = tn(grad_hidden, rows_in[:, :width]).astype(BF)
    products = grad_first, grad_second
    parts[0].returned = after(parts[0].returned, products)
    backward_router(parts[0])
    grad_first, grad_second = after(products, parts[0].grad_mix)
    grad_second = lax.psum_scatter(grad_second, "seq", scatter_dimension=0, tiled=True)
    grad_first = lax.psum_scatter(grad_first, "seq", scatter_dimension=0, tiled=True)
    for p, earlier in zip(parts[1:], parts):
        p.returned = after(p.returned, earlier.grad_mix)
        backward_router(p)
    g_feat = jnp.concatenate([added("g_gain_two")[:, None], added("g_router")], axis=1)
    background = jnp.concatenate(
        [
            added_products("normed", "grad_gate_in").astype(BF),
            side_by_side(added_products("gated", "grad_branch").astype(BF), rows),
            pad_cols(g_feat, 128).astype(BF),
        ],
        axis=1,
    )
    background = lax.psum_scatter(background, ("batch", "seq"), scatter_dimension=0, tiled=True)
    background = background.astype(F32)
    g_gate_half = background[:, :DI]
    g_back = one_below(background[:, DI : 2 * DI], rows)
    g_feat = background[:, 2 * DI :]
    for p in parts:
        backward_mixer(p)
    g_conv_half = added_products("normed", "grad_conv_in")
    for p in parts:
        backward_taps(p, g_conv_half)
    g_chan = jnp.concatenate(
        [
            added("g_proj"),
            added("g_step"),
            added("g_log"),
            added("g_taps"),
            added("g_conv_bias")[:, None],
            added("g_step_bias")[:, None],
            added("g_skip")[:, None],
        ],
        axis=1,
    )
    g_chan = pad_cols(g_chan, 256).reshape(-1, 512)
    g_rest = jnp.concatenate([sum_over_seq(g_conv_half), sum_over_seq(g_chan)], axis=2)
    for p in parts:
        p.grad_conv_in = after(p.grad_conv_in, (g_conv_half, background))
        backward_input(p)
    grad_first, grad_second = after((grad_first, grad_second), g_conv_half)
    grad_first = grad_first.astype(F32).T
    grad_second = grad_second.astype(F32)
    g_rest = after(g_rest, (parts[0].input_grad, grad_first, grad_second))
    g_rest = over_batch(g_rest)
    g_rest = after(g_rest, parts[-1].input_grad)
    g_conv_half = g_rest[:, :DI]
    g_chan = g_rest[:, DI:].reshape(-1, 256)
    g_in = jnp.concatenate([g_conv_half, g_gate_half], axis=1)
    g_gain_one = jnp.sum(g_in * in_proj.astype(F32), axis=1) / norm_gain.astype(F32)
    at = maps + DT_RANK
    return (
        joined("activations"),
        joined("input_grad"),
        g_gain_one,
        g_in,
        g_chan[:, at + STATE : at + STATE + CONV],
        g_chan[:, at + STATE + CONV],
        g_chan[:, :maps],
        g_chan[:, maps:at],
        g_chan[:, at + STATE + CONV + 1],
        g_chan[:, at : at + STATE],
        g_chan[:, at + STATE + CONV + 2],
        g_back,
        g_feat[:, 0],
        g_feat[:, 1 : 1 + experts],
        grad_first[None],
        grad_second[None],
    )


def solution(mesh):
    return jax.shard_map(
        shards,
        mesh=mesh,
        in_specs=(
            P("batch", "seq", None),
            P("batch", "seq", None),
            P(),
            P("batch"),
            P("batch", "seq"),
            P("batch", "seq"),
            P(("batch", "seq")),
            P(("batch", "seq"), None),
            P(("batch", "seq"), None),
            P(("batch", "seq")),
            P(("batch", "seq"), None),
            P(("batch", "seq"), None),
            P(("batch", "seq")),
            P(("batch", "seq"), None),
            P(("batch", "seq")),
            P(("batch", "seq"), None),
            P(("batch", "seq")),
            P(("batch", "seq"), None),
            P("batch", None, "seq"),
            P("batch", "seq", None),
        ),
        out_specs=(
            P("batch", "seq", None),
            P("batch", "seq", None),
            P(("batch", "seq")),
            P(("batch", "seq"), None),
            P(("batch", "seq"), None),
            P(("batch", "seq")),
            P(("batch", "seq"), None),
            P(("batch", "seq"), None),
            P(("batch", "seq")),
            P(("batch", "seq"), None),
            P(("batch", "seq")),
            P(("batch", "seq"), None),
            P(("batch", "seq")),
            P(("batch", "seq"), None),
            P("batch", None, "seq"),
            P("batch", "seq", None),
        ),
        check_vma=False,
    )
```

```python
import functools
import math

import jax
import jax.numpy as jnp
from jax import lax
from jax.experimental import pallas as pl
from jax.experimental.pallas import tpu as pltpu
from jax.sharding import PartitionSpec as P

DI = 1536
STATE = 16
DT_RANK = 48
CONV = 4
SEQ_MB = 1
EPSILON = 1e-05
F32 = jnp.float32
BF = jnp.bfloat16
U = 16
CB = 512
CE = 768
VM = 48 << 20
EXPERT_VM = 48 << 20
COST = 1
LOG2E = 1.0 / math.log(2.0)
LN2 = math.log(2.0)
HALO = 8


def end_f_kernel(chunks, s_ref, x_ref, bt_ref, r_ref, h_ref):
    r = r_ref[...]
    width = r.shape[1]
    def chunk(c, h):
        rows = pl.ds(pl.multiple_of(c*U,U),U)
        s8 = s_ref[0, rows, :]
        d8 = x_ref[0, rows, :].astype(F32)*s8
        bt = bt_ref[0, c]
        for k in range(U):
            s = jnp.broadcast_to(s8[k:k+1], (STATE,width))
            d = jnp.broadcast_to(d8[k:k+1], (STATE,width))
            b = jnp.broadcast_to(bt[0:STATE, k:k+1], (STATE,width))
            h = jnp.exp2(s*r)*h + d*b
        return h
    h_ref[0] = lax.fori_loop(0, chunks, chunk, jnp.zeros((STATE,width),F32))


def scan_end_f(s, x, bt, r):
    S,T,C = s.shape
    cb=min(CE,C)
    row=pl.BlockSpec((1,T,cb), lambda i,j:(i,0,j))
    return pl.pallas_call(functools.partial(end_f_kernel, T//U),
        grid=(S,C//cb),
        in_specs=[row,row,pl.BlockSpec((1,T//U,2*STATE,U),lambda i,j:(i,0,0,0)),pl.BlockSpec((STATE,cb),lambda i,j:(0,j))],
        out_specs=pl.BlockSpec((1,STATE,cb),lambda i,j:(i,0,j)),
        out_shape=jax.ShapeDtypeStruct((S,STATE,C),F32),
        compiler_params=pltpu.CompilerParams(vmem_limit_bytes=VM),
        cost_estimate=pl.CostEstimate(flops=COST*S*T*C,bytes_accessed=COST*S*T*C,transcendentals=0),
        name="scan_end_f",
    )(s,x,bt,r)


def end_b_kernel(chunks, s_ref, g_ref, bt_ref, r_ref, h_ref, out_ref, go_ref):
    r = r_ref[...]
    width = r.shape[1]
    @pl.when(pl.program_id(1)==0)
    def _():
        go_ref[...]=jnp.zeros_like(go_ref)
    def chunk(c, h):
        c = chunks-1-c
        rows = pl.ds(pl.multiple_of(c*U,U),U)
        s8 = s_ref[0, rows, :]
        g8 = g_ref[0, rows, :]
        bt = bt_ref[0, c]
        go_ref[0, rows, :] += lax.dot_general(g8.astype(BF), h_ref[0, pl.ds(pl.multiple_of(c*U*STATE,U*STATE),U*STATE), :], (((1,),(1,)),((),())), preferred_element_type=F32)
        for k in range(U-1,-1,-1):
            s = jnp.broadcast_to(s8[k:k+1], (STATE,width))
            g = jnp.broadcast_to(g8[k:k+1], (STATE,width))
            cc = jnp.broadcast_to(bt[STATE:2*STATE, k:k+1], (STATE,width))
            h = jnp.exp2(s*r)*(h + g*cc)
        return h
    out_ref[0] = lax.fori_loop(0, chunks, chunk, jnp.zeros((STATE,width),F32))


def scan_end_b(s, g, bt, r, h):
    S,T,C = s.shape
    cb=min(CE,C)
    row=pl.BlockSpec((1,T,cb), lambda i,j:(i,0,j))
    return pl.pallas_call(functools.partial(end_b_kernel, T//U),
        grid=(S,C//cb),
        in_specs=[row,row,pl.BlockSpec((1,T//U,2*STATE,U),lambda i,j:(i,0,0,0)),pl.BlockSpec((STATE,cb),lambda i,j:(0,j)),pl.BlockSpec((1,T*STATE,cb),lambda i,j:(i,0,j))],
        out_specs=[pl.BlockSpec((1,STATE,cb),lambda i,j:(i,0,j)),pl.BlockSpec((1,T,U*STATE),lambda i,j:(i,0,0))],
        out_shape=[jax.ShapeDtypeStruct((S,STATE,C),F32),jax.ShapeDtypeStruct((S,T,U*STATE),F32)],
        compiler_params=pltpu.CompilerParams(vmem_limit_bytes=VM),
        cost_estimate=pl.CostEstimate(flops=COST*S*T*C,bytes_accessed=COST*S*T*C,transcendentals=0),
        name="scan_end_b",
    )(s,g,bt,r,h)


def fwd_kernel(chunks, s_ref, x_ref, bt_ref, l_ref, r_ref, h0_ref, y_ref, h_ref, even, odd):
    r = r_ref[...]
    width = r.shape[1]
    def rows_at(c, size):
        return pl.ds(pl.multiple_of(c*size,size),size)
    def chunk(c, h, mine, other):
        before = jnp.maximum(c-1,0)
        y_ref[0, rows_at(before,U), :] = jnp.dot(l_ref[0, rows_at(before,U), :], other[...], preferred_element_type=F32)
        rows = rows_at(c,U)
        s8 = s_ref[0, rows, :]
        d8 = x_ref[0, rows, :].astype(F32)*s8
        bt = bt_ref[0, c]
        for k in range(U):
            s = jnp.broadcast_to(s8[k:k+1], (STATE,width))
            d = jnp.broadcast_to(d8[k:k+1], (STATE,width))
            b = jnp.broadcast_to(bt[0:STATE, k:k+1], (STATE,width))
            h = jnp.exp2(s*r)*h + d*b
            low = h.astype(BF)
            mine[k*STATE:(k+1)*STATE, :] = low
            h_ref[0, pl.ds(pl.multiple_of(c*U*STATE+k*STATE,STATE),STATE), :] = low
        return h
    def pair(i, h):
        h = chunk(2*i, h, even, odd)
        return chunk(2*i+1, h, odd, even)
    odd[...] = jnp.zeros_like(odd)
    lax.fori_loop(0, chunks//2, pair, h0_ref[0])
    last = pl.ds((chunks-1)*U,U)
    y_ref[0, last, :] = jnp.dot(l_ref[0, last, :], odd[...], preferred_element_type=F32)

def scan_fwd(s, x, bt, l, r, h0):
    S,T,C = s.shape
    cb=min(CB,C)
    row=pl.BlockSpec((1,T,cb), lambda i,j:(i,0,j))
    st=pl.BlockSpec((1,STATE,cb),lambda i,j:(i,0,j))
    return pl.pallas_call(functools.partial(fwd_kernel, T//U),
        grid=(S,C//cb),
        in_specs=[row,row,pl.BlockSpec((1,T//U,2*STATE,U),lambda i,j:(i,0,0,0)),pl.BlockSpec((1,T,U*STATE),lambda i,j:(i,0,0)),pl.BlockSpec((STATE,cb),lambda i,j:(0,j)),st],
        out_specs=[row,pl.BlockSpec((1,T*STATE,cb),lambda i,j:(i,0,j))],
        out_shape=[jax.ShapeDtypeStruct((S,T,C),F32),jax.ShapeDtypeStruct((S,T*STATE,C),BF)],
        scratch_shapes=[pltpu.VMEM((U*STATE,cb),BF)]*2,
        compiler_params=pltpu.CompilerParams(vmem_limit_bytes=VM),
        cost_estimate=pl.CostEstimate(flops=COST*S*T*C,bytes_accessed=COST*S*T*C,transcendentals=0),
        name="scan_fwd",
    )(s,x,bt,l,r,h0)


def bwd_kernel(chunks, s_ref, x_ref, g_ref, bt_ref, l_ref, one_ref, r_ref, k_ref, h0_ref, m0_ref, h_ref,
               pre_ref, base_ref, bias_ref, alog_ref, gi_ref, lam_e, fr_e, lam_o, fr_o):
    r = r_ref[...]
    width = r.shape[1]
    j = pl.program_id(1)
    nt=(((1,),(1,)),((),()))
    def rows_at(c, size):
        return pl.ds(pl.multiple_of(c*size,size),size)
    @pl.when(j==0)
    def _():
        gi_ref[...]=jnp.zeros_like(gi_ref)
    bias_ref[...] = jnp.zeros_like(bias_ref)
    lam_o[...] = jnp.zeros_like(lam_o)
    fr_o[...] = jnp.zeros_like(fr_o)
    def sums(c, lam_s, fr_s, first=None):
        rows = rows_at(c,U)
        s8 = s_ref[0, rows, :]
        x8 = x_ref[0, rows, :].astype(F32)
        d8 = (x8*s8).astype(BF)
        lam_all = lam_s[...]
        pull = jnp.dot(l_ref[0, rows, :], lam_all, preferred_element_type=F32)
        gs = jnp.dot(one_ref[...], fr_s[...], preferred_element_type=F32)
        slope = jnp.where(s8 < 0.03, s8*(1.0-s8*(0.5-s8*(1.0/6.0))), 1.0-jnp.exp(-s8))
        arg = (gs*LN2 + x8*pull)*slope
        pre_ref[0, rows, :] = arg.astype(BF)
        base_ref[0, rows, :] = k_ref[...]*g_ref[0, rows, :] + s8*pull
        part = arg[:8]+arg[8:]
        gi = lax.dot_general(d8, lam_all, nt, preferred_element_type=F32)
        if first is not None:
            gi = jnp.where(first, 0.0, gi)
            part = jnp.where(first, 0.0, part)
        gi_ref[0, rows, :] += gi
        bias_ref[0] += part
    def chunk(c, carry, mine, other, first=None):
        lam_c, alog = carry
        sums(jnp.minimum(c+1,chunks-1), *other, first)
        lam_s, fr_s = mine
        rows = rows_at(c,U)
        s8 = s_ref[0, rows, :]
        g8 = g_ref[0, rows, :]
        bt = bt_ref[0, c]
        for k in range(U-1,-1,-1):
            s = jnp.broadcast_to(s8[k:k+1], (STATE,width))
            g = jnp.broadcast_to(g8[k:k+1], (STATE,width))
            cc = jnp.broadcast_to(bt[STATE:2*STATE, k:k+1], (STATE,width))
            if k:
                hp = h_ref[0, pl.ds(pl.multiple_of(c*U*STATE+(k-1)*STATE,STATE),STATE), :].astype(F32)
            else:
                hp = h_ref[0, pl.ds(pl.multiple_of(jnp.maximum(c*U*STATE-STATE,0),STATE),STATE), :].astype(F32)
                hp = jnp.where(c==0, h0_ref[0], hp)
            lam = lam_c + g*cc
            lam_c = jnp.exp2(s*r)*lam
            fr = lam_c*hp*r
            alog = alog + fr*s
            lam_s[k*STATE:(k+1)*STATE,:] = lam.astype(BF)
            fr_s[k*STATE:(k+1)*STATE,:] = fr.astype(BF)
        return lam_c, alog
    E=(lam_e,fr_e); O=(lam_o,fr_o)
    def pair(i, carry):
        c = chunks-1-2*i
        carry = chunk(c, carry, E, O, i==0)
        return chunk(c-1, carry, O, E)
    _, alog = lax.fori_loop(0, chunks//2, pair, (m0_ref[0], jnp.zeros((STATE,width),F32)))
    sums(0, *O)
    alog_ref[0] = alog

def scan_bwd(s, x, g, bt, l, one, r, k, h0, m0, h):
    S,T,C = s.shape
    cb=min(CB,C)
    row=pl.BlockSpec((1,T,cb), lambda i,j:(i,0,j))
    st=pl.BlockSpec((1,STATE,cb),lambda i,j:(i,0,j))
    lo=pl.BlockSpec((1,T,U*STATE),lambda i,j:(i,0,0))
    return pl.pallas_call(functools.partial(bwd_kernel, T//U),
        grid=(S,C//cb),
        in_specs=[row,row,row,pl.BlockSpec((1,T//U,2*STATE,U),lambda i,j:(i,0,0,0)),lo,pl.BlockSpec((U,U*STATE),lambda i,j:(0,0)),pl.BlockSpec((STATE,cb),lambda i,j:(0,j)),pl.BlockSpec((1,cb),lambda i,j:(0,j)),st,st,pl.BlockSpec((1,T*STATE,cb),lambda i,j:(i,0,j))],
        out_specs=[row,row,pl.BlockSpec((1,8,cb),lambda i,j:(i,0,j)),st,lo],
        out_shape=[jax.ShapeDtypeStruct((S,T,C),BF),jax.ShapeDtypeStruct((S,T,C),F32),jax.ShapeDtypeStruct((S,8,C),F32),jax.ShapeDtypeStruct((S,STATE,C),F32),jax.ShapeDtypeStruct((S,T,U*STATE),F32)],
        scratch_shapes=[pltpu.VMEM((U*STATE,cb),BF)]*4,
        compiler_params=pltpu.CompilerParams(vmem_limit_bytes=VM),
        cost_estimate=pl.CostEstimate(flops=COST*S*T*C,bytes_accessed=COST*S*T*C,transcendentals=0),
        name="scan_bwd",
    )(s,x,g,bt,l,one,r,k,h0,m0,h)


def gelu_and_slope(x):
    root = math.sqrt(2.0 / math.pi)
    square = x * x
    t = jnp.tanh(x * (root + (root * 0.044715) * square))
    half = 0.5 + 0.5 * t
    slope = half + (0.5 * x) * (1.0 - t * t) * (root + (3.0 * root * 0.044715) * square)
    return x * half, slope


def expert_kernel(pieces, tile, second_at, x_ref, f_ref, w_ref, *refs):
    back_ref, value_ref, grad_ref, first_s, second_s, out_s, gin_s, sems = refs[-8:]
    j = pl.program_id(0)
    rows, width = out_s.shape
    hidden = first_s.shape[2]
    copies = [
        pltpu.make_async_copy(f_ref.at[q, pl.ds(0, width), :], first_s.at[q], sems.at[q])
        for q in range(pieces)
    ] + [
        pltpu.make_async_copy(
            w_ref.at[q, pl.ds(second_at, hidden), :], second_s.at[q], sems.at[pieces + q]
        )
        for q in range(pieces)
    ]

    @pl.when(j == 0)
    def _():
        for q in range(pieces):
            copies[q].start()
            copies[q + pieces].start()

    for q in range(pieces):
        @pl.when(j == q)
        def _():
            copies[q].wait()
            copies[q + pieces].wait()

    def mm(a, b, dims):
        return lax.dot_general(a, b, (dims, ((), ())), preferred_element_type=F32)

    first = first_s[j]
    second = second_s[j]
    for i in range(rows // tile):
        at = slice(i * tile, (i + 1) * tile)
        hidden = mm(x_ref[at, :width], first, ((1,), (0,)))
        grad = mm(x_ref[at, width:], second, ((1,), (1,)))
        value, slope = gelu_and_slope(hidden)
        value = value.astype(BF)
        grad = (grad * slope).astype(BF)
        value_ref[at, :] = value
        grad_ref[at, :] = grad
        out = mm(value, second, ((1,), (0,)))
        gin = mm(grad, first, ((1,), (1,)))

        @pl.when(j == 0)
        def _():
            out_s[at, :] = out
            gin_s[at, :] = gin

        @pl.when(j > 0)
        def _():
            out_s[at, :] += out
            gin_s[at, :] += gin

    @pl.when(j == pieces - 1)
    def _():
        back_ref[:, :width] = out_s[...].astype(BF)
        back_ref[:, width:] = gin_s[...].astype(BF)


def expert_call(x, firsts, seconds, second_at, part, groups, shared):
    rows, width = x.shape[0], x.shape[1] // 2
    pieces, _, quarter = firsts.shape
    tile = math.gcd(rows, 320)
    wide = pl.BlockSpec((rows, quarter), lambda j: (part, j))
    anywhere = pl.BlockSpec(memory_space=pl.ANY)
    whole = pl.BlockSpec((rows, 2 * width), lambda j: (0, 0))
    big = jax.ShapeDtypeStruct((groups * rows, pieces * quarter), BF)
    count = 3
    return pl.pallas_call(
        functools.partial(expert_kernel, pieces, tile, second_at),
        grid=(pieces,),
        in_specs=[whole] + [anywhere] * (2 + len(shared)),
        out_specs=[whole, wide, wide],
        out_shape=[jax.ShapeDtypeStruct((rows, 2 * width), BF), big, big],
        scratch_shapes=[
            pltpu.VMEM((pieces, width, quarter), BF),
            pltpu.VMEM((pieces, quarter, width), BF),
            pltpu.VMEM((rows, width), F32),
            pltpu.VMEM((rows, width), F32),
            pltpu.SemaphoreType.DMA((2 * pieces,)),
        ],
        input_output_aliases={count: 1, count + 1: 2} if shared else {},
        compiler_params=pltpu.CompilerParams(vmem_limit_bytes=EXPERT_VM),
        cost_estimate=pl.CostEstimate(
            flops=COST * rows * width, bytes_accessed=COST * rows * width, transcendentals=0
        ),
        name="expert",
    )(x, firsts, seconds, *shared)


def own_rows(span):
    return jnp.arange(span)[:, None] % U == jnp.arange(U * STATE)[None] // STATE


def state_picker():
    return (jnp.arange(STATE)[:, None] == jnp.arange(U * STATE)[None] % STATE).astype(BF)


def fold(z):
    z = jnp.where(own_rows(z.shape[1]), z, 0).astype(BF)
    return nt(z, state_picker())


def spread_rows(m):
    wide = nn(m.astype(BF), state_picker())
    return jnp.where(own_rows(m.shape[1]), wide, 0).astype(BF)


def bits_of(axis):
    return lax.axis_size(axis).bit_length() - 1


def my_bit(axis, k):
    return (lax.axis_index(axis) >> k) & 1


def swap(x, axis, k):
    count = lax.axis_size(axis)
    return lax.ppermute(x, axis, [(i, i ^ (1 << k)) for i in range(count)])


def shift(x, axis, distance):
    count = lax.axis_size(axis)
    return lax.ppermute(
        x, axis, [(i, i + distance) for i in range(count) if 0 <= i + distance < count]
    )


def joined_pair(x, other, axis, k, place):
    high = my_bit(axis, k) == 1
    return jnp.where(
        high,
        jnp.concatenate([other, x], axis=place),
        jnp.concatenate([x, other], axis=place),
    )


def from_batch(x):
    copies = jnp.broadcast_to(x[None], (lax.axis_size("batch"),) + x.shape)
    return lax.all_to_all(copies, "batch", split_axis=0, concat_axis=0, tiled=True)


def over_seq(x):
    bits = bits_of("seq")
    out = x.reshape(x.shape[:1] + (1,) * bits + x.shape[1:])
    for k in reversed(range(bits)):
        out = joined_pair(out, swap(out, "seq", k), "seq", k, bits - k)
    return out.reshape((-1,) + x.shape[2:])


def over_batch(x):
    got = lax.all_to_all(x.astype(BF), "batch", split_axis=0, concat_axis=0, tiled=True)
    return jnp.sum(got.astype(F32), axis=0)


def halved(x, k, place):
    bit = my_bit("seq", k)
    mine = lax.dynamic_index_in_dim(x, bit, place, True)
    theirs = lax.dynamic_index_in_dim(x, 1 - bit, place, True).astype(BF)
    return mine + swap(theirs, "seq", k).astype(F32)


def sum_over_seq(x):
    bits = bits_of("seq")
    rows = x.shape[0] // (lax.axis_size("batch") << bits)
    out = x.reshape((lax.axis_size("batch"),) + (2,) * bits + (rows,) + x.shape[1:])
    for k in range(bits):
        out = halved(out, k, bits - k)
    return out.reshape((lax.axis_size("batch"), rows) + x.shape[1:])


def totals_of(total):
    levels = []
    for k in range(bits_of("seq")):
        other = swap(total, "seq", k)
        levels.append((total, other))
        total = total + other
    return levels


def prefix(levels, state, rate, backward):
    before = jnp.zeros_like(state)
    before_total = jnp.zeros_like(levels[0][0])
    for k, (total, other_total) in enumerate(levels):
        other = swap(state.astype(BF), "seq", k).astype(F32)
        first = my_bit("seq", k) == (0 if backward else 1)
        before = jnp.where(
            first, before + jnp.exp2(before_total[:, None, :] * rate) * other, before
        )
        before_total = jnp.where(first, before_total + other_total, before_total)
        if k + 1 < len(levels):
            near = jnp.where(first, state, other)
            far = jnp.where(first, other, state)
            near_total = jnp.where(first, total, other_total)
            state = near + jnp.exp2(near_total[:, None, :] * rate) * far
    return before


def after(value, event):
    return lax.optimization_barrier((value, event))[0]


def mm(left, right, dims):
    return lax.dot_general(left, right, (dims, ((), ())), preferred_element_type=F32)


def nn(left, right):
    return mm(left, right, ((left.ndim - 1,), (0,)))


def nt(left, right):
    return mm(left, right, ((left.ndim - 1,), (1,)))


def tn(left, right):
    lead = tuple(range(left.ndim - 1))
    return mm(left, right, (lead, lead))


def silu_slope(v):
    s = jax.nn.sigmoid(v)
    return s * (1.0 + v * (1.0 - s))


def norm_back(grad_norm, x, scale):
    return scale * grad_norm - x * scale**3 * jnp.mean(grad_norm * x, axis=-1, keepdims=True)


def gelu_tanh(v):
    return jax.nn.gelu(v, approximate=True)


def rms(x):
    return lax.rsqrt(jnp.mean(x * x, axis=-1, keepdims=True) + EPSILON)


def side_by_side(x, rows):
    width = x.shape[1]
    x = x.reshape(-1, 2, rows, width)
    return jnp.concatenate([x[:, h].reshape(-1, width) for h in range(2)], axis=1)


def one_below(x, rows):
    width = x.shape[1] // 2
    halves = [x[:, h * width : (h + 1) * width].reshape(-1, rows, width) for h in range(2)]
    return jnp.concatenate(halves, axis=1).reshape(-1, width)


def pad_cols(x, width):
    return jnp.pad(x, ((0, 0), (0, width - x.shape[1])))


def shards(
    tokens,
    cotangent,
    lengths,
    order,
    expert_route,
    slot_index,
    norm_gain,
    in_proj,
    conv_weight,
    conv_bias,
    x_proj,
    dt_proj,
    dt_bias,
    a_log,
    skip_gain,
    out_proj,
    moe_gain,
    router,
    expert_in,
    expert_out,
):
    seqs, span, width = tokens.shape
    batch = lax.axis_size("batch")
    experts = expert_in.shape[0] * batch
    capacity = max(2, (5 * SEQ_MB * span + 4 * experts - 1) // (4 * experts))
    maps = DT_RANK + 2 * STATE
    lo = HALO - (CONV - 1)
    groups = 2
    size = seqs // groups

    rows = in_proj.shape[0]
    chan = jnp.concatenate(
        [
            x_proj,
            dt_proj,
            a_log,
            conv_weight,
            conv_bias[:, None],
            dt_bias[:, None],
            skip_gain[:, None],
        ],
        axis=1,
    )
    feat = jnp.concatenate([norm_gain[:, None], moe_gain[:, None], router], axis=1)
    used = chan.shape[1]
    second_set = jnp.concatenate(
        [
            pad_cols(jnp.concatenate([chan[:rows], feat], axis=1), 192),
            pad_cols(chan[rows:], 192),
        ],
        axis=1,
    )
    second_set = over_seq(second_set[None])
    first_set = from_batch(in_proj[:, :DI])
    second_set = from_batch(after(second_set, first_set)).reshape(-1, second_set.shape[1])
    later = jnp.concatenate([in_proj[:, DI:], side_by_side(out_proj, rows)], axis=1)
    later = after(later, first_set)
    later = lax.all_gather(later, ("batch", "seq"), axis=0, tiled=True)
    w_gate_in = later[:, :DI]
    w_back = one_below(later[:, DI:], rows)
    if expert_in.shape[2] == width:
        both = jnp.concatenate([expert_in[0], expert_out[0]], axis=0)
        both = lax.all_gather(after(both, later), "seq", axis=0, tiled=False)
        expert_weights = both, both, width
    else:
        own = after((expert_in[0], expert_out[0]), later)
        expert_weights = *(lax.all_gather(x, "seq", axis=0, tiled=False) for x in own), 0
    first_set = over_seq(first_set)
    w_conv_in = first_set
    chan = one_below(second_set, rows)
    feat = chan.reshape(-1, 2, rows, 192)[:, 0].reshape(-1, 192)[:, used:]
    gain_one = feat[:, 0].astype(F32)
    gain_two = feat[:, 1].astype(F32)
    router_weight = feat[:, 2 : 2 + experts]
    w_proj = chan[:, :maps]
    at = maps + DT_RANK
    w_step = chan[:, maps:at]
    rate = -jnp.exp(chan[:, at : at + STATE].astype(F32)).T * LOG2E
    at = at + STATE
    taps = chan[:, at : at + CONV].astype(F32).T
    bias_conv = chan[:, at + CONV].astype(F32)
    bias_step = chan[:, at + CONV + 1].astype(F32)
    skip = chan[:, at + CONV + 2].astype(F32)

    halo_all = shift(tokens[:, span - HALO :, :], "seq", 1)
    tail = jnp.arange(HALO)[:, None] >= lo
    halo_all = jnp.where(tail, halo_all, 0)


    positions = lax.axis_index("seq") * span + jnp.arange(span, dtype=jnp.int32)
    row_length = jnp.sum(
        jnp.where(
            order[:, None] == jnp.arange(lengths.shape[0], dtype=jnp.int32)[None, :],
            lengths[None, :],
            0,
        ),
        axis=1,
    )
    keep_all = (positions[None, :] < row_length[:, None]).astype(F32)
    ones = (jnp.arange(U)[:, None] == jnp.arange(U * STATE)[None] // STATE).astype(BF)
    slots = jnp.arange(experts * capacity, dtype=jnp.int32)
    expert_ids = jnp.arange(experts, dtype=jnp.int32)

    class Part:
        pass

    def forward(m, event, second_event):
        p = Part()
        here = slice(m * size, (m + 1) * size)
        own = tokens[here]
        if event is not None:
            own = after(own, event)
        p.block = own.astype(F32)
        p.scale_one = rms(p.block)
        ext = jnp.concatenate([halo_all[here], own], axis=1).astype(F32)
        normed_ext = (ext * rms(ext) * gain_one).astype(BF)
        p.normed = normed_ext[:, HALO:]
        p.conv_ext = nn(normed_ext, w_conv_in)
        p.conv_out = bias_conv + sum(
            p.conv_ext[:, lo + k : lo + k + span, :] * taps[k] for k in range(CONV)
        )
        p.act = jax.nn.silu(p.conv_out).astype(BF)
        projected = nn(p.act, w_proj)
        p.delta = projected[..., :DT_RANK].astype(BF)
        input_map = projected[..., DT_RANK : DT_RANK + STATE]
        output_map = projected[..., DT_RANK + STATE :]
        p.step_arg = nt(p.delta, w_step) + bias_step
        p.step = jax.nn.softplus(p.step_arg)
        p.levels = totals_of(jnp.sum(p.step, axis=1))
        p.both = jnp.swapaxes(
            projected[..., DT_RANK:].reshape(size, span // U, U, 2 * STATE), 2, 3
        )
        p.in_rows = spread_rows(input_map)
        out_rows = spread_rows(output_map)
        end = scan_end_f(p.step, p.act, p.both, rate)
        p.init = prefix(p.levels, end, rate, False)
        if second_event is not None:
            p.init = after(p.init, second_event)
        p.gate_in = nn(p.normed, w_gate_in)
        y, p.states = scan_fwd(p.step, p.act, p.both, out_rows, rate, p.init)
        p.actf = p.act.astype(F32)
        p.mix = y + skip * p.actf
        p.gate_act = jax.nn.silu(p.gate_in)
        p.gated = (p.mix * p.gate_act).astype(BF)
        p.mixed = p.block + nn(p.gated, w_back)
        p.scale_two = rms(p.mixed)
        p.routed = (p.mixed * p.scale_two * gain_two).astype(BF)
        p.probs = jax.nn.softmax(nn(p.routed, router_weight), axis=-1)
        route = expert_route[here]
        slot = slot_index[here]
        kept = slot >= 0
        target = jnp.where(kept, route * capacity + slot, -1)
        p.selector = (target[..., None] == slots).astype(BF)
        p.chosen = jnp.logical_and(route[..., None] == expert_ids, kept[..., None])
        p.gate = jnp.sum(jnp.where(p.chosen, p.probs, 0.0), axis=-1)[..., None]
        p.grad_out = cotangent[here].astype(F32) * keep_all[here][..., None]
        grad_value = (p.gate * p.grad_out).astype(BF)
        packed = jnp.concatenate([p.routed, grad_value], axis=-1)
        send = jnp.einsum("stc,std->scd", p.selector, packed, preferred_element_type=F32)
        send = jnp.swapaxes(send.astype(BF).reshape(size, batch, capacity, 2 * width), 0, 1)
        p.send = send
        p.arrived = lax.all_to_all(send, "batch", split_axis=0, concat_axis=0, tiled=True)
        return p

    def expert(m, shared):
        p = parts[m]
        arrived = after(p.arrived, parts[m - 1].back) if m else p.arrived
        p.rows_in = arrived.reshape(batch * size * capacity, 2 * width)
        p.back, *shared = expert_call(p.rows_in, *expert_weights, m, groups, shared)
        back = p.back.reshape(batch, size, capacity, 2 * width)
        if m:
            back = after(back, parts[m - 1].returned)
        back = lax.all_to_all(back, "batch", split_axis=0, concat_axis=0, tiled=True)
        p.returned = jnp.swapaxes(back, 0, 1).reshape(size, experts * capacity, 2 * width)
        return shared

    def backward_router(p):
        picked = jnp.einsum("stc,scd->std", p.selector, p.returned, preferred_element_type=F32)
        expert_tok = picked[..., :width]
        p.activations = (p.mixed + p.gate * expert_tok).astype(BF)
        grad_gate = jnp.sum(expert_tok * p.grad_out, axis=-1, keepdims=True)
        grad_prob = jnp.where(p.chosen, grad_gate, 0.0)
        grad_logits = (
            p.probs * (grad_prob - jnp.sum(p.probs * grad_prob, axis=-1, keepdims=True))
        ).astype(BF)
        p.g_router = tn(p.routed, grad_logits)
        grad_routed = picked[..., width:] + nt(grad_logits, router_weight)
        p.g_gain_two = jnp.sum(grad_routed * p.mixed * p.scale_two, axis=(0, 1))
        p.grad_mixed = p.grad_out + norm_back(grad_routed * gain_two, p.mixed, p.scale_two)
        p.grad_branch = p.grad_mixed.astype(BF)
        grad_gated = nt(p.grad_branch, w_back)
        p.grad_mix = grad_gated * p.gate_act
        p.grad_gate_in = (grad_gated * p.mix * silu_slope(p.gate_in)).astype(BF)
        p.behind, p.grad_out_map = scan_end_b(p.step, p.grad_mix, p.both, rate, p.states)
        p.after = prefix(p.levels, p.behind, rate, True)
        p.g_skip = jnp.sum(p.grad_mix * p.actf, axis=(0, 1))

    def backward_mixer(p):
        grad_pre, base, bias, g_log, grad_in_map = scan_bwd(
            p.step,
            p.act,
            p.grad_mix,
            p.both,
            p.in_rows,
            ones,
            rate,
            skip[None],
            p.init,
            p.after,
            p.states,
        )
        p.g_log = jnp.sum(g_log, axis=0).T * LN2
        p.g_step_bias = jnp.sum(bias, axis=(0, 1))
        p.g_step = tn(grad_pre, p.delta)
        grad_proj = jnp.concatenate(
            [nn(grad_pre, w_step), fold(grad_in_map), fold(p.grad_out_map)], axis=-1
        ).astype(BF)
        p.g_proj = tn(p.act, grad_proj)
        grad_act = base + nt(grad_proj, w_proj)
        grad_conv = grad_act * silu_slope(p.conv_out)
        p.grad_conv = grad_conv
        rim = shift(grad_conv[:, :HALO, :], "seq", -1)
        longer = lax.optimization_barrier(jnp.concatenate([grad_conv, rim], axis=1))
        p.grad_conv_in = sum(
            longer[:, CONV - 1 - k : CONV - 1 - k + span, :] * taps[k] for k in range(CONV)
        ).astype(BF)

    def backward_taps(p, event):
        grad_conv = after(p.grad_conv, event)
        p.g_conv_bias = jnp.sum(grad_conv, axis=(0, 1))
        p.g_taps = jnp.stack(
            [
                jnp.sum(grad_conv * p.conv_ext[:, lo + k : lo + k + span, :], axis=(0, 1))
                for k in range(CONV)
            ],
            axis=-1,
        )

    def backward_input(p):
        grad_normed = nt(p.grad_conv_in, w_conv_in) + nt(p.grad_gate_in, w_gate_in)
        p.input_grad = p.grad_mixed + norm_back(grad_normed * gain_one, p.block, p.scale_one)

    parts = []
    parts.append(forward(0, None, None))
    for m in range(1, groups):
        parts.append(forward(m, parts[-1].send, parts[-1].arrived))
    shared = ()
    for m in range(groups):
        shared = expert(m, shared)
    values, grad_hidden = shared

    def joined(name):
        return jnp.concatenate([getattr(p, name) for p in parts], axis=0)

    def added(name):
        return functools.reduce(jnp.add, [getattr(p, name) for p in parts])

    def added_products(left, right):
        return functools.reduce(
            jnp.add, [tn(getattr(p, left), getattr(p, right)) for p in parts]
        )

    rows_in = joined("rows_in")
    rows_in, values, grad_hidden = after((rows_in, values, grad_hidden), parts[-1].back)
    grad_second = tn(values, rows_in[:, width:]).astype(BF)
    grad_first = tn(grad_hidden, rows_in[:, :width]).astype(BF)
    products = grad_first, grad_second
    parts[0].returned = after(parts[0].returned, products)
    backward_router(parts[0])
    grad_first, grad_second = after(products, parts[0].grad_mix)
    grad_second = lax.psum_scatter(grad_second, "seq", scatter_dimension=0, tiled=True)
    grad_first = lax.psum_scatter(grad_first, "seq", scatter_dimension=0, tiled=True)
    for p, earlier in zip(parts[1:], parts):
        p.returned = after(p.returned, earlier.grad_mix)
        backward_router(p)
    g_feat = jnp.concatenate([added("g_gain_two")[:, None], added("g_router")], axis=1)
    background = jnp.concatenate(
        [
            added_products("normed", "grad_gate_in").astype(BF),
            side_by_side(added_products("gated", "grad_branch").astype(BF), rows),
            pad_cols(g_feat, 128).astype(BF),
        ],
        axis=1,
    )
    background = lax.psum_scatter(background, ("batch", "seq"), scatter_dimension=0, tiled=True)
    background = background.astype(F32)
    g_gate_half = background[:, :DI]
    g_back = one_below(background[:, DI : 2 * DI], rows)
    g_feat = background[:, 2 * DI :]
    for p in parts:
        backward_mixer(p)
    g_conv_half = added_products("normed", "grad_conv_in")
    for p in parts:
        backward_taps(p, g_conv_half)
    g_chan = jnp.concatenate(
        [
            added("g_proj"),
            added("g_step"),
            added("g_log"),
            added("g_taps"),
            added("g_conv_bias")[:, None],
            added("g_step_bias")[:, None],
            added("g_skip")[:, None],
        ],
        axis=1,
    )
    g_chan = pad_cols(g_chan, 256).reshape(-1, 512)
    g_rest = jnp.concatenate([sum_over_seq(g_conv_half), sum_over_seq(g_chan)], axis=2)
    for p in parts:
        p.grad_conv_in = after(p.grad_conv_in, (g_conv_half, background))
        backward_input(p)
    grad_first, grad_second = after((grad_first, grad_second), g_conv_half)
    grad_first = grad_first.astype(F32).T
    grad_second = grad_second.astype(F32)
    g_rest = after(g_rest, (parts[0].input_grad, grad_first, grad_second))
    g_rest = over_batch(g_rest)
    g_rest = after(g_rest, parts[-1].input_grad)
    g_conv_half = g_rest[:, :DI]
    g_chan = g_rest[:, DI:].reshape(-1, 256)
    g_in = jnp.concatenate([g_conv_half, g_gate_half], axis=1)
    g_gain_one = jnp.sum(g_in * in_proj.astype(F32), axis=1) / norm_gain.astype(F32)
    at = maps + DT_RANK
    return (
        joined("activations"),
        joined("input_grad"),
        g_gain_one,
        g_in,
        g_chan[:, at + STATE : at + STATE + CONV],
        g_chan[:, at + STATE + CONV],
        g_chan[:, :maps],
        g_chan[:, maps:at],
        g_chan[:, at + STATE + CONV + 1],
        g_chan[:, at : at + STATE],
        g_chan[:, at + STATE + CONV + 2],
        g_back,
        g_feat[:, 0],
        g_feat[:, 1 : 1 + experts],
        grad_first[None],
        grad_second[None],
    )


def solution(mesh):
    return jax.shard_map(
        shards,
        mesh=mesh,
        in_specs=(
            P("batch", "seq", None),
            P("batch", "seq", None),
            P(),
            P("batch"),
            P("batch", "seq"),
            P("batch", "seq"),
            P(("batch", "seq")),
            P(("batch", "seq"), None),
            P(("batch", "seq"), None),
            P(("batch", "seq")),
            P(("batch", "seq"), None),
            P(("batch", "seq"), None),
            P(("batch", "seq")),
            P(("batch", "seq"), None),
            P(("batch", "seq")),
            P(("batch", "seq"), None),
            P(("batch", "seq")),
            P(("batch", "seq"), None),
            P("batch", None, "seq"),
            P("batch", "seq", None),
        ),
        out_specs=(
            P("batch", "seq", None),
            P("batch", "seq", None),
            P(("batch", "seq")),
            P(("batch", "seq"), None),
            P(("batch", "seq"), None),
            P(("batch", "seq")),
            P(("batch", "seq"), None),
            P(("batch", "seq"), None),
            P(("batch", "seq")),
            P(("batch", "seq"), None),
            P(("batch", "seq")),
            P(("batch", "seq"), None),
            P(("batch", "seq")),
            P(("batch", "seq"), None),
            P("batch", None, "seq"),
            P("batch", "seq", None),
        ),
        check_vma=False,
    )
```

```python
import functools
import math

import jax
import jax.numpy as jnp
from jax import lax
from jax.experimental import pallas as pl
from jax.experimental.pallas import tpu as pltpu
from jax.sharding import PartitionSpec as P

DI = 1536
STATE = 16
DT_RANK = 48
CONV = 4
SEQ_MB = 1
EPSILON = 1e-05
F32 = jnp.float32
BF = jnp.bfloat16
U = 16
CB = 512
CE = 768
VM = 48 << 20
EXPERT_VM = 48 << 20
COST = 1
LOG2E = 1.0 / math.log(2.0)
LN2 = math.log(2.0)
HALO = 8


def end_f_kernel(chunks, s_ref, x_ref, bt_ref, r_ref, h_ref):
    r = r_ref[...]
    width = r.shape[1]
    def chunk(c, h):
        rows = pl.ds(pl.multiple_of(c*U,U),U)
        s8 = s_ref[0, rows, :]
        d8 = x_ref[0, rows, :].astype(F32)*s8
        bt = bt_ref[0, c]
        for k in range(U):
            s = jnp.broadcast_to(s8[k:k+1], (STATE,width))
            d = jnp.broadcast_to(d8[k:k+1], (STATE,width))
            b = jnp.broadcast_to(bt[0:STATE, k:k+1], (STATE,width))
            h = jnp.exp2(s*r)*h + d*b
        return h
    h_ref[0] = lax.fori_loop(0, chunks, chunk, jnp.zeros((STATE,width),F32))


def scan_end_f(s, x, bt, r):
    S,T,C = s.shape
    cb=min(CE,C)
    row=pl.BlockSpec((1,T,cb), lambda i,j:(i,0,j))
    return pl.pallas_call(functools.partial(end_f_kernel, T//U),
        grid=(S,C//cb),
        in_specs=[row,row,pl.BlockSpec((1,T//U,2*STATE,U),lambda i,j:(i,0,0,0)),pl.BlockSpec((STATE,cb),lambda i,j:(0,j))],
        out_specs=pl.BlockSpec((1,STATE,cb),lambda i,j:(i,0,j)),
        out_shape=jax.ShapeDtypeStruct((S,STATE,C),F32),
        compiler_params=pltpu.CompilerParams(vmem_limit_bytes=VM),
        cost_estimate=pl.CostEstimate(flops=COST*S*T*C,bytes_accessed=COST*S*T*C,transcendentals=0),
        name="scan_end_f",
    )(s,x,bt,r)


def end_b_kernel(chunks, s_ref, g_ref, bt_ref, r_ref, h_ref, out_ref, go_ref):
    r = r_ref[...]
    width = r.shape[1]
    @pl.when(pl.program_id(1)==0)
    def _():
        go_ref[...]=jnp.zeros_like(go_ref)
    def chunk(c, h):
        c = chunks-1-c
        rows = pl.ds(pl.multiple_of(c*U,U),U)
        s8 = s_ref[0, rows, :]
        g8 = g_ref[0, rows, :]
        bt = bt_ref[0, c]
        go_ref[0, rows, :] += lax.dot_general(g8.astype(BF), h_ref[0, pl.ds(pl.multiple_of(c*U*STATE,U*STATE),U*STATE), :], (((1,),(1,)),((),())), preferred_element_type=F32)
        for k in range(U-1,-1,-1):
            s = jnp.broadcast_to(s8[k:k+1], (STATE,width))
            g = jnp.broadcast_to(g8[k:k+1], (STATE,width))
            cc = jnp.broadcast_to(bt[STATE:2*STATE, k:k+1], (STATE,width))
            h = jnp.exp2(s*r)*(h + g*cc)
        return h
    out_ref[0] = lax.fori_loop(0, chunks, chunk, jnp.zeros((STATE,width),F32))


def scan_end_b(s, g, bt, r, h):
    S,T,C = s.shape
    cb=min(CE,C)
    row=pl.BlockSpec((1,T,cb), lambda i,j:(i,0,j))
    return pl.pallas_call(functools.partial(end_b_kernel, T//U),
        grid=(S,C//cb),
        in_specs=[row,row,pl.BlockSpec((1,T//U,2*STATE,U),lambda i,j:(i,0,0,0)),pl.BlockSpec((STATE,cb),lambda i,j:(0,j)),pl.BlockSpec((1,T*STATE,cb),lambda i,j:(i,0,j))],
        out_specs=[pl.BlockSpec((1,STATE,cb),lambda i,j:(i,0,j)),pl.BlockSpec((1,T,U*STATE),lambda i,j:(i,0,0))],
        out_shape=[jax.ShapeDtypeStruct((S,STATE,C),F32),jax.ShapeDtypeStruct((S,T,U*STATE),F32)],
        compiler_params=pltpu.CompilerParams(vmem_limit_bytes=VM),
        cost_estimate=pl.CostEstimate(flops=COST*S*T*C,bytes_accessed=COST*S*T*C,transcendentals=0),
        name="scan_end_b",
    )(s,g,bt,r,h)


def fwd_kernel(chunks, s_ref, x_ref, bt_ref, l_ref, r_ref, h0_ref, y_ref, h_ref, even, odd):
    r = r_ref[...]
    width = r.shape[1]
    def rows_at(c, size):
        return pl.ds(pl.multiple_of(c*size,size),size)
    def chunk(c, h, mine, other):
        before = jnp.maximum(c-1,0)
        y_ref[0, rows_at(before,U), :] = jnp.dot(l_ref[0, rows_at(before,U), :], other[...], preferred_element_type=F32)
        rows = rows_at(c,U)
        s8 = s_ref[0, rows, :]
        d8 = x_ref[0, rows, :].astype(F32)*s8
        bt = bt_ref[0, c]
        for k in range(U):
            s = jnp.broadcast_to(s8[k:k+1], (STATE,width))
            d = jnp.broadcast_to(d8[k:k+1], (STATE,width))
            b = jnp.broadcast_to(bt[0:STATE, k:k+1], (STATE,width))
            h = jnp.exp2(s*r)*h + d*b
            low = h.astype(BF)
            mine[k*STATE:(k+1)*STATE, :] = low
            h_ref[0, pl.ds(pl.multiple_of(c*U*STATE+k*STATE,STATE),STATE), :] = low
        return h
    def pair(i, h):
        h = chunk(2*i, h, even, odd)
        return chunk(2*i+1, h, odd, even)
    odd[...] = jnp.zeros_like(odd)
    lax.fori_loop(0, chunks//2, pair, h0_ref[0])
    last = pl.ds((chunks-1)*U,U)
    y_ref[0, last, :] = jnp.dot(l_ref[0, last, :], odd[...], preferred_element_type=F32)

def scan_fwd(s, x, bt, l, r, h0):
    S,T,C = s.shape
    cb=min(CB,C)
    row=pl.BlockSpec((1,T,cb), lambda i,j:(i,0,j))
    st=pl.BlockSpec((1,STATE,cb),lambda i,j:(i,0,j))
    return pl.pallas_call(functools.partial(fwd_kernel, T//U),
        grid=(S,C//cb),
        in_specs=[row,row,pl.BlockSpec((1,T//U,2*STATE,U),lambda i,j:(i,0,0,0)),pl.BlockSpec((1,T,U*STATE),lambda i,j:(i,0,0)),pl.BlockSpec((STATE,cb),lambda i,j:(0,j)),st],
        out_specs=[row,pl.BlockSpec((1,T*STATE,cb),lambda i,j:(i,0,j))],
        out_shape=[jax.ShapeDtypeStruct((S,T,C),F32),jax.ShapeDtypeStruct((S,T*STATE,C),BF)],
        scratch_shapes=[pltpu.VMEM((U*STATE,cb),BF)]*2,
        compiler_params=pltpu.CompilerParams(vmem_limit_bytes=VM),
        cost_estimate=pl.CostEstimate(flops=COST*S*T*C,bytes_accessed=COST*S*T*C,transcendentals=0),
        name="scan_fwd",
    )(s,x,bt,l,r,h0)


def bwd_kernel(chunks, s_ref, x_ref, g_ref, bt_ref, l_ref, one_ref, r_ref, k_ref, h0_ref, m0_ref, h_ref,
               pre_ref, base_ref, bias_ref, alog_ref, gi_ref, lam_e, fr_e, lam_o, fr_o):
    r = r_ref[...]
    width = r.shape[1]
    j = pl.program_id(1)
    nt=(((1,),(1,)),((),()))
    def rows_at(c, size):
        return pl.ds(pl.multiple_of(c*size,size),size)
    @pl.when(j==0)
    def _():
        gi_ref[...]=jnp.zeros_like(gi_ref)
    bias_ref[...] = jnp.zeros_like(bias_ref)
    lam_o[...] = jnp.zeros_like(lam_o)
    fr_o[...] = jnp.zeros_like(fr_o)
    def sums(c, lam_s, fr_s, first=None):
        rows = rows_at(c,U)
        s8 = s_ref[0, rows, :]
        x8 = x_ref[0, rows, :].astype(F32)
        d8 = (x8*s8).astype(BF)
        lam_all = lam_s[...]
        pull = jnp.dot(l_ref[0, rows, :], lam_all, preferred_element_type=F32)
        gs = jnp.dot(one_ref[...], fr_s[...], preferred_element_type=F32)
        slope = jnp.where(s8 < 0.03, s8*(1.0-s8*(0.5-s8*(1.0/6.0))), 1.0-jnp.exp(-s8))
        arg = (gs*LN2 + x8*pull)*slope
        pre_ref[0, rows, :] = arg.astype(BF)
        base_ref[0, rows, :] = k_ref[...]*g_ref[0, rows, :] + s8*pull
        part = arg[:8]+arg[8:]
        gi = lax.dot_general(d8, lam_all, nt, preferred_element_type=F32)
        if first is not None:
            gi = jnp.where(first, 0.0, gi)
            part = jnp.where(first, 0.0, part)
        gi_ref[0, rows, :] += gi
        bias_ref[0] += part
    def chunk(c, carry, mine, other, first=None):
        lam_c, alog = carry
        sums(jnp.minimum(c+1,chunks-1), *other, first)
        lam_s, fr_s = mine
        rows = rows_at(c,U)
        s8 = s_ref[0, rows, :]
        g8 = g_ref[0, rows, :]
        bt = bt_ref[0, c]
        for k in range(U-1,-1,-1):
            s = jnp.broadcast_to(s8[k:k+1], (STATE,width))
            g = jnp.broadcast_to(g8[k:k+1], (STATE,width))
            cc = jnp.broadcast_to(bt[STATE:2*STATE, k:k+1], (STATE,width))
            if k:
                hp = h_ref[0, pl.ds(pl.multiple_of(c*U*STATE+(k-1)*STATE,STATE),STATE), :].astype(F32)
            else:
                hp = h_ref[0, pl.ds(pl.multiple_of(jnp.maximum(c*U*STATE-STATE,0),STATE),STATE), :].astype(F32)
                hp = jnp.where(c==0, h0_ref[0], hp)
            lam = lam_c + g*cc
            lam_c = jnp.exp2(s*r)*lam
            fr = lam_c*hp*r
            alog = alog + fr*s
            lam_s[k*STATE:(k+1)*STATE,:] = lam.astype(BF)
            fr_s[k*STATE:(k+1)*STATE,:] = fr.astype(BF)
        return lam_c, alog
    E=(lam_e,fr_e); O=(lam_o,fr_o)
    def pair(i, carry):
        c = chunks-1-2*i
        carry = chunk(c, carry, E, O, i==0)
        return chunk(c-1, carry, O, E)
    _, alog = lax.fori_loop(0, chunks//2, pair, (m0_ref[0], jnp.zeros((STATE,width),F32)))
    sums(0, *O)
    alog_ref[0] = alog

def scan_bwd(s, x, g, bt, l, one, r, k, h0, m0, h):
    S,T,C = s.shape
    cb=min(CB,C)
    row=pl.BlockSpec((1,T,cb), lambda i,j:(i,0,j))
    st=pl.BlockSpec((1,STATE,cb),lambda i,j:(i,0,j))
    lo=pl.BlockSpec((1,T,U*STATE),lambda i,j:(i,0,0))
    return pl.pallas_call(functools.partial(bwd_kernel, T//U),
        grid=(S,C//cb),
        in_specs=[row,row,row,pl.BlockSpec((1,T//U,2*STATE,U),lambda i,j:(i,0,0,0)),lo,pl.BlockSpec((U,U*STATE),lambda i,j:(0,0)),pl.BlockSpec((STATE,cb),lambda i,j:(0,j)),pl.BlockSpec((1,cb),lambda i,j:(0,j)),st,st,pl.BlockSpec((1,T*STATE,cb),lambda i,j:(i,0,j))],
        out_specs=[row,row,pl.BlockSpec((1,8,cb),lambda i,j:(i,0,j)),st,lo],
        out_shape=[jax.ShapeDtypeStruct((S,T,C),BF),jax.ShapeDtypeStruct((S,T,C),F32),jax.ShapeDtypeStruct((S,8,C),F32),jax.ShapeDtypeStruct((S,STATE,C),F32),jax.ShapeDtypeStruct((S,T,U*STATE),F32)],
        scratch_shapes=[pltpu.VMEM((U*STATE,cb),BF)]*4,
        compiler_params=pltpu.CompilerParams(vmem_limit_bytes=VM),
        cost_estimate=pl.CostEstimate(flops=COST*S*T*C,bytes_accessed=COST*S*T*C,transcendentals=0),
        name="scan_bwd",
    )(s,x,g,bt,l,one,r,k,h0,m0,h)


def gelu_and_slope(x):
    root = math.sqrt(2.0 / math.pi)
    square = x * x
    t = jnp.tanh(x * (root + (root * 0.044715) * square))
    half = 0.5 + 0.5 * t
    slope = half + (0.5 * x) * (1.0 - t * t) * (root + (3.0 * root * 0.044715) * square)
    return x * half, slope


def expert_kernel(pieces, tile, second_at, x_ref, f_ref, w_ref, *refs):
    back_ref, value_ref, grad_ref, first_s, second_s, out_s, gin_s, sems = refs[-8:]
    j = pl.program_id(0)
    rows, width = out_s.shape
    hidden = first_s.shape[2]
    copies = [
        pltpu.make_async_copy(f_ref.at[q, pl.ds(0, width), :], first_s.at[q], sems.at[q])
        for q in range(pieces)
    ] + [
        pltpu.make_async_copy(
            w_ref.at[q, pl.ds(second_at, hidden), :], second_s.at[q], sems.at[pieces + q]
        )
        for q in range(pieces)
    ]

    @pl.when(j == 0)
    def _():
        for q in range(pieces):
            copies[q].start()
            copies[q + pieces].start()
        out_s[...] = jnp.zeros_like(out_s)
        gin_s[...] = jnp.zeros_like(gin_s)

    for q in range(pieces):
        @pl.when(j == q)
        def _():
            copies[q].wait()
            copies[q + pieces].wait()

    def mm(a, b, dims):
        return lax.dot_general(a, b, (dims, ((), ())), preferred_element_type=F32)

    first = first_s[j]
    second = second_s[j]
    for i in range(rows // tile):
        at = slice(i * tile, (i + 1) * tile)
        hidden = mm(x_ref[at, :width], first, ((1,), (0,)))
        grad = mm(x_ref[at, width:], second, ((1,), (1,)))
        value, slope = gelu_and_slope(hidden)
        value = value.astype(BF)
        grad = (grad * slope).astype(BF)
        value_ref[at, :] = value
        grad_ref[at, :] = grad
        out = mm(value, second, ((1,), (0,)))
        gin = mm(grad, first, ((1,), (1,)))

        out_s[at, :] += out
        gin_s[at, :] += gin

    @pl.when(j == pieces - 1)
    def _():
        back_ref[:, :width] = out_s[...].astype(BF)
        back_ref[:, width:] = gin_s[...].astype(BF)


def expert_call(x, firsts, seconds, second_at, part, groups, shared):
    rows, width = x.shape[0], x.shape[1] // 2
    pieces, _, quarter = firsts.shape
    tile = math.gcd(rows, 320)
    wide = pl.BlockSpec((rows, quarter), lambda j: (part, j))
    anywhere = pl.BlockSpec(memory_space=pl.ANY)
    whole = pl.BlockSpec((rows, 2 * width), lambda j: (0, 0))
    big = jax.ShapeDtypeStruct((groups * rows, pieces * quarter), BF)
    count = 3
    return pl.pallas_call(
        functools.partial(expert_kernel, pieces, tile, second_at),
        grid=(pieces,),
        in_specs=[whole] + [anywhere] * (2 + len(shared)),
        out_specs=[whole, wide, wide],
        out_shape=[jax.ShapeDtypeStruct((rows, 2 * width), BF), big, big],
        scratch_shapes=[
            pltpu.VMEM((pieces, width, quarter), BF),
            pltpu.VMEM((pieces, quarter, width), BF),
            pltpu.VMEM((rows, width), F32),
            pltpu.VMEM((rows, width), F32),
            pltpu.SemaphoreType.DMA((2 * pieces,)),
        ],
        input_output_aliases={count: 1, count + 1: 2} if shared else {},
        compiler_params=pltpu.CompilerParams(vmem_limit_bytes=EXPERT_VM),
        cost_estimate=pl.CostEstimate(
            flops=COST * rows * width, bytes_accessed=COST * rows * width, transcendentals=0
        ),
        name="expert",
    )(x, firsts, seconds, *shared)


def own_rows(span):
    return jnp.arange(span)[:, None] % U == jnp.arange(U * STATE)[None] // STATE


def state_picker():
    return (jnp.arange(STATE)[:, None] == jnp.arange(U * STATE)[None] % STATE).astype(BF)


def fold(z):
    z = jnp.where(own_rows(z.shape[1]), z, 0).astype(BF)
    return nt(z, state_picker())


def spread_rows(m):
    wide = nn(m.astype(BF), state_picker())
    return jnp.where(own_rows(m.shape[1]), wide, 0).astype(BF)


def bits_of(axis):
    return lax.axis_size(axis).bit_length() - 1


def my_bit(axis, k):
    return (lax.axis_index(axis) >> k) & 1


def swap(x, axis, k):
    count = lax.axis_size(axis)
    return lax.ppermute(x, axis, [(i, i ^ (1 << k)) for i in range(count)])


def shift(x, axis, distance):
    count = lax.axis_size(axis)
    return lax.ppermute(
        x, axis, [(i, i + distance) for i in range(count) if 0 <= i + distance < count]
    )


def joined_pair(x, other, axis, k, place):
    high = my_bit(axis, k) == 1
    return jnp.where(
        high,
        jnp.concatenate([other, x], axis=place),
        jnp.concatenate([x, other], axis=place),
    )


def from_batch(x):
    copies = jnp.broadcast_to(x[None], (lax.axis_size("batch"),) + x.shape)
    return lax.all_to_all(copies, "batch", split_axis=0, concat_axis=0, tiled=True)


def over_seq(x):
    bits = bits_of("seq")
    out = x.reshape(x.shape[:1] + (1,) * bits + x.shape[1:])
    for k in reversed(range(bits)):
        out = joined_pair(out, swap(out, "seq", k), "seq", k, bits - k)
    return out.reshape((-1,) + x.shape[2:])


def over_batch(x):
    got = lax.all_to_all(x.astype(BF), "batch", split_axis=0, concat_axis=0, tiled=True)
    return jnp.sum(got.astype(F32), axis=0)


def halved(x, k, place):
    bit = my_bit("seq", k)
    mine = lax.dynamic_index_in_dim(x, bit, place, True)
    theirs = lax.dynamic_index_in_dim(x, 1 - bit, place, True).astype(BF)
    return mine + swap(theirs, "seq", k).astype(F32)


def sum_over_seq(x):
    bits = bits_of("seq")
    rows = x.shape[0] // (lax.axis_size("batch") << bits)
    out = x.reshape((lax.axis_size("batch"),) + (2,) * bits + (rows,) + x.shape[1:])
    for k in range(bits):
        out = halved(out, k, bits - k)
    return out.reshape((lax.axis_size("batch"), rows) + x.shape[1:])


def totals_of(total):
    levels = []
    for k in range(bits_of("seq")):
        other = swap(total, "seq", k)
        levels.append((total, other))
        total = total + other
    return levels


def prefix(levels, state, rate, backward):
    before = jnp.zeros_like(state)
    before_total = jnp.zeros_like(levels[0][0])
    for k, (total, other_total) in enumerate(levels):
        other = swap(state.astype(BF), "seq", k).astype(F32)
        first = my_bit("seq", k) == (0 if backward else 1)
        before = jnp.where(
            first, before + jnp.exp2(before_total[:, None, :] * rate) * other, before
        )
        before_total = jnp.where(first, before_total + other_total, before_total)
        if k + 1 < len(levels):
            near = jnp.where(first, state, other)
            far = jnp.where(first, other, state)
            near_total = jnp.where(first, total, other_total)
            state = near + jnp.exp2(near_total[:, None, :] * rate) * far
    return before


def after(value, event):
    return lax.optimization_barrier((value, event))[0]


def mm(left, right, dims):
    return lax.dot_general(left, right, (dims, ((), ())), preferred_element_type=F32)


def nn(left, right):
    return mm(left, right, ((left.ndim - 1,), (0,)))


def nt(left, right):
    return mm(left, right, ((left.ndim - 1,), (1,)))


def tn(left, right):
    lead = tuple(range(left.ndim - 1))
    return mm(left, right, (lead, lead))


def silu_slope(v):
    s = jax.nn.sigmoid(v)
    return s * (1.0 + v * (1.0 - s))


def norm_back(grad_norm, x, scale):
    return scale * grad_norm - x * scale**3 * jnp.mean(grad_norm * x, axis=-1, keepdims=True)


def gelu_tanh(v):
    return jax.nn.gelu(v, approximate=True)


def rms(x):
    return lax.rsqrt(jnp.mean(x * x, axis=-1, keepdims=True) + EPSILON)


def side_by_side(x, rows):
    width = x.shape[1]
    x = x.reshape(-1, 2, rows, width)
    return jnp.concatenate([x[:, h].reshape(-1, width) for h in range(2)], axis=1)


def one_below(x, rows):
    width = x.shape[1] // 2
    halves = [x[:, h * width : (h + 1) * width].reshape(-1, rows, width) for h in range(2)]
    return jnp.concatenate(halves, axis=1).reshape(-1, width)


def pad_cols(x, width):
    return jnp.pad(x, ((0, 0), (0, width - x.shape[1])))


def shards(
    tokens,
    cotangent,
    lengths,
    order,
    expert_route,
    slot_index,
    norm_gain,
    in_proj,
    conv_weight,
    conv_bias,
    x_proj,
    dt_proj,
    dt_bias,
    a_log,
    skip_gain,
    out_proj,
    moe_gain,
    router,
    expert_in,
    expert_out,
):
    seqs, span, width = tokens.shape
    batch = lax.axis_size("batch")
    experts = expert_in.shape[0] * batch
    capacity = max(2, (5 * SEQ_MB * span + 4 * experts - 1) // (4 * experts))
    maps = DT_RANK + 2 * STATE
    lo = HALO - (CONV - 1)
    groups = 2
    size = seqs // groups

    rows = in_proj.shape[0]
    chan = jnp.concatenate(
        [
            x_proj,
            dt_proj,
            a_log,
            conv_weight,
            conv_bias[:, None],
            dt_bias[:, None],
            skip_gain[:, None],
        ],
        axis=1,
    )
    feat = jnp.concatenate([norm_gain[:, None], moe_gain[:, None], router], axis=1)
    used = chan.shape[1]
    second_set = jnp.concatenate(
        [
            pad_cols(jnp.concatenate([chan[:rows], feat], axis=1), 192),
            pad_cols(chan[rows:], 192),
        ],
        axis=1,
    )
    second_set = over_seq(second_set[None])
    first_set = from_batch(in_proj[:, :DI])
    second_set = from_batch(after(second_set, first_set)).reshape(-1, second_set.shape[1])
    later = jnp.concatenate([in_proj[:, DI:], side_by_side(out_proj, rows)], axis=1)
    later = after(later, first_set)
    later = lax.all_gather(later, ("batch", "seq"), axis=0, tiled=True)
    w_gate_in = later[:, :DI]
    w_back = one_below(later[:, DI:], rows)
    if expert_in.shape[2] == width:
        both = jnp.concatenate([expert_in[0], expert_out[0]], axis=0)
        both = lax.all_gather(after(both, later), "seq", axis=0, tiled=False)
        expert_weights = both, both, width
    else:
        own = after((expert_in[0], expert_out[0]), later)
        expert_weights = *(lax.all_gather(x, "seq", axis=0, tiled=False) for x in own), 0
    first_set = over_seq(first_set)
    w_conv_in = first_set
    chan = one_below(second_set, rows)
    feat = chan.reshape(-1, 2, rows, 192)[:, 0].reshape(-1, 192)[:, used:]
    gain_one = feat[:, 0].astype(F32)
    gain_two = feat[:, 1].astype(F32)
    router_weight = feat[:, 2 : 2 + experts]
    w_proj = chan[:, :maps]
    at = maps + DT_RANK
    w_step = chan[:, maps:at]
    rate = -jnp.exp(chan[:, at : at + STATE].astype(F32)).T * LOG2E
    at = at + STATE
    taps = chan[:, at : at + CONV].astype(F32).T
    bias_conv = chan[:, at + CONV].astype(F32)
    bias_step = chan[:, at + CONV + 1].astype(F32)
    skip = chan[:, at + CONV + 2].astype(F32)

    halo_all = shift(tokens[:, span - HALO :, :], "seq", 1)
    tail = jnp.arange(HALO)[:, None] >= lo
    halo_all = jnp.where(tail, halo_all, 0)


    positions = lax.axis_index("seq") * span + jnp.arange(span, dtype=jnp.int32)
    row_length = jnp.sum(
        jnp.where(
            order[:, None] == jnp.arange(lengths.shape[0], dtype=jnp.int32)[None, :],
            lengths[None, :],
            0,
        ),
        axis=1,
    )
    keep_all = (positions[None, :] < row_length[:, None]).astype(F32)
    ones = (jnp.arange(U)[:, None] == jnp.arange(U * STATE)[None] // STATE).astype(BF)
    slots = jnp.arange(experts * capacity, dtype=jnp.int32)
    expert_ids = jnp.arange(experts, dtype=jnp.int32)

    class Part:
        pass

    def forward(m, event, second_event):
        p = Part()
        here = slice(m * size, (m + 1) * size)
        own = tokens[here]
        if event is not None:
            own = after(own, event)
        p.block = own.astype(F32)
        p.scale_one = rms(p.block)
        ext = jnp.concatenate([halo_all[here], own], axis=1).astype(F32)
        normed_ext = (ext * rms(ext) * gain_one).astype(BF)
        p.normed = normed_ext[:, HALO:]
        p.conv_ext = nn(normed_ext, w_conv_in)
        p.conv_out = bias_conv + sum(
            p.conv_ext[:, lo + k : lo + k + span, :] * taps[k] for k in range(CONV)
        )
        p.act = jax.nn.silu(p.conv_out).astype(BF)
        projected = nn(p.act, w_proj)
        p.delta = projected[..., :DT_RANK].astype(BF)
        input_map = projected[..., DT_RANK : DT_RANK + STATE]
        output_map = projected[..., DT_RANK + STATE :]
        p.step_arg = nt(p.delta, w_step) + bias_step
        p.step = jax.nn.softplus(p.step_arg)
        p.levels = totals_of(jnp.sum(p.step, axis=1))
        p.both = jnp.swapaxes(
            projected[..., DT_RANK:].reshape(size, span // U, U, 2 * STATE), 2, 3
        )
        p.in_rows = spread_rows(input_map)
        out_rows = spread_rows(output_map)
        end = scan_end_f(p.step, p.act, p.both, rate)
        p.init = prefix(p.levels, end, rate, False)
        if second_event is not None:
            p.init = after(p.init, second_event)
        p.gate_in = nn(p.normed, w_gate_in)
        y, p.states = scan_fwd(p.step, p.act, p.both, out_rows, rate, p.init)
        p.actf = p.act.astype(F32)
        p.mix = y + skip * p.actf
        p.gate_act = jax.nn.silu(p.gate_in)
        p.gated = (p.mix * p.gate_act).astype(BF)
        p.mixed = p.block + nn(p.gated, w_back)
        p.scale_two = rms(p.mixed)
        p.routed = (p.mixed * p.scale_two * gain_two).astype(BF)
        p.probs = jax.nn.softmax(nn(p.routed, router_weight), axis=-1)
        route = expert_route[here]
        slot = slot_index[here]
        kept = slot >= 0
        target = jnp.where(kept, route * capacity + slot, -1)
        p.selector = (target[..., None] == slots).astype(BF)
        p.chosen = jnp.logical_and(route[..., None] == expert_ids, kept[..., None])
        p.gate = jnp.sum(jnp.where(p.chosen, p.probs, 0.0), axis=-1)[..., None]
        p.grad_out = cotangent[here].astype(F32) * keep_all[here][..., None]
        grad_value = (p.gate * p.grad_out).astype(BF)
        packed = jnp.concatenate([p.routed, grad_value], axis=-1)
        send = jnp.einsum("stc,std->scd", p.selector, packed, preferred_element_type=F32)
        send = jnp.swapaxes(send.astype(BF).reshape(size, batch, capacity, 2 * width), 0, 1)
        p.send = send
        p.arrived = lax.all_to_all(send, "batch", split_axis=0, concat_axis=0, tiled=True)
        return p

    def expert(m, shared):
        p = parts[m]
        arrived = after(p.arrived, parts[m - 1].back) if m else p.arrived
        p.rows_in = arrived.reshape(batch * size * capacity, 2 * width)
        p.back, *shared = expert_call(p.rows_in, *expert_weights, m, groups, shared)
        back = p.back.reshape(batch, size, capacity, 2 * width)
        if m:
            back = after(back, parts[m - 1].returned)
        back = lax.all_to_all(back, "batch", split_axis=0, concat_axis=0, tiled=True)
        p.returned = jnp.swapaxes(back, 0, 1).reshape(size, experts * capacity, 2 * width)
        return shared

    def backward_router(p):
        picked = jnp.einsum("stc,scd->std", p.selector, p.returned, preferred_element_type=F32)
        expert_tok = picked[..., :width]
        p.activations = (p.mixed + p.gate * expert_tok).astype(BF)
        grad_gate = jnp.sum(expert_tok * p.grad_out, axis=-1, keepdims=True)
        grad_prob = jnp.where(p.chosen, grad_gate, 0.0)
        grad_logits = (
            p.probs * (grad_prob - jnp.sum(p.probs * grad_prob, axis=-1, keepdims=True))
        ).astype(BF)
        p.g_router = tn(p.routed, grad_logits)
        grad_routed = picked[..., width:] + nt(grad_logits, router_weight)
        p.g_gain_two = jnp.sum(grad_routed * p.mixed * p.scale_two, axis=(0, 1))
        p.grad_mixed = p.grad_out + norm_back(grad_routed * gain_two, p.mixed, p.scale_two)
        p.grad_branch = p.grad_mixed.astype(BF)
        grad_gated = nt(p.grad_branch, w_back)
        p.grad_mix = grad_gated * p.gate_act
        p.grad_gate_in = (grad_gated * p.mix * silu_slope(p.gate_in)).astype(BF)
        p.behind, p.grad_out_map = scan_end_b(p.step, p.grad_mix, p.both, rate, p.states)
        p.after = prefix(p.levels, p.behind, rate, True)
        p.g_skip = jnp.sum(p.grad_mix * p.actf, axis=(0, 1))

    def backward_mixer(p):
        grad_pre, base, bias, g_log, grad_in_map = scan_bwd(
            p.step,
            p.act,
            p.grad_mix,
            p.both,
            p.in_rows,
            ones,
            rate,
            skip[None],
            p.init,
            p.after,
            p.states,
        )
        p.g_log = jnp.sum(g_log, axis=0).T * LN2
        p.g_step_bias = jnp.sum(bias, axis=(0, 1))
        p.g_step = tn(grad_pre, p.delta)
        grad_proj = jnp.concatenate(
            [nn(grad_pre, w_step), fold(grad_in_map), fold(p.grad_out_map)], axis=-1
        ).astype(BF)
        p.g_proj = tn(p.act, grad_proj)
        grad_act = base + nt(grad_proj, w_proj)
        grad_conv = grad_act * silu_slope(p.conv_out)
        p.grad_conv = grad_conv
        rim = shift(grad_conv[:, :HALO, :], "seq", -1)
        longer = lax.optimization_barrier(jnp.concatenate([grad_conv, rim], axis=1))
        p.grad_conv_in = sum(
            longer[:, CONV - 1 - k : CONV - 1 - k + span, :] * taps[k] for k in range(CONV)
        ).astype(BF)

    def backward_taps(p, event):
        grad_conv = after(p.grad_conv, event)
        p.g_conv_bias = jnp.sum(grad_conv, axis=(0, 1))
        p.g_taps = jnp.stack(
            [
                jnp.sum(grad_conv * p.conv_ext[:, lo + k : lo + k + span, :], axis=(0, 1))
                for k in range(CONV)
            ],
            axis=-1,
        )

    def backward_input(p):
        grad_normed = nt(p.grad_conv_in, w_conv_in) + nt(p.grad_gate_in, w_gate_in)
        p.input_grad = p.grad_mixed + norm_back(grad_normed * gain_one, p.block, p.scale_one)

    parts = []
    parts.append(forward(0, None, None))
    for m in range(1, groups):
        parts.append(forward(m, parts[-1].send, parts[-1].arrived))
    shared = ()
    for m in range(groups):
        shared = expert(m, shared)
    values, grad_hidden = shared

    def joined(name):
        return jnp.concatenate([getattr(p, name) for p in parts], axis=0)

    def added(name):
        return functools.reduce(jnp.add, [getattr(p, name) for p in parts])

    def added_products(left, right):
        return functools.reduce(
            jnp.add, [tn(getattr(p, left), getattr(p, right)) for p in parts]
        )

    rows_in = joined("rows_in")
    rows_in, values, grad_hidden = after((rows_in, values, grad_hidden), parts[-1].back)
    grad_second = tn(values, rows_in[:, width:]).astype(BF)
    grad_first = tn(grad_hidden, rows_in[:, :width]).astype(BF)
    products = grad_first, grad_second
    parts[0].returned = after(parts[0].returned, products)
    backward_router(parts[0])
    grad_first, grad_second = after(products, parts[0].grad_mix)
    grad_second = lax.psum_scatter(grad_second, "seq", scatter_dimension=0, tiled=True)
    grad_first = lax.psum_scatter(grad_first, "seq", scatter_dimension=0, tiled=True)
    for p, earlier in zip(parts[1:], parts):
        p.returned = after(p.returned, earlier.grad_mix)
        backward_router(p)
    g_feat = jnp.concatenate([added("g_gain_two")[:, None], added("g_router")], axis=1)
    background = jnp.concatenate(
        [
            added_products("normed", "grad_gate_in").astype(BF),
            side_by_side(added_products("gated", "grad_branch").astype(BF), rows),
            pad_cols(g_feat, 128).astype(BF),
        ],
        axis=1,
    )
    background = lax.psum_scatter(background, ("batch", "seq"), scatter_dimension=0, tiled=True)
    background = background.astype(F32)
    g_gate_half = background[:, :DI]
    g_back = one_below(background[:, DI : 2 * DI], rows)
    g_feat = background[:, 2 * DI :]
    for p in parts:
        backward_mixer(p)
    g_conv_half = added_products("normed", "grad_conv_in")
    for p in parts:
        backward_taps(p, g_conv_half)
    g_chan = jnp.concatenate(
        [
            added("g_proj"),
            added("g_step"),
            added("g_log"),
            added("g_taps"),
            added("g_conv_bias")[:, None],
            added("g_step_bias")[:, None],
            added("g_skip")[:, None],
        ],
        axis=1,
    )
    g_chan = pad_cols(g_chan, 256).reshape(-1, 512)
    g_rest = jnp.concatenate([sum_over_seq(g_conv_half), sum_over_seq(g_chan)], axis=2)
    for p in parts:
        p.grad_conv_in = after(p.grad_conv_in, (g_conv_half, background))
        backward_input(p)
    grad_first, grad_second = after((grad_first, grad_second), g_conv_half)
    grad_first = grad_first.astype(F32).T
    grad_second = grad_second.astype(F32)
    g_rest = after(g_rest, (parts[0].input_grad, grad_first, grad_second))
    g_rest = over_batch(g_rest)
    g_rest = after(g_rest, parts[-1].input_grad)
    g_conv_half = g_rest[:, :DI]
    g_chan = g_rest[:, DI:].reshape(-1, 256)
    g_in = jnp.concatenate([g_conv_half, g_gate_half], axis=1)
    g_gain_one = jnp.sum(g_in * in_proj.astype(F32), axis=1) / norm_gain.astype(F32)
    at = maps + DT_RANK
    return (
        joined("activations"),
        joined("input_grad"),
        g_gain_one,
        g_in,
        g_chan[:, at + STATE : at + STATE + CONV],
        g_chan[:, at + STATE + CONV],
        g_chan[:, :maps],
        g_chan[:, maps:at],
        g_chan[:, at + STATE + CONV + 1],
        g_chan[:, at : at + STATE],
        g_chan[:, at + STATE + CONV + 2],
        g_back,
        g_feat[:, 0],
        g_feat[:, 1 : 1 + experts],
        grad_first[None],
        grad_second[None],
    )


def solution(mesh):
    return jax.shard_map(
        shards,
        mesh=mesh,
        in_specs=(
            P("batch", "seq", None),
            P("batch", "seq", None),
            P(),
            P("batch"),
            P("batch", "seq"),
            P("batch", "seq"),
            P(("batch", "seq")),
            P(("batch", "seq"), None),
            P(("batch", "seq"), None),
            P(("batch", "seq")),
            P(("batch", "seq"), None),
            P(("batch", "seq"), None),
            P(("batch", "seq")),
            P(("batch", "seq"), None),
            P(("batch", "seq")),
            P(("batch", "seq"), None),
            P(("batch", "seq")),
            P(("batch", "seq"), None),
            P("batch", None, "seq"),
            P("batch", "seq", None),
        ),
        out_specs=(
            P("batch", "seq", None),
            P("batch", "seq", None),
            P(("batch", "seq")),
            P(("batch", "seq"), None),
            P(("batch", "seq"), None),
            P(("batch", "seq")),
            P(("batch", "seq"), None),
            P(("batch", "seq"), None),
            P(("batch", "seq")),
            P(("batch", "seq"), None),
            P(("batch", "seq")),
            P(("batch", "seq"), None),
            P(("batch", "seq")),
            P(("batch", "seq"), None),
            P("batch", None, "seq"),
            P("batch", "seq", None),
        ),
        check_vma=False,
    )
```

```python
import functools
import math

import jax
import jax.numpy as jnp
from jax import lax
from jax.experimental import pallas as pl
from jax.experimental.pallas import tpu as pltpu
from jax.sharding import PartitionSpec as P

DI = 1536
STATE = 16
DT_RANK = 48
CONV = 4
SEQ_MB = 1
EPSILON = 1e-05
F32 = jnp.float32
BF = jnp.bfloat16
U = 16
CB = 512
CE = 1536
VM = 48 << 20
EXPERT_VM = 48 << 20
COST = 1
LOG2E = 1.0 / math.log(2.0)
LN2 = math.log(2.0)
HALO = 8


def end_f_kernel(chunks, s_ref, x_ref, bt_ref, r_ref, h_ref):
    r = r_ref[...]
    width = r.shape[1]
    def chunk(c, h):
        rows = pl.ds(pl.multiple_of(c*U,U),U)
        s8 = s_ref[0, rows, :]
        d8 = x_ref[0, rows, :].astype(F32)*s8
        bt = bt_ref[0, c]
        for k in range(U):
            s = jnp.broadcast_to(s8[k:k+1], (STATE,width))
            d = jnp.broadcast_to(d8[k:k+1], (STATE,width))
            b = jnp.broadcast_to(bt[0:STATE, k:k+1], (STATE,width))
            h = jnp.exp2(s*r)*h + d*b
        return h
    h_ref[0] = lax.fori_loop(0, chunks, chunk, jnp.zeros((STATE,width),F32))


def scan_end_f(s, x, bt, r):
    S,T,C = s.shape
    cb=min(CE,C)
    row=pl.BlockSpec((1,T,cb), lambda i,j:(i,0,j))
    return pl.pallas_call(functools.partial(end_f_kernel, T//U),
        grid=(S,C//cb),
        in_specs=[row,row,pl.BlockSpec((1,T//U,2*STATE,U),lambda i,j:(i,0,0,0)),pl.BlockSpec((STATE,cb),lambda i,j:(0,j))],
        out_specs=pl.BlockSpec((1,STATE,cb),lambda i,j:(i,0,j)),
        out_shape=jax.ShapeDtypeStruct((S,STATE,C),F32),
        compiler_params=pltpu.CompilerParams(vmem_limit_bytes=VM),
        cost_estimate=pl.CostEstimate(flops=COST*S*T*C,bytes_accessed=COST*S*T*C,transcendentals=0),
        name="scan_end_f",
    )(s,x,bt,r)


def end_b_kernel(chunks, s_ref, g_ref, bt_ref, r_ref, h_ref, out_ref, go_ref):
    r = r_ref[...]
    width = r.shape[1]
    @pl.when(pl.program_id(1)==0)
    def _():
        go_ref[...]=jnp.zeros_like(go_ref)
    def chunk(c, h):
        c = chunks-1-c
        rows = pl.ds(pl.multiple_of(c*U,U),U)
        s8 = s_ref[0, rows, :]
        g8 = g_ref[0, rows, :]
        bt = bt_ref[0, c]
        go_ref[0, rows, :] += lax.dot_general(g8.astype(BF), h_ref[0, pl.ds(pl.multiple_of(c*U*STATE,U*STATE),U*STATE), :], (((1,),(1,)),((),())), preferred_element_type=F32)
        for k in range(U-1,-1,-1):
            s = jnp.broadcast_to(s8[k:k+1], (STATE,width))
            g = jnp.broadcast_to(g8[k:k+1], (STATE,width))
            cc = jnp.broadcast_to(bt[STATE:2*STATE, k:k+1], (STATE,width))
            h = jnp.exp2(s*r)*(h + g*cc)
        return h
    out_ref[0] = lax.fori_loop(0, chunks, chunk, jnp.zeros((STATE,width),F32))


def scan_end_b(s, g, bt, r, h):
    S,T,C = s.shape
    cb=min(CE,C)
    row=pl.BlockSpec((1,T,cb), lambda i,j:(i,0,j))
    return pl.pallas_call(functools.partial(end_b_kernel, T//U),
        grid=(S,C//cb),
        in_specs=[row,row,pl.BlockSpec((1,T//U,2*STATE,U),lambda i,j:(i,0,0,0)),pl.BlockSpec((STATE,cb),lambda i,j:(0,j)),pl.BlockSpec((1,T*STATE,cb),lambda i,j:(i,0,j))],
        out_specs=[pl.BlockSpec((1,STATE,cb),lambda i,j:(i,0,j)),pl.BlockSpec((1,T,U*STATE),lambda i,j:(i,0,0))],
        out_shape=[jax.ShapeDtypeStruct((S,STATE,C),F32),jax.ShapeDtypeStruct((S,T,U*STATE),F32)],
        compiler_params=pltpu.CompilerParams(vmem_limit_bytes=VM),
        cost_estimate=pl.CostEstimate(flops=COST*S*T*C,bytes_accessed=COST*S*T*C,transcendentals=0),
        name="scan_end_b",
    )(s,g,bt,r,h)


def fwd_kernel(chunks, s_ref, x_ref, bt_ref, l_ref, r_ref, h0_ref, y_ref, h_ref, even, odd):
    r = r_ref[...]
    width = r.shape[1]
    def rows_at(c, size):
        return pl.ds(pl.multiple_of(c*size,size),size)
    def chunk(c, h, mine, other):
        before = jnp.maximum(c-1,0)
        y_ref[0, rows_at(before,U), :] = jnp.dot(l_ref[0, rows_at(before,U), :], other[...], preferred_element_type=F32)
        rows = rows_at(c,U)
        s8 = s_ref[0, rows, :]
        d8 = x_ref[0, rows, :].astype(F32)*s8
        bt = bt_ref[0, c]
        for k in range(U):
            s = jnp.broadcast_to(s8[k:k+1], (STATE,width))
            d = jnp.broadcast_to(d8[k:k+1], (STATE,width))
            b = jnp.broadcast_to(bt[0:STATE, k:k+1], (STATE,width))
            h = jnp.exp2(s*r)*h + d*b
            low = h.astype(BF)
            mine[k*STATE:(k+1)*STATE, :] = low
            h_ref[0, pl.ds(pl.multiple_of(c*U*STATE+k*STATE,STATE),STATE), :] = low
        return h
    def pair(i, h):
        h = chunk(2*i, h, even, odd)
        return chunk(2*i+1, h, odd, even)
    odd[...] = jnp.zeros_like(odd)
    lax.fori_loop(0, chunks//2, pair, h0_ref[0])
    last = pl.ds((chunks-1)*U,U)
    y_ref[0, last, :] = jnp.dot(l_ref[0, last, :], odd[...], preferred_element_type=F32)

def scan_fwd(s, x, bt, l, r, h0):
    S,T,C = s.shape
    cb=min(CB,C)
    row=pl.BlockSpec((1,T,cb), lambda i,j:(i,0,j))
    st=pl.BlockSpec((1,STATE,cb),lambda i,j:(i,0,j))
    return pl.pallas_call(functools.partial(fwd_kernel, T//U),
        grid=(S,C//cb),
        in_specs=[row,row,pl.BlockSpec((1,T//U,2*STATE,U),lambda i,j:(i,0,0,0)),pl.BlockSpec((1,T,U*STATE),lambda i,j:(i,0,0)),pl.BlockSpec((STATE,cb),lambda i,j:(0,j)),st],
        out_specs=[row,pl.BlockSpec((1,T*STATE,cb),lambda i,j:(i,0,j))],
        out_shape=[jax.ShapeDtypeStruct((S,T,C),F32),jax.ShapeDtypeStruct((S,T*STATE,C),BF)],
        scratch_shapes=[pltpu.VMEM((U*STATE,cb),BF)]*2,
        compiler_params=pltpu.CompilerParams(vmem_limit_bytes=VM),
        cost_estimate=pl.CostEstimate(flops=COST*S*T*C,bytes_accessed=COST*S*T*C,transcendentals=0),
        name="scan_fwd",
    )(s,x,bt,l,r,h0)


def bwd_kernel(chunks, s_ref, x_ref, g_ref, bt_ref, l_ref, one_ref, r_ref, k_ref, h0_ref, m0_ref, h_ref,
               pre_ref, base_ref, bias_ref, alog_ref, gi_ref, lam_e, fr_e, lam_o, fr_o):
    r = r_ref[...]
    width = r.shape[1]
    j = pl.program_id(1)
    nt=(((1,),(1,)),((),()))
    def rows_at(c, size):
        return pl.ds(pl.multiple_of(c*size,size),size)
    @pl.when(j==0)
    def _():
        gi_ref[...]=jnp.zeros_like(gi_ref)
    bias_ref[...] = jnp.zeros_like(bias_ref)
    lam_o[...] = jnp.zeros_like(lam_o)
    fr_o[...] = jnp.zeros_like(fr_o)
    def sums(c, lam_s, fr_s, first=None):
        rows = rows_at(c,U)
        s8 = s_ref[0, rows, :]
        x8 = x_ref[0, rows, :].astype(F32)
        d8 = (x8*s8).astype(BF)
        lam_all = lam_s[...]
        pull = jnp.dot(l_ref[0, rows, :], lam_all, preferred_element_type=F32)
        gs = jnp.dot(one_ref[...], fr_s[...], preferred_element_type=F32)
        slope = jnp.where(s8 < 0.03, s8*(1.0-s8*(0.5-s8*(1.0/6.0))), 1.0-jnp.exp(-s8))
        arg = (gs*LN2 + x8*pull)*slope
        pre_ref[0, rows, :] = arg.astype(BF)
        base_ref[0, rows, :] = k_ref[...]*g_ref[0, rows, :] + s8*pull
        part = arg[:8]+arg[8:]
        gi = lax.dot_general(d8, lam_all, nt, preferred_element_type=F32)
        if first is not None:
            gi = jnp.where(first, 0.0, gi)
            part = jnp.where(first, 0.0, part)
        gi_ref[0, rows, :] += gi
        bias_ref[0] += part
    def chunk(c, carry, mine, other, first=None):
        lam_c, alog = carry
        sums(jnp.minimum(c+1,chunks-1), *other, first)
        lam_s, fr_s = mine
        rows = rows_at(c,U)
        s8 = s_ref[0, rows, :]
        g8 = g_ref[0, rows, :]
        bt = bt_ref[0, c]
        for k in range(U-1,-1,-1):
            s = jnp.broadcast_to(s8[k:k+1], (STATE,width))
            g = jnp.broadcast_to(g8[k:k+1], (STATE,width))
            cc = jnp.broadcast_to(bt[STATE:2*STATE, k:k+1], (STATE,width))
            if k:
                hp = h_ref[0, pl.ds(pl.multiple_of(c*U*STATE+(k-1)*STATE,STATE),STATE), :].astype(F32)
            else:
                hp = h_ref[0, pl.ds(pl.multiple_of(jnp.maximum(c*U*STATE-STATE,0),STATE),STATE), :].astype(F32)
                hp = jnp.where(c==0, h0_ref[0], hp)
            lam = lam_c + g*cc
            lam_c = jnp.exp2(s*r)*lam
            fr = lam_c*hp*r
            alog = alog + fr*s
            lam_s[k*STATE:(k+1)*STATE,:] = lam.astype(BF)
            fr_s[k*STATE:(k+1)*STATE,:] = fr.astype(BF)
        return lam_c, alog
    E=(lam_e,fr_e); O=(lam_o,fr_o)
    def pair(i, carry):
        c = chunks-1-2*i
        carry = chunk(c, carry, E, O, i==0)
        return chunk(c-1, carry, O, E)
    _, alog = lax.fori_loop(0, chunks//2, pair, (m0_ref[0], jnp.zeros((STATE,width),F32)))
    sums(0, *O)
    alog_ref[0] = alog

def scan_bwd(s, x, g, bt, l, one, r, k, h0, m0, h):
    S,T,C = s.shape
    cb=min(CB,C)
    row=pl.BlockSpec((1,T,cb), lambda i,j:(i,0,j))
    st=pl.BlockSpec((1,STATE,cb),lambda i,j:(i,0,j))
    lo=pl.BlockSpec((1,T,U*STATE),lambda i,j:(i,0,0))
    return pl.pallas_call(functools.partial(bwd_kernel, T//U),
        grid=(S,C//cb),
        in_specs=[row,row,row,pl.BlockSpec((1,T//U,2*STATE,U),lambda i,j:(i,0,0,0)),lo,pl.BlockSpec((U,U*STATE),lambda i,j:(0,0)),pl.BlockSpec((STATE,cb),lambda i,j:(0,j)),pl.BlockSpec((1,cb),lambda i,j:(0,j)),st,st,pl.BlockSpec((1,T*STATE,cb),lambda i,j:(i,0,j))],
        out_specs=[row,row,pl.BlockSpec((1,8,cb),lambda i,j:(i,0,j)),st,lo],
        out_shape=[jax.ShapeDtypeStruct((S,T,C),BF),jax.ShapeDtypeStruct((S,T,C),F32),jax.ShapeDtypeStruct((S,8,C),F32),jax.ShapeDtypeStruct((S,STATE,C),F32),jax.ShapeDtypeStruct((S,T,U*STATE),F32)],
        scratch_shapes=[pltpu.VMEM((U*STATE,cb),BF)]*4,
        compiler_params=pltpu.CompilerParams(vmem_limit_bytes=VM),
        cost_estimate=pl.CostEstimate(flops=COST*S*T*C,bytes_accessed=COST*S*T*C,transcendentals=0),
        name="scan_bwd",
    )(s,x,g,bt,l,one,r,k,h0,m0,h)


def gelu_and_slope(x):
    root = math.sqrt(2.0 / math.pi)
    square = x * x
    t = jnp.tanh(x * (root + (root * 0.044715) * square))
    half = 0.5 + 0.5 * t
    slope = half + (0.5 * x) * (1.0 - t * t) * (root + (3.0 * root * 0.044715) * square)
    return x * half, slope


def expert_kernel(pieces, tile, second_at, x_ref, f_ref, w_ref, *refs):
    back_ref, value_ref, grad_ref, first_s, second_s, out_s, gin_s, sems = refs[-8:]
    j = pl.program_id(0)
    rows, width = out_s.shape
    hidden = first_s.shape[2]
    copies = [
        pltpu.make_async_copy(f_ref.at[q, pl.ds(0, width), :], first_s.at[q], sems.at[q])
        for q in range(pieces)
    ] + [
        pltpu.make_async_copy(
            w_ref.at[q, pl.ds(second_at, hidden), :], second_s.at[q], sems.at[pieces + q]
        )
        for q in range(pieces)
    ]

    @pl.when(j == 0)
    def _():
        for q in range(pieces):
            copies[q].start()
            copies[q + pieces].start()
        out_s[...] = jnp.zeros_like(out_s)
        gin_s[...] = jnp.zeros_like(gin_s)

    for q in range(pieces):
        @pl.when(j == q)
        def _():
            copies[q].wait()
            copies[q + pieces].wait()

    def mm(a, b, dims):
        return lax.dot_general(a, b, (dims, ((), ())), preferred_element_type=F32)

    first = first_s[j]
    second = second_s[j]
    for i in range(rows // tile):
        at = slice(i * tile, (i + 1) * tile)
        hidden = mm(x_ref[at, :width], first, ((1,), (0,)))
        grad = mm(x_ref[at, width:], second, ((1,), (1,)))
        value, slope = gelu_and_slope(hidden)
        value = value.astype(BF)
        grad = (grad * slope).astype(BF)
        value_ref[at, :] = value
        grad_ref[at, :] = grad
        out = mm(value, second, ((1,), (0,)))
        gin = mm(grad, first, ((1,), (1,)))

        out_s[at, :] += out
        gin_s[at, :] += gin

    @pl.when(j == pieces - 1)
    def _():
        back_ref[:, :width] = out_s[...].astype(BF)
        back_ref[:, width:] = gin_s[...].astype(BF)


def expert_call(x, firsts, seconds, second_at, part, groups, shared):
    rows, width = x.shape[0], x.shape[1] // 2
    pieces, _, quarter = firsts.shape
    tile = math.gcd(rows, 320)
    wide = pl.BlockSpec((rows, quarter), lambda j: (part, j))
    anywhere = pl.BlockSpec(memory_space=pl.ANY)
    whole = pl.BlockSpec((rows, 2 * width), lambda j: (0, 0))
    big = jax.ShapeDtypeStruct((groups * rows, pieces * quarter), BF)
    count = 3
    return pl.pallas_call(
        functools.partial(expert_kernel, pieces, tile, second_at),
        grid=(pieces,),
        in_specs=[whole] + [anywhere] * (2 + len(shared)),
        out_specs=[whole, wide, wide],
        out_shape=[jax.ShapeDtypeStruct((rows, 2 * width), BF), big, big],
        scratch_shapes=[
            pltpu.VMEM((pieces, width, quarter), BF),
            pltpu.VMEM((pieces, quarter, width), BF),
            pltpu.VMEM((rows, width), F32),
            pltpu.VMEM((rows, width), F32),
            pltpu.SemaphoreType.DMA((2 * pieces,)),
        ],
        input_output_aliases={count: 1, count + 1: 2} if shared else {},
        compiler_params=pltpu.CompilerParams(vmem_limit_bytes=EXPERT_VM),
        cost_estimate=pl.CostEstimate(
            flops=COST * rows * width, bytes_accessed=COST * rows * width, transcendentals=0
        ),
        name="expert",
    )(x, firsts, seconds, *shared)


def own_rows(span):
    return jnp.arange(span)[:, None] % U == jnp.arange(U * STATE)[None] // STATE


def state_picker():
    return (jnp.arange(STATE)[:, None] == jnp.arange(U * STATE)[None] % STATE).astype(BF)


def fold(z):
    z = jnp.where(own_rows(z.shape[1]), z, 0).astype(BF)
    return nt(z, state_picker())


def spread_rows(m):
    wide = nn(m.astype(BF), state_picker())
    return jnp.where(own_rows(m.shape[1]), wide, 0).astype(BF)


def bits_of(axis):
    return lax.axis_size(axis).bit_length() - 1


def my_bit(axis, k):
    return (lax.axis_index(axis) >> k) & 1


def swap(x, axis, k):
    count = lax.axis_size(axis)
    return lax.ppermute(x, axis, [(i, i ^ (1 << k)) for i in range(count)])


def shift(x, axis, distance):
    count = lax.axis_size(axis)
    return lax.ppermute(
        x, axis, [(i, i + distance) for i in range(count) if 0 <= i + distance < count]
    )


def joined_pair(x, other, axis, k, place):
    high = my_bit(axis, k) == 1
    return jnp.where(
        high,
        jnp.concatenate([other, x], axis=place),
        jnp.concatenate([x, other], axis=place),
    )


def from_batch(x):
    copies = jnp.broadcast_to(x[None], (lax.axis_size("batch"),) + x.shape)
    return lax.all_to_all(copies, "batch", split_axis=0, concat_axis=0, tiled=True)


def over_seq(x):
    bits = bits_of("seq")
    out = x.reshape(x.shape[:1] + (1,) * bits + x.shape[1:])
    for k in reversed(range(bits)):
        out = joined_pair(out, swap(out, "seq", k), "seq", k, bits - k)
    return out.reshape((-1,) + x.shape[2:])


def over_batch(x):
    got = lax.all_to_all(x.astype(BF), "batch", split_axis=0, concat_axis=0, tiled=True)
    return jnp.sum(got.astype(F32), axis=0)


def halved(x, k, place):
    bit = my_bit("seq", k)
    mine = lax.dynamic_index_in_dim(x, bit, place, True)
    theirs = lax.dynamic_index_in_dim(x, 1 - bit, place, True).astype(BF)
    return mine + swap(theirs, "seq", k).astype(F32)


def sum_over_seq(x):
    bits = bits_of("seq")
    rows = x.shape[0] // (lax.axis_size("batch") << bits)
    out = x.reshape((lax.axis_size("batch"),) + (2,) * bits + (rows,) + x.shape[1:])
    for k in range(bits):
        out = halved(out, k, bits - k)
    return out.reshape((lax.axis_size("batch"), rows) + x.shape[1:])


def totals_of(total):
    levels = []
    for k in range(bits_of("seq")):
        other = swap(total, "seq", k)
        levels.append((total, other))
        total = total + other
    return levels


def prefix(levels, state, rate, backward):
    before = jnp.zeros_like(state)
    before_total = jnp.zeros_like(levels[0][0])
    for k, (total, other_total) in enumerate(levels):
        other = swap(state.astype(BF), "seq", k).astype(F32)
        first = my_bit("seq", k) == (0 if backward else 1)
        before = jnp.where(
            first, before + jnp.exp2(before_total[:, None, :] * rate) * other, before
        )
        before_total = jnp.where(first, before_total + other_total, before_total)
        if k + 1 < len(levels):
            near = jnp.where(first, state, other)
            far = jnp.where(first, other, state)
            near_total = jnp.where(first, total, other_total)
            state = near + jnp.exp2(near_total[:, None, :] * rate) * far
    return before


def after(value, event):
    return lax.optimization_barrier((value, event))[0]


def mm(left, right, dims):
    return lax.dot_general(left, right, (dims, ((), ())), preferred_element_type=F32)


def nn(left, right):
    return mm(left, right, ((left.ndim - 1,), (0,)))


def nt(left, right):
    return mm(left, right, ((left.ndim - 1,), (1,)))


def tn(left, right):
    lead = tuple(range(left.ndim - 1))
    return mm(left, right, (lead, lead))


def silu_slope(v):
    s = jax.nn.sigmoid(v)
    return s * (1.0 + v * (1.0 - s))


def norm_back(grad_norm, x, scale):
    return scale * grad_norm - x * scale**3 * jnp.mean(grad_norm * x, axis=-1, keepdims=True)


def gelu_tanh(v):
    return jax.nn.gelu(v, approximate=True)


def rms(x):
    return lax.rsqrt(jnp.mean(x * x, axis=-1, keepdims=True) + EPSILON)


def side_by_side(x, rows):
    width = x.shape[1]
    x = x.reshape(-1, 2, rows, width)
    return jnp.concatenate([x[:, h].reshape(-1, width) for h in range(2)], axis=1)


def one_below(x, rows):
    width = x.shape[1] // 2
    halves = [x[:, h * width : (h + 1) * width].reshape(-1, rows, width) for h in range(2)]
    return jnp.concatenate(halves, axis=1).reshape(-1, width)


def pad_cols(x, width):
    return jnp.pad(x, ((0, 0), (0, width - x.shape[1])))


def shards(
    tokens,
    cotangent,
    lengths,
    order,
    expert_route,
    slot_index,
    norm_gain,
    in_proj,
    conv_weight,
    conv_bias,
    x_proj,
    dt_proj,
    dt_bias,
    a_log,
    skip_gain,
    out_proj,
    moe_gain,
    router,
    expert_in,
    expert_out,
):
    seqs, span, width = tokens.shape
    batch = lax.axis_size("batch")
    experts = expert_in.shape[0] * batch
    capacity = max(2, (5 * SEQ_MB * span + 4 * experts - 1) // (4 * experts))
    maps = DT_RANK + 2 * STATE
    lo = HALO - (CONV - 1)
    groups = 2
    size = seqs // groups

    rows = in_proj.shape[0]
    chan = jnp.concatenate(
        [
            x_proj,
            dt_proj,
            a_log,
            conv_weight,
            conv_bias[:, None],
            dt_bias[:, None],
            skip_gain[:, None],
        ],
        axis=1,
    )
    feat = jnp.concatenate([norm_gain[:, None], moe_gain[:, None], router], axis=1)
    used = chan.shape[1]
    second_set = jnp.concatenate(
        [
            pad_cols(jnp.concatenate([chan[:rows], feat], axis=1), 192),
            pad_cols(chan[rows:], 192),
        ],
        axis=1,
    )
    second_set = over_seq(second_set[None])
    first_set = from_batch(in_proj[:, :DI])
    second_set = from_batch(after(second_set, first_set)).reshape(-1, second_set.shape[1])
    later = jnp.concatenate([in_proj[:, DI:], side_by_side(out_proj, rows)], axis=1)
    later = after(later, first_set)
    later = lax.all_gather(later, ("batch", "seq"), axis=0, tiled=True)
    w_gate_in = later[:, :DI]
    w_back = one_below(later[:, DI:], rows)
    if expert_in.shape[2] == width:
        both = jnp.concatenate([expert_in[0], expert_out[0]], axis=0)
        both = lax.all_gather(after(both, later), "seq", axis=0, tiled=False)
        expert_weights = both, both, width
    else:
        own = after((expert_in[0], expert_out[0]), later)
        expert_weights = *(lax.all_gather(x, "seq", axis=0, tiled=False) for x in own), 0
    first_set = over_seq(first_set)
    w_conv_in = first_set
    chan = one_below(second_set, rows)
    feat = chan.reshape(-1, 2, rows, 192)[:, 0].reshape(-1, 192)[:, used:]
    gain_one = feat[:, 0].astype(F32)
    gain_two = feat[:, 1].astype(F32)
    router_weight = feat[:, 2 : 2 + experts]
    w_proj = chan[:, :maps]
    at = maps + DT_RANK
    w_step = chan[:, maps:at]
    rate = -jnp.exp(chan[:, at : at + STATE].astype(F32)).T * LOG2E
    at = at + STATE
    taps = chan[:, at : at + CONV].astype(F32).T
    bias_conv = chan[:, at + CONV].astype(F32)
    bias_step = chan[:, at + CONV + 1].astype(F32)
    skip = chan[:, at + CONV + 2].astype(F32)

    halo_all = shift(tokens[:, span - HALO :, :], "seq", 1)
    tail = jnp.arange(HALO)[:, None] >= lo
    halo_all = jnp.where(tail, halo_all, 0)


    positions = lax.axis_index("seq") * span + jnp.arange(span, dtype=jnp.int32)
    row_length = jnp.sum(
        jnp.where(
            order[:, None] == jnp.arange(lengths.shape[0], dtype=jnp.int32)[None, :],
            lengths[None, :],
            0,
        ),
        axis=1,
    )
    keep_all = (positions[None, :] < row_length[:, None]).astype(F32)
    ones = (jnp.arange(U)[:, None] == jnp.arange(U * STATE)[None] // STATE).astype(BF)
    slots = jnp.arange(experts * capacity, dtype=jnp.int32)
    expert_ids = jnp.arange(experts, dtype=jnp.int32)

    class Part:
        pass

    def forward(m, event, second_event):
        p = Part()
        here = slice(m * size, (m + 1) * size)
        own = tokens[here]
        if event is not None:
            own = after(own, event)
        p.block = own.astype(F32)
        p.scale_one = rms(p.block)
        ext = jnp.concatenate([halo_all[here], own], axis=1).astype(F32)
        normed_ext = (ext * rms(ext) * gain_one).astype(BF)
        p.normed = normed_ext[:, HALO:]
        p.conv_ext = nn(normed_ext, w_conv_in)
        p.conv_out = bias_conv + sum(
            p.conv_ext[:, lo + k : lo + k + span, :] * taps[k] for k in range(CONV)
        )
        p.act = jax.nn.silu(p.conv_out).astype(BF)
        projected = nn(p.act, w_proj)
        p.delta = projected[..., :DT_RANK].astype(BF)
        input_map = projected[..., DT_RANK : DT_RANK + STATE]
        output_map = projected[..., DT_RANK + STATE :]
        p.step_arg = nt(p.delta, w_step) + bias_step
        p.step = jax.nn.softplus(p.step_arg)
        p.levels = totals_of(jnp.sum(p.step, axis=1))
        p.both = jnp.swapaxes(
            projected[..., DT_RANK:].reshape(size, span // U, U, 2 * STATE), 2, 3
        )
        p.in_rows = spread_rows(input_map)
        out_rows = spread_rows(output_map)
        end = scan_end_f(p.step, p.act, p.both, rate)
        p.init = prefix(p.levels, end, rate, False)
        if second_event is not None:
            p.init = after(p.init, second_event)
        p.gate_in = nn(p.normed, w_gate_in)
        y, p.states = scan_fwd(p.step, p.act, p.both, out_rows, rate, p.init)
        p.actf = p.act.astype(F32)
        p.mix = y + skip * p.actf
        p.gate_act = jax.nn.silu(p.gate_in)
        p.gated = (p.mix * p.gate_act).astype(BF)
        p.mixed = p.block + nn(p.gated, w_back)
        p.scale_two = rms(p.mixed)
        p.routed = (p.mixed * p.scale_two * gain_two).astype(BF)
        p.probs = jax.nn.softmax(nn(p.routed, router_weight), axis=-1)
        route = expert_route[here]
        slot = slot_index[here]
        kept = slot >= 0
        target = jnp.where(kept, route * capacity + slot, -1)
        p.selector = (target[..., None] == slots).astype(BF)
        p.chosen = jnp.logical_and(route[..., None] == expert_ids, kept[..., None])
        p.gate = jnp.sum(jnp.where(p.chosen, p.probs, 0.0), axis=-1)[..., None]
        p.grad_out = cotangent[here].astype(F32) * keep_all[here][..., None]
        grad_value = (p.gate * p.grad_out).astype(BF)
        packed = jnp.concatenate([p.routed, grad_value], axis=-1)
        send = jnp.einsum("stc,std->scd", p.selector, packed, preferred_element_type=F32)
        send = jnp.swapaxes(send.astype(BF).reshape(size, batch, capacity, 2 * width), 0, 1)
        p.send = send
        p.arrived = lax.all_to_all(send, "batch", split_axis=0, concat_axis=0, tiled=True)
        return p

    def expert(m, shared):
        p = parts[m]
        arrived = after(p.arrived, parts[m - 1].back) if m else p.arrived
        p.rows_in = arrived.reshape(batch * size * capacity, 2 * width)
        p.back, *shared = expert_call(p.rows_in, *expert_weights, m, groups, shared)
        back = p.back.reshape(batch, size, capacity, 2 * width)
        if m:
            back = after(back, parts[m - 1].returned)
        back = lax.all_to_all(back, "batch", split_axis=0, concat_axis=0, tiled=True)
        p.returned = jnp.swapaxes(back, 0, 1).reshape(size, experts * capacity, 2 * width)
        return shared

    def backward_router(p):
        picked = jnp.einsum("stc,scd->std", p.selector, p.returned, preferred_element_type=F32)
        expert_tok = picked[..., :width]
        p.activations = (p.mixed + p.gate * expert_tok).astype(BF)
        grad_gate = jnp.sum(expert_tok * p.grad_out, axis=-1, keepdims=True)
        grad_prob = jnp.where(p.chosen, grad_gate, 0.0)
        grad_logits = (
            p.probs * (grad_prob - jnp.sum(p.probs * grad_prob, axis=-1, keepdims=True))
        ).astype(BF)
        p.g_router = tn(p.routed, grad_logits)
        grad_routed = picked[..., width:] + nt(grad_logits, router_weight)
        p.g_gain_two = jnp.sum(grad_routed * p.mixed * p.scale_two, axis=(0, 1))
        p.grad_mixed = p.grad_out + norm_back(grad_routed * gain_two, p.mixed, p.scale_two)
        p.grad_branch = p.grad_mixed.astype(BF)
        grad_gated = nt(p.grad_branch, w_back)
        p.grad_mix = grad_gated * p.gate_act
        p.grad_gate_in = (grad_gated * p.mix * silu_slope(p.gate_in)).astype(BF)
        p.behind, p.grad_out_map = scan_end_b(p.step, p.grad_mix, p.both, rate, p.states)
        p.after = prefix(p.levels, p.behind, rate, True)
        p.g_skip = jnp.sum(p.grad_mix * p.actf, axis=(0, 1))

    def backward_mixer(p):
        grad_pre, base, bias, g_log, grad_in_map = scan_bwd(
            p.step,
            p.act,
            p.grad_mix,
            p.both,
            p.in_rows,
            ones,
            rate,
            skip[None],
            p.init,
            p.after,
            p.states,
        )
        p.g_log = jnp.sum(g_log, axis=0).T * LN2
        p.g_step_bias = jnp.sum(bias, axis=(0, 1))
        p.g_step = tn(grad_pre, p.delta)
        grad_proj = jnp.concatenate(
            [nn(grad_pre, w_step), fold(grad_in_map), fold(p.grad_out_map)], axis=-1
        ).astype(BF)
        p.g_proj = tn(p.act, grad_proj)
        grad_act = base + nt(grad_proj, w_proj)
        grad_conv = grad_act * silu_slope(p.conv_out)
        p.grad_conv = grad_conv
        rim = shift(grad_conv[:, :HALO, :], "seq", -1)
        longer = lax.optimization_barrier(jnp.concatenate([grad_conv, rim], axis=1))
        p.grad_conv_in = sum(
            longer[:, CONV - 1 - k : CONV - 1 - k + span, :] * taps[k] for k in range(CONV)
        ).astype(BF)

    def backward_taps(p, event):
        grad_conv = after(p.grad_conv, event)
        p.g_conv_bias = jnp.sum(grad_conv, axis=(0, 1))
        p.g_taps = jnp.stack(
            [
                jnp.sum(grad_conv * p.conv_ext[:, lo + k : lo + k + span, :], axis=(0, 1))
                for k in range(CONV)
            ],
            axis=-1,
        )

    def backward_input(p):
        grad_normed = nt(p.grad_conv_in, w_conv_in) + nt(p.grad_gate_in, w_gate_in)
        p.input_grad = p.grad_mixed + norm_back(grad_normed * gain_one, p.block, p.scale_one)

    parts = []
    parts.append(forward(0, None, None))
    for m in range(1, groups):
        parts.append(forward(m, parts[-1].send, parts[-1].arrived))
    shared = ()
    for m in range(groups):
        shared = expert(m, shared)
    values, grad_hidden = shared

    def joined(name):
        return jnp.concatenate([getattr(p, name) for p in parts], axis=0)

    def added(name):
        return functools.reduce(jnp.add, [getattr(p, name) for p in parts])

    def added_products(left, right):
        return functools.reduce(
            jnp.add, [tn(getattr(p, left), getattr(p, right)) for p in parts]
        )

    rows_in = joined("rows_in")
    rows_in, values, grad_hidden = after((rows_in, values, grad_hidden), parts[-1].back)
    grad_second = tn(values, rows_in[:, width:]).astype(BF)
    grad_first = tn(grad_hidden, rows_in[:, :width]).astype(BF)
    products = grad_first, grad_second
    parts[0].returned = after(parts[0].returned, products)
    backward_router(parts[0])
    grad_first, grad_second = after(products, parts[0].grad_mix)
    grad_second = lax.psum_scatter(grad_second, "seq", scatter_dimension=0, tiled=True)
    grad_first = lax.psum_scatter(grad_first, "seq", scatter_dimension=0, tiled=True)
    for p, earlier in zip(parts[1:], parts):
        p.returned = after(p.returned, earlier.grad_mix)
        backward_router(p)
    g_feat = jnp.concatenate([added("g_gain_two")[:, None], added("g_router")], axis=1)
    background = jnp.concatenate(
        [
            added_products("normed", "grad_gate_in").astype(BF),
            side_by_side(added_products("gated", "grad_branch").astype(BF), rows),
            pad_cols(g_feat, 128).astype(BF),
        ],
        axis=1,
    )
    background = lax.psum_scatter(background, ("batch", "seq"), scatter_dimension=0, tiled=True)
    background = background.astype(F32)
    g_gate_half = background[:, :DI]
    g_back = one_below(background[:, DI : 2 * DI], rows)
    g_feat = background[:, 2 * DI :]
    for p in parts:
        backward_mixer(p)
    g_conv_half = added_products("normed", "grad_conv_in")
    for p in parts:
        backward_taps(p, g_conv_half)
    g_chan = jnp.concatenate(
        [
            added("g_proj"),
            added("g_step"),
            added("g_log"),
            added("g_taps"),
            added("g_conv_bias")[:, None],
            added("g_step_bias")[:, None],
            added("g_skip")[:, None],
        ],
        axis=1,
    )
    g_chan = pad_cols(g_chan, 256).reshape(-1, 512)
    g_rest = jnp.concatenate([sum_over_seq(g_conv_half), sum_over_seq(g_chan)], axis=2)
    for p in parts:
        p.grad_conv_in = after(p.grad_conv_in, (g_conv_half, background))
        backward_input(p)
    grad_first, grad_second = after((grad_first, grad_second), g_conv_half)
    grad_first = grad_first.astype(F32).T
    grad_second = grad_second.astype(F32)
    g_rest = after(g_rest, (parts[0].input_grad, grad_first, grad_second))
    g_rest = over_batch(g_rest)
    g_rest = after(g_rest, parts[-1].input_grad)
    g_conv_half = g_rest[:, :DI]
    g_chan = g_rest[:, DI:].reshape(-1, 256)
    g_in = jnp.concatenate([g_conv_half, g_gate_half], axis=1)
    g_gain_one = jnp.sum(g_in * in_proj.astype(F32), axis=1) / norm_gain.astype(F32)
    at = maps + DT_RANK
    return (
        joined("activations"),
        joined("input_grad"),
        g_gain_one,
        g_in,
        g_chan[:, at + STATE : at + STATE + CONV],
        g_chan[:, at + STATE + CONV],
        g_chan[:, :maps],
        g_chan[:, maps:at],
        g_chan[:, at + STATE + CONV + 1],
        g_chan[:, at : at + STATE],
        g_chan[:, at + STATE + CONV + 2],
        g_back,
        g_feat[:, 0],
        g_feat[:, 1 : 1 + experts],
        grad_first[None],
        grad_second[None],
    )


def solution(mesh):
    return jax.shard_map(
        shards,
        mesh=mesh,
        in_specs=(
            P("batch", "seq", None),
            P("batch", "seq", None),
            P(),
            P("batch"),
            P("batch", "seq"),
            P("batch", "seq"),
            P(("batch", "seq")),
            P(("batch", "seq"), None),
            P(("batch", "seq"), None),
            P(("batch", "seq")),
            P(("batch", "seq"), None),
            P(("batch", "seq"), None),
            P(("batch", "seq")),
            P(("batch", "seq"), None),
            P(("batch", "seq")),
            P(("batch", "seq"), None),
            P(("batch", "seq")),
            P(("batch", "seq"), None),
            P("batch", None, "seq"),
            P("batch", "seq", None),
        ),
        out_specs=(
            P("batch", "seq", None),
            P("batch", "seq", None),
            P(("batch", "seq")),
            P(("batch", "seq"), None),
            P(("batch", "seq"), None),
            P(("batch", "seq")),
            P(("batch", "seq"), None),
            P(("batch", "seq"), None),
            P(("batch", "seq")),
            P(("batch", "seq"), None),
            P(("batch", "seq")),
            P(("batch", "seq"), None),
            P(("batch", "seq")),
            P(("batch", "seq"), None),
            P("batch", None, "seq"),
            P("batch", "seq", None),
        ),
        check_vma=False,
    )
```
